32 devices in a mesh: groups: 2 (over y), space: 16 (over z, x, core).
Axes of the slice: x: 2, y: 2, z: 4, core: 2. Of those that a mesh axis runs over, the one named last changes fastest.
Arguments:
- links: float32 [3, 3, 3, 2, 1024, 32], P(None, None, None, None, 'space', 'groups'), parts along dimension 5, may hold values from -1 to 1, as said below
- sources: float32 [24, 3, 2, 1024, 32], P(None, None, None, 'space', 'groups'), parts along dimension 4, may hold values from -6 to 6
Outputs:
- filtered: float32 [24, 3, 2, 1024, 32], P(None, None, None, 'space', 'groups'), parts along dimension 4
The draws below stay inside these ranges and needn't reach their ends.
There are 2 independent parts, one for each index of `groups`. The reference program is written for one: setup_inputs(seed, part) draws one part's arguments, and reference() takes and returns one part's arrays. A program takes and returns all parts, laid end to end along the dimension named above; each array names one. Nothing has to cross between parts.
Inputs may be any that keep to these rules, and one draw needn't show every extreme that they name: At every site and direction, links[mu, :, :, 0, s] + i links[mu, :, :, 1, s] is a special unitary 3 x 3 matrix.
All inputs are finite; a program needn't handle non-finite values.
Results may differ from the reference program's by a relative error of at most 0.00002.
Values sent between devices are 32-bit elements; how exact they have to be, the bound alone decides.
No kernel may reach another device: no remote copies, remote signals or barrier semaphores. Data moves between devices by JAX's collectives and lax.ppermute only.
A program may use at most 64 MiB of HBM per device.

```python
import jax
import jax.numpy as jnp
from jax import lax

NV = 24
NT = 8
LS = 32
XS = 2
YZ = 1024
TX = 16


def complex_mul(a_re, a_im, b_re, b_im):
    return (a_re * b_re - a_im * b_im, a_re * b_im + a_im * b_re)


def normalized(parts_re, parts_im):
    total = parts_re[0] * parts_re[0] + parts_im[0] * parts_im[0]
    for comp in range(1, 3):
        total = total + parts_re[comp] * parts_re[comp] + parts_im[comp] * parts_im[comp]
    factor = lax.rsqrt(total + 1e-12)
    return ([p * factor for p in parts_re], [p * factor for p in parts_im])


def draw_links(key, part):
    key = jax.random.fold_in(key, 11)
    offset = 3.0
    noise_draw = jax.random.uniform(key, (2, 2, 3, 3, LS * LS, NT * XS), jnp.float32, -1.0, 1.0)
    first_re = [noise_draw[0, 0, :, comp] for comp in range(3)]
    first_im = [noise_draw[0, 1, :, comp] for comp in range(3)]
    second_re = [noise_draw[1, 0, :, comp] for comp in range(3)]
    second_im = [noise_draw[1, 1, :, comp] for comp in range(3)]
    first_re[0] = first_re[0] + offset
    second_re[0] = second_re[0] * 0.4
    second_re[1] = second_re[1] + offset
    second_re[2] = second_re[2] * 0.4
    row_one_re, row_one_im = normalized(first_re, first_im)
    proj_re = 0.0
    proj_im = 0.0
    for comp in range(3):
        proj_re = proj_re + row_one_re[comp] * second_re[comp] + row_one_im[comp] * second_im[comp]
        proj_im = proj_im + row_one_re[comp] * second_im[comp] - row_one_im[comp] * second_re[comp]
    other_re = []
    other_im = []
    for comp in range(3):
        other_re.append(second_re[comp] - (proj_re * row_one_re[comp] - proj_im * row_one_im[comp]))
        other_im.append(second_im[comp] - (proj_re * row_one_im[comp] + proj_im * row_one_re[comp]))
    row_two_re, row_two_im = normalized(other_re, other_im)
    row_three_re = []
    row_three_im = []
    for comp in range(3):
        left = (comp + 1) % 3
        right = (comp + 2) % 3
        lead_re, lead_im = complex_mul(row_one_re[left], row_one_im[left], row_two_re[right], row_two_im[right])
        tail_re, tail_im = complex_mul(row_one_re[right], row_one_im[right], row_two_re[left], row_two_im[left])
        row_three_re.append(lead_re - tail_re)
        row_three_im.append(tail_im - lead_im)
    real_rows = jnp.stack([jnp.stack(row_one_re, axis=1), jnp.stack(row_two_re, axis=1), jnp.stack(row_three_re, axis=1)], axis=1)
    imag_rows = jnp.stack([jnp.stack(row_one_im, axis=1), jnp.stack(row_two_im, axis=1), jnp.stack(row_three_im, axis=1)], axis=1)
    return jnp.stack([real_rows, imag_rows], axis=3).astype(jnp.float32)


def block_scale(own_key, extent, split, least, top_value):
    loudness, own = 1.0, jax.random.fold_in(own_key, 6)
    for dim, parts in split:
        draws = jnp.exp(jax.random.uniform(jax.random.fold_in(own, dim), (parts,), jnp.float32, least / len(split), top_value / len(split)))
        loudness = loudness * jnp.repeat(draws, extent[dim] // parts).reshape([-1 if axis == dim else 1 for axis in range(len(extent))])
    return loudness


def centred(key, extent, scale, limit, split=(), held_as=jnp.bfloat16):
    gain = block_scale(key, extent, split, -0.22, 0.18) if split else 1.0
    values = jax.random.normal(key, extent, jnp.float32) * scale * gain
    return jnp.minimum(jnp.maximum(values, -limit), limit).astype(held_as)


def setup_inputs(seed: int = 0, part: int = 0) -> dict:
    arg_keys = jax.random.split(jax.random.key(seed), 3)
    part_keys = jax.random.split(jax.random.fold_in(arg_keys[2], part), 3)
    links = draw_links(jax.random.fold_in(jax.random.fold_in(arg_keys[2], part), 71), part)
    sources = centred(part_keys[1], (NV, 3, 2, YZ, TX), 1.0, 6.0, ((3, 16),), jnp.float32)
    return dict(links=links, sources=sources)


cheb_coeffs = (0.6, -0.5, 0.35, -0.25, 0.15)


def apply_link(link, vector):
    real_part = 0.0
    imag_part = 0.0
    for column in range(3):
        link_re = link[:, column, 0][None]
        link_im = link[:, column, 1][None]
        vec_re = vector[:, column, 0][:, None]
        vec_im = vector[:, column, 1][:, None]
        real_part = real_part + link_re * vec_re - link_im * vec_im
        imag_part = imag_part + link_re * vec_im + link_im * vec_re
    return jnp.stack([real_part, imag_part], axis=2)


def apply_dagger(link, vector):
    real_part = 0.0
    imag_part = 0.0
    for column in range(3):
        link_re = link[column, :, 0][None]
        link_im = link[column, :, 1][None]
        vec_re = vector[:, column, 0][:, None]
        vec_im = vector[:, column, 1][:, None]
        real_part = real_part + link_re * vec_re + link_im * vec_im
        imag_part = imag_part + link_re * vec_im - link_im * vec_re
    return jnp.stack([real_part, imag_part], axis=2)


def reference(links, sources):
    gauge_all = links.reshape(3, 3, 3, 2, LS, LS, NT, XS)
    source_field = sources.reshape(NV, 3, 2, LS, LS, NT, XS)
    roll_axes = (-1, -4, -3)

    def hop_sum(vector):
        summed = None
        for direction in range(3):
            axis_id = roll_axes[direction]
            ahead = apply_link(gauge_all[direction], jnp.roll(vector, -1, axis=axis_id))
            behind = apply_dagger(jnp.roll(gauge_all[direction], 1, axis=axis_id), jnp.roll(vector, 1, axis=axis_id))
            if direction == 0:
                summed = ahead + behind
            else:
                summed = summed + ahead + behind
        return summed

    def scaled(vector):
        return hop_sum(vector) * (-1.0 / 6.0)

    previous = source_field
    current = scaled(previous)
    filtered = cheb_coeffs[0] * previous + cheb_coeffs[1] * current
    for degree in range(2, 5):
        following = 2.0 * scaled(current) - previous
        filtered = filtered + cheb_coeffs[degree] * following
        previous, current = current, following
    return filtered.reshape(NV, 3, 2, LS * LS, NT * XS)
```

```python
import functools

import jax
import jax.numpy as jnp
from jax import lax
from jax.experimental import pallas as pl
from jax.experimental.pallas import tpu as pltpu
from jax.sharding import PartitionSpec as P

NT = 8
LS = 32

cheb_coeffs = (0.6, -0.5, 0.35, -0.25, 0.15)


def power_coeffs():
    c0, c1, c2, c3, c4 = cheb_coeffs
    return (c0 - c2 + c4, c1 - 3.0 * c3, 2.0 * c2 - 8.0 * c4, 4.0 * c3, 8.0 * c4)


def lane_ids():
    return lax.broadcasted_iota(jnp.int32, (8, 128), 1)


def sublane_ids():
    return lax.broadcasted_iota(jnp.int32, (8, 128), 0)


def low_half():
    return (lane_ids() // LS) % 2 == 0


def first_of(p, q, low):
    return jnp.where(low, p, pltpu.roll(q, LS, 1))


def second_of(p, q, low):
    return jnp.where(low, pltpu.roll(p, 128 - LS, 1), q)


def z_next(value, z):
    return jnp.where(z == LS - 1, pltpu.roll(value, LS - 1, 1), pltpu.roll(value, 127, 1))


def z_prev(value, z):
    return jnp.where(z == 0, pltpu.roll(value, 129 - LS, 1), pltpu.roll(value, 1, 1))


def x_other(value, even):
    return jnp.where(even, pltpu.roll(value, 7, 0), pltpu.roll(value, 1, 0))


def pack_kernel(src, links, row0, row1, inner, edge, send):
    low = low_half()
    z = lane_ids() % LS
    even = sublane_ids() % 2 == 0
    half = src.shape[0] // 2

    def tile(ref, index):
        return jnp.concatenate([ref[index + (slice(0, 8),)], ref[index + (slice(8, 16),)]], axis=1)

    for a in range(3):
        for b in range(3):
            for part in range(2):
                sign = 1.0 - 2.0 * part
                x_link = tile(links, (0, a, b, part)) * (-1.0 / 6.0)
                y_link = tile(links, (1, a, b, part)) * (-1.0 / 6.0)
                z_link = tile(links, (2, a, b, part)) * (-1.0 / 6.0)
                for row, pick in enumerate((first_of, second_of)):
                    u_x = pick(x_link, x_link, low)
                    inner[row, 0, a, b, part] = u_x
                    u_z = pick(z_link, z_link, low)
                    inner[row, 1, a, b, part] = u_z
                    inner[row, 2, b, a, part] = sign * z_prev(u_z, z)
                u_y = first_of(y_link, y_link, low)
                inner[0, 3, a, b, part] = u_y
                inner[1, 3, b, a, part] = sign * u_y
                edge[a, b, part] = second_of(y_link, y_link, low)
            y_re = tile(links, (1, a, b, 0)) * (-1.0 / 6.0)
            y_im = tile(links, (1, a, b, 1)) * (-1.0 / 6.0)
            send[a, b] = second_of(y_re, y_im, low)
    for row in range(2):
        for part in range(2):
            sign = 1.0 - 2.0 * part
            own = [[inner[row, 0, a, b, part] for b in range(3)] for a in range(3)]
            for a in range(3):
                for b in range(3):
                    inner[row, 0, a, b, part] = own[a][b] + sign * x_other(own[b][a], even)

    def step(n, carry):
        for k in range(6):
            p = tile(src, (n, k))
            q = tile(src, (n + half, k))
            row0[n, k] = first_of(p, q, low)
            row1[n, k] = second_of(p, q, low)
        return carry

    lax.fori_loop(0, half, step, 0)


def mat_vec(load, vectors, sums):
    for a in range(3):
        for b in range(3):
            w_re, w_im = load(a, b)
            for vec, acc in zip(vectors, sums):
                v_re, v_im = vec[2 * b], vec[2 * b + 1]
                acc[2 * a] = acc[2 * a] + w_re * v_re - w_im * v_im
                acc[2 * a + 1] = acc[2 * a + 1] + w_re * v_im + w_im * v_re


def inner_kernel(coeff, width, y0, y1, inner, v0, v1, sum0, sum1):
    z = lane_ids() % LS
    even = sublane_ids() % 2 == 0

    def step(i, carry):
        pairs = [i * width + w for w in range(width)]
        for row, (here, there, start, out) in enumerate(((y0, y1, v0, sum0), (y1, y0, v1, sum1))):
            sums = [[coeff * start[n, k] for k in range(6)] for n in pairs]

            def term(index, vectors):
                mat_vec(
                    lambda a, b: (inner[row, index, a, b, 0], inner[row, index, a, b, 1]),
                    vectors,
                    sums,
                )

            term(0, [[x_other(here[n, k], even) for k in range(6)] for n in pairs])
            term(1, [[z_next(here[n, k], z) for k in range(6)] for n in pairs])
            term(2, [[z_prev(here[n, k], z) for k in range(6)] for n in pairs])
            term(3, [[there[n, k] for k in range(6)] for n in pairs])
            for n, acc in zip(pairs, sums):
                for k in range(6):
                    out[n, k] = acc[k]
        return carry

    lax.fori_loop(0, y0.shape[0] // width, step, 0)


def edge_sums(pairs, below, above, edge, links_below, sum0, sum1):
    acc0 = [[sum0[n, k] for k in range(6)] for n in pairs]
    mat_vec(
        lambda a, b: (links_below[b, a, 0], links_below[b, a, 1]),
        [[below[n, k] for k in range(6)] for n in pairs],
        acc0,
    )
    acc1 = [[sum1[n, k] for k in range(6)] for n in pairs]
    mat_vec(
        lambda a, b: (edge[a, b, 0], edge[a, b, 1]),
        [[above[n, k] for k in range(6)] for n in pairs],
        acc1,
    )
    return acc0, acc1


def unpack_links(received, links_below, low):
    for a in range(3):
        for b in range(3):
            w = received[a, b]
            links_below[a, b, 0] = first_of(w, w, low)
            links_below[a, b, 1] = -second_of(w, w, low)


def edge_kernel(width, below, above, edge, received, sum0, sum1, row0, row1, links_below):
    unpack_links(received, links_below, low_half())

    def step(i, carry):
        pairs = [i * width + w for w in range(width)]
        acc0, acc1 = edge_sums(pairs, below, above, edge, links_below, sum0, sum1)
        for n, top, bottom in zip(pairs, acc0, acc1):
            for k in range(6):
                row0[n, k] = top[k]
                row1[n, k] = bottom[k]
        return carry

    lax.fori_loop(0, below.shape[0] // width, step, 0)


def last_kernel(width, lead, below, above, edge, received, sum0, sum1, out, links_below):
    low = low_half()
    unpack_links(received, links_below, low)
    half = below.shape[0]

    def step(i, carry):
        pairs = [i * width + w for w in range(width)]
        acc0, acc1 = edge_sums(pairs, below, above, edge, links_below, sum0, sum1)
        for n, top, bottom in zip(pairs, acc0, acc1):
            for k in range(6):
                p = first_of(top[k], bottom[k], low) * lead
                q = second_of(top[k], bottom[k], low) * lead
                for m, value in ((n, p), (n + half, q)):
                    out[m, k, 0:8] = value[:, : 2 * LS]
                    out[m, k, 8:16] = value[:, 2 * LS :]
        return carry

    lax.fori_loop(0, half // width, step, 0)


VMEM_LIMIT = 32 * 1024 * 1024


def call(kernel, outs, args, flops, scratch=()):
    moved = sum(4 * a.size for a in args) + sum(4 * o.size for o in outs)
    return pl.pallas_call(
        kernel,
        out_shape=outs,
        in_specs=[pl.BlockSpec(memory_space=pltpu.VMEM)] * len(args),
        out_specs=[pl.BlockSpec(memory_space=pltpu.VMEM)] * len(outs),
        scratch_shapes=list(scratch),
        compiler_params=pltpu.CompilerParams(vmem_limit_bytes=VMEM_LIMIT),
        cost_estimate=pl.CostEstimate(flops=flops, bytes_accessed=moved, transcendentals=0),
    )(*args)


def halo_body(links, sources):
    vectors = sources.shape[0]
    half = vectors // 2
    width = 2
    sites, planes = links.shape[4:]
    f32 = functools.partial(jax.ShapeDtypeStruct, dtype=jnp.float32)
    field = f32((half, 6, 8, 128))
    inner_shape = f32((2, 4, 3, 3, 2, 8, 128))
    edge_shape = f32((3, 3, 2, 8, 128))
    send_shape = f32((3, 3, 8, 128))
    source_view = jnp.swapaxes(sources, 3, 4).reshape(vectors, 6, planes, sites)
    link_view = jnp.swapaxes(links, 4, 5)
    powers = power_coeffs()
    lead = powers[4]
    work = 2 * half * 36 * 2 * 1024

    v0, v1, inner, edge, link_send = call(
        pack_kernel,
        [field, field, inner_shape, edge_shape, send_shape],
        [source_view, link_view],
        2 * half * 6 * 1024,
    )
    count = lax.axis_size("space")
    up = [(d, (d + 1) % count) for d in range(count)]
    down = [(d, (d - 1) % count) for d in range(count)]
    received = lax.ppermute(link_send, "space", up)
    y0, y1 = v0, v1
    for power in (3, 2, 1, 0):
        below = lax.ppermute(y1, "space", up)
        above = lax.ppermute(y0, "space", down)
        sum0, sum1 = call(
            functools.partial(inner_kernel, powers[power] / lead, width),
            [field, field],
            [y0, y1, inner, v0, v1],
            4 * work,
        )
        args = [below, above, edge, received, sum0, sum1]
        scratch = [pltpu.VMEM(edge_shape.shape, jnp.float32)]
        if power:
            y0, y1 = call(
                functools.partial(edge_kernel, width), [field, field], args, work, scratch
            )
        else:
            (out,) = call(
                functools.partial(last_kernel, width, lead),
                [f32(source_view.shape)],
                args,
                work,
                scratch,
            )
    return jnp.swapaxes(out.reshape(vectors, 3, 2, planes, sites), 3, 4)


def shifted(value, axis, steps):
    count = lax.axis_size(axis)
    pairs = [(source, (source + steps) % count) for source in range(count)]
    return lax.ppermute(value, axis, pairs)


def apply_link(link, vector):
    real_part = 0.0
    imag_part = 0.0
    for column in range(3):
        link_re = link[:, column, 0][None]
        link_im = link[:, column, 1][None]
        vec_re = vector[:, column, 0][:, None]
        vec_im = vector[:, column, 1][:, None]
        real_part = real_part + link_re * vec_re - link_im * vec_im
        imag_part = imag_part + link_re * vec_im + link_im * vec_re
    return jnp.stack([real_part, imag_part], axis=2)


def apply_dagger(link, vector):
    real_part = 0.0
    imag_part = 0.0
    for column in range(3):
        link_re = link[column, :, 0][None]
        link_im = link[column, :, 1][None]
        vec_re = vector[:, column, 0][:, None]
        vec_im = vector[:, column, 1][:, None]
        real_part = real_part + link_re * vec_re + link_im * vec_im
        imag_part = imag_part + link_re * vec_im - link_im * vec_re
    return jnp.stack([real_part, imag_part], axis=2)


def z_ahead(array, extent, z_index):
    return jnp.where(
        z_index == extent - 1, jnp.roll(array, extent - 1, axis=-1), jnp.roll(array, -1, axis=-1)
    )


def z_behind(array, extent, z_index):
    return jnp.where(
        z_index == 0, jnp.roll(array, 1 - extent, axis=-1), jnp.roll(array, 1, axis=-1)
    )


def plane_body(links, sources):
    device_count = lax.axis_size("space")
    slabs = device_count // NT
    yz_local = links.shape[4]
    planes = links.shape[5] // device_count
    plane_sites = yz_local * device_count
    vectors = sources.shape[0]
    link_parts = links.reshape(54, yz_local, NT, slabs, planes)
    source_parts = sources.reshape(vectors * 6, yz_local, NT, slabs, planes)
    link_send = jnp.transpose(link_parts, (0, 3, 2, 4, 1)).reshape(
        54, device_count, planes, yz_local
    )
    source_send = jnp.transpose(source_parts, (0, 3, 2, 4, 1)).reshape(
        vectors * 6, device_count, planes, yz_local
    )
    link_recv, source_recv = (
        lax.all_to_all(link_send, "space", split_axis=1, concat_axis=3, tiled=True),
        lax.all_to_all(source_send, "space", split_axis=1, concat_axis=3, tiled=True),
    )
    gauge_local = link_recv.reshape(3, 3, 3, 2, planes, plane_sites)
    source_field = source_recv.reshape(vectors, 3, 2, planes, plane_sites)
    z_index = jnp.arange(plane_sites, dtype=jnp.int32) % LS
    x_top = gauge_local[0]
    x_rest = gauge_local[0][:, :, :, :-1]
    y_back = jnp.roll(gauge_local[1], LS, axis=-1)
    z_back = z_behind(gauge_local[2], LS, z_index)

    def fetch_lower(vector):
        return shifted(apply_dagger(x_top, vector), "space", NT)

    def hop_sum(vector):
        upper_face = shifted(vector, "space", -NT)
        lower_face = fetch_lower(vector)
        ahead = apply_link(
            gauge_local[0], jnp.concatenate([vector[:, :, :, 1:], upper_face], axis=3)
        )
        behind = jnp.concatenate([lower_face, apply_dagger(x_rest, vector[:, :, :, :-1])], axis=3)
        summed = ahead + behind
        summed = (
            summed
            + apply_link(gauge_local[1], jnp.roll(vector, -LS, axis=-1))
            + apply_dagger(y_back, jnp.roll(vector, LS, axis=-1))
        )
        summed = (
            summed
            + apply_link(gauge_local[2], z_ahead(vector, LS, z_index))
            + apply_dagger(z_back, z_behind(vector, LS, z_index))
        )
        return summed

    def scaled(vector):
        return hop_sum(vector) * (-1.0 / 6.0)

    previous = source_field
    current = scaled(previous)
    filtered = cheb_coeffs[0] * previous + cheb_coeffs[1] * current
    for degree in range(2, 5):
        following = 2.0 * scaled(current) - previous
        filtered = filtered + cheb_coeffs[degree] * following
        previous, current = (current, following)
    outgoing = filtered.reshape(vectors * 6, 1, planes, plane_sites)
    returned = lax.all_to_all(outgoing, "space", split_axis=3, concat_axis=1, tiled=True)
    ordered = jnp.transpose(
        returned.reshape(vectors * 6, slabs, NT, planes, yz_local), (0, 4, 2, 1, 3)
    )
    return ordered.reshape(vectors, 3, 2, yz_local, NT * slabs * planes)


def body(links, sources):
    sites, planes = sources.shape[3:]
    if sites == 2 * LS and planes == 2 * NT and sources.shape[0] % 4 == 0:
        return halo_body(links, sources)
    return plane_body(links, sources)


def solution(mesh):
    in_specs = (
        P(None, None, None, None, "space", "groups"),
        P(None, None, None, "space", "groups"),
    )
    out_specs = P(None, None, None, "space", "groups")
    return jax.shard_map(body, mesh=mesh, in_specs=in_specs, out_specs=out_specs, check_vma=False)
```

```python
import functools

import jax
import jax.numpy as jnp
from jax import lax
from jax.experimental import pallas as pl
from jax.experimental.pallas import tpu as pltpu
from jax.sharding import PartitionSpec as P

NT = 8
LS = 32

cheb_coeffs = (0.6, -0.5, 0.35, -0.25, 0.15)


def power_coeffs():
    c0, c1, c2, c3, c4 = cheb_coeffs
    return (c0 - c2 + c4, c1 - 3.0 * c3, 2.0 * c2 - 8.0 * c4, 4.0 * c3, 8.0 * c4)


def lane_ids():
    return lax.broadcasted_iota(jnp.int32, (8, 128), 1)


def sublane_ids():
    return lax.broadcasted_iota(jnp.int32, (8, 128), 0)


def low_half():
    return (lane_ids() // LS) % 2 == 0


def first_of(p, q, low):
    return jnp.where(low, p, pltpu.roll(q, LS, 1))


def second_of(p, q, low):
    return jnp.where(low, pltpu.roll(p, 128 - LS, 1), q)


def z_next(value, z):
    return jnp.where(z == LS - 1, pltpu.roll(value, LS - 1, 1), pltpu.roll(value, 127, 1))


def z_prev(value, z):
    return jnp.where(z == 0, pltpu.roll(value, 129 - LS, 1), pltpu.roll(value, 1, 1))


def x_other(value, even):
    return jnp.where(even, pltpu.roll(value, 7, 0), pltpu.roll(value, 1, 0))


def mat_vec(load, vectors, sums, dagger=False):
    for a in range(3):
        for b in range(3):
            w_re, w_im = load(b, a) if dagger else load(a, b)
            for vec, acc in zip(vectors, sums):
                v_re, v_im = vec[2 * b], vec[2 * b + 1]
                if dagger:
                    acc[2 * a] = acc[2 * a] + w_re * v_re + w_im * v_im
                    acc[2 * a + 1] = acc[2 * a + 1] + w_re * v_im - w_im * v_re
                else:
                    acc[2 * a] = acc[2 * a] + w_re * v_re - w_im * v_im
                    acc[2 * a + 1] = acc[2 * a + 1] + w_re * v_im + w_im * v_re


def zeros(count):
    return [[jnp.zeros((8, 128), jnp.float32) for _ in range(6)] for _ in range(count)]


def edge_link(edge):
    return lambda a, b: (edge[a, b, 0], edge[a, b, 1])


def tile(ref, index):
    return jnp.concatenate([ref[index + (slice(0, 8),)], ref[index + (slice(8, 16),)]], axis=1)


def pack_edge(links, edge):
    low = low_half()
    for a in range(3):
        for b in range(3):
            for part in range(2):
                y_link = tile(links, (a, b, part)) * (-1.0 / 6.0)
                edge[a, b, part] = second_of(y_link, y_link, low)


def pack_sources(first, src, edge, row0, row1, up, arrived, sems):
    low = low_half()
    pairs = row0.shape[0]

    def fetch(i):
        here = pl.ds(2 * i, 2)
        there = pl.ds(first + 2 * i, 2)
        return pltpu.make_async_copy(src.at[there], arrived.at[here], sems.at[i])

    for i in range(pairs):
        fetch(i).start()

    def finish():
        def step(i, carry):
            fetch(i).wait()
            upper = []
            for k in range(6):
                p = tile(arrived, (2 * i, k))
                q = tile(arrived, (2 * i + 1, k))
                row0[i, k] = first_of(p, q, low)
                upper.append(second_of(p, q, low))
                row1[i, k] = upper[k]
            sums = zeros(1)
            mat_vec(edge_link(edge), [upper], sums, dagger=True)
            for k in range(6):
                up[i, k] = sums[0][k]
            return carry

        lax.fori_loop(0, pairs, step, 0)

    return finish


def first_pack_kernel(first, src, links, edge, row0, row1, up, arrived, y_links, sems, link_sem):
    link_copy = pltpu.make_async_copy(links.at[1], y_links, link_sem)
    link_copy.start()
    finish = pack_sources(first, src, edge, row0, row1, up, arrived, sems)
    link_copy.wait()
    pack_edge(y_links, edge)
    finish()


def pack_kernel(first, src, edge, row0, row1, up, arrived, sems):
    pack_sources(first, src, edge, row0, row1, up, arrived, sems)()


def link_kernel(links, inner):
    low = low_half()
    z = lane_ids() % LS
    even = sublane_ids() % 2 == 0
    for a in range(3):
        for b in range(3):
            for part in range(2):
                sign = 1.0 - 2.0 * part
                x_link = tile(links, (0, a, b, part)) * (-1.0 / 6.0)
                y_link = tile(links, (1, a, b, part)) * (-1.0 / 6.0)
                z_link = tile(links, (2, a, b, part)) * (-1.0 / 6.0)
                for row, pick in enumerate((first_of, second_of)):
                    inner[row, 0, a, b, part] = pick(x_link, x_link, low)
                    u_z = pick(z_link, z_link, low)
                    inner[row, 1, a, b, part] = u_z
                    inner[row, 2, b, a, part] = sign * z_prev(u_z, z)
                u_y = first_of(y_link, y_link, low)
                inner[0, 3, a, b, part] = u_y
                inner[1, 3, b, a, part] = sign * u_y
    for row in range(2):
        for part in range(2):
            sign = 1.0 - 2.0 * part
            own = [[inner[row, 0, a, b, part] for b in range(3)] for a in range(3)]
            for a in range(3):
                for b in range(3):
                    inner[row, 0, a, b, part] = own[a][b] + sign * x_other(own[b][a], even)


def inner_kernel(coeff, width, y0, y1, inner, v0, v1, sum0, sum1):
    z = lane_ids() % LS
    even = sublane_ids() % 2 == 0

    def step(i, carry):
        pairs = [i * width + w for w in range(width)]
        for row, (here, there, start, out) in enumerate(((y0, y1, v0, sum0), (y1, y0, v1, sum1))):
            sums = [[coeff * start[n, k] for k in range(6)] for n in pairs]

            def term(index, vectors):
                mat_vec(
                    lambda a, b: (inner[row, index, a, b, 0], inner[row, index, a, b, 1]),
                    vectors,
                    sums,
                )

            term(0, [[x_other(here[n, k], even) for k in range(6)] for n in pairs])
            term(1, [[z_next(here[n, k], z) for k in range(6)] for n in pairs])
            term(2, [[z_prev(here[n, k], z) for k in range(6)] for n in pairs])
            term(3, [[there[n, k] for k in range(6)] for n in pairs])
            for n, acc in zip(pairs, sums):
                for k in range(6):
                    out[n, k] = acc[k]
        return carry

    lax.fori_loop(0, y0.shape[0] // width, step, 0)


def edge_sums(pairs, below, above, edge, sum0, sum1):
    lower = [[sum0[n, k] + below[n, k] for k in range(6)] for n in pairs]
    upper = [[sum1[n, k] for k in range(6)] for n in pairs]
    mat_vec(edge_link(edge), [[above[n, k] for k in range(6)] for n in pairs], upper)
    return lower, upper


def edge_kernel(width, below, above, edge, sum0, sum1, row0, row1, up):
    def step(i, carry):
        pairs = [i * width + w for w in range(width)]
        lower, upper = edge_sums(pairs, below, above, edge, sum0, sum1)
        back = zeros(width)
        mat_vec(edge_link(edge), upper, back, dagger=True)
        for n, bottom, top, product in zip(pairs, lower, upper, back):
            for k in range(6):
                row0[n, k] = bottom[k]
                row1[n, k] = top[k]
                up[n, k] = product[k]
        return carry

    lax.fori_loop(0, below.shape[0] // width, step, 0)


def last_kernel(first, lead, below, above, edge, sum0, sum1, *rest):
    out, filled, sems = rest[-3:]
    low = low_half()
    pairs = below.shape[0]

    def store(i):
        here = pl.ds(2 * i, 2)
        there = pl.ds(first + 2 * i, 2)
        return pltpu.make_async_copy(filled.at[here], out.at[there], sems.at[i])

    def step(i, carry):
        (lower,), (upper,) = edge_sums([i], below, above, edge, sum0, sum1)
        for k in range(6):
            p = first_of(lower[k], upper[k], low) * lead
            q = second_of(lower[k], upper[k], low) * lead
            for m, value in ((2 * i, p), (2 * i + 1, q)):
                filled[m, k, 0:8] = value[:, : 2 * LS]
                filled[m, k, 8:16] = value[:, 2 * LS :]
        store(i).start()
        return carry

    def drain(i, carry):
        store(i).wait()
        return carry

    lax.fori_loop(0, pairs, step, 0)
    lax.fori_loop(0, pairs, drain, 0)


VMEM_LIMIT = 32 * 1024 * 1024
CHUNKS = 2


def call(kernel, outs, args, flops, scratch=(), in_hbm=(), out_hbm=False, aliases={}):
    moved = sum(4 * a.size for a in args) + sum(4 * o.size for o in outs)
    args = [
        pltpu.with_memory_space_constraint(a, pltpu.HBM) if i in in_hbm else a
        for i, a in enumerate(args)
    ]
    vmem = pl.BlockSpec(memory_space=pltpu.VMEM)
    hbm = pl.BlockSpec(memory_space=pltpu.HBM)
    return pl.pallas_call(
        kernel,
        out_shape=outs,
        in_specs=[hbm if i in in_hbm else vmem for i in range(len(args))],
        out_specs=[hbm if out_hbm else vmem] * len(outs),
        scratch_shapes=list(scratch),
        input_output_aliases=aliases,
        compiler_params=pltpu.CompilerParams(vmem_limit_bytes=VMEM_LIMIT),
        cost_estimate=pl.CostEstimate(flops=flops, bytes_accessed=moved, transcendentals=0),
    )(*args)


def halo_body(links, sources):
    vectors = sources.shape[0]
    share = vectors // CHUNKS
    pairs = share // 2
    width = 2
    sites, planes = links.shape[4:]
    f32 = functools.partial(jax.ShapeDtypeStruct, dtype=jnp.float32)
    field = f32((pairs, 6, 8, 128))
    inner_shape = f32((2, 4, 3, 3, 2, 8, 128))
    edge_shape = f32((3, 3, 2, 8, 128))
    source_view = jnp.swapaxes(sources, 3, 4).reshape(vectors, 6, planes, sites)
    link_view = jnp.swapaxes(links, 4, 5)
    powers = power_coeffs()
    lead = powers[4]
    work = 2 * pairs * 36 * 2 * 1024
    count = lax.axis_size("space")
    up = [(d, (d + 1) % count) for d in range(count)]
    down = [(d, (d - 1) % count) for d in range(count)]
    arrived = pltpu.VMEM((share, 6, planes, sites), jnp.float32)
    sems = pltpu.SemaphoreType.DMA((pairs,))

    edge = None
    start, halo = [], []
    for chunk in range(CHUNKS):
        if chunk == 0:
            edge, row0, row1, product = call(
                functools.partial(first_pack_kernel, 0),
                [edge_shape, field, field, field],
                [source_view, link_view],
                work,
                [
                    arrived,
                    pltpu.VMEM(link_view.shape[1:], jnp.float32),
                    sems,
                    pltpu.SemaphoreType.DMA,
                ],
                (0, 1),
            )
        else:
            row0, row1, product = call(
                functools.partial(pack_kernel, chunk * share),
                [field, field, field],
                [source_view, edge],
                work,
                [arrived, sems],
                (0,),
            )
        start.append((row0, row1))
        halo.append((lax.ppermute(product, "space", up), lax.ppermute(row0, "space", down)))
    (inner,) = call(link_kernel, [inner_shape], [link_view], 8 * 18 * 1024)
    current = list(start)
    out = None
    for power in (3, 2, 1, 0):
        for chunk in range(CHUNKS):
            sum0, sum1 = call(
                functools.partial(inner_kernel, powers[power] / lead, width),
                [field, field],
                [*current[chunk], inner, *start[chunk]],
                4 * work,
            )
            args = [*halo[chunk], edge, sum0, sum1]
            if power:
                row0, row1, product = call(
                    functools.partial(edge_kernel, width), [field, field, field], args, work
                )
                current[chunk] = (row0, row1)
                halo[chunk] = (
                    lax.ppermute(product, "space", up),
                    lax.ppermute(row0, "space", down),
                )
            else:
                (out,) = call(
                    functools.partial(last_kernel, chunk * share, lead),
                    [f32(source_view.shape)],
                    args if out is None else args + [out],
                    work,
                    [arrived, sems],
                    () if out is None else (len(args),),
                    True,
                    {} if out is None else {len(args): 0},
                )
    return jnp.swapaxes(out.reshape(vectors, 3, 2, planes, sites), 3, 4)


def shifted(value, axis, steps):
    count = lax.axis_size(axis)
    pairs = [(source, (source + steps) % count) for source in range(count)]
    return lax.ppermute(value, axis, pairs)


def apply_link(link, vector):
    real_part = 0.0
    imag_part = 0.0
    for column in range(3):
        link_re = link[:, column, 0][None]
        link_im = link[:, column, 1][None]
        vec_re = vector[:, column, 0][:, None]
        vec_im = vector[:, column, 1][:, None]
        real_part = real_part + link_re * vec_re - link_im * vec_im
        imag_part = imag_part + link_re * vec_im + link_im * vec_re
    return jnp.stack([real_part, imag_part], axis=2)


def apply_dagger(link, vector):
    real_part = 0.0
    imag_part = 0.0
    for column in range(3):
        link_re = link[column, :, 0][None]
        link_im = link[column, :, 1][None]
        vec_re = vector[:, column, 0][:, None]
        vec_im = vector[:, column, 1][:, None]
        real_part = real_part + link_re * vec_re + link_im * vec_im
        imag_part = imag_part + link_re * vec_im - link_im * vec_re
    return jnp.stack([real_part, imag_part], axis=2)


def z_ahead(array, extent, z_index):
    return jnp.where(
        z_index == extent - 1, jnp.roll(array, extent - 1, axis=-1), jnp.roll(array, -1, axis=-1)
    )


def z_behind(array, extent, z_index):
    return jnp.where(
        z_index == 0, jnp.roll(array, 1 - extent, axis=-1), jnp.roll(array, 1, axis=-1)
    )


def plane_body(links, sources):
    device_count = lax.axis_size("space")
    slabs = device_count // NT
    yz_local = links.shape[4]
    planes = links.shape[5] // device_count
    plane_sites = yz_local * device_count
    vectors = sources.shape[0]
    link_parts = links.reshape(54, yz_local, NT, slabs, planes)
    source_parts = sources.reshape(vectors * 6, yz_local, NT, slabs, planes)
    link_send = jnp.transpose(link_parts, (0, 3, 2, 4, 1)).reshape(
        54, device_count, planes, yz_local
    )
    source_send = jnp.transpose(source_parts, (0, 3, 2, 4, 1)).reshape(
        vectors * 6, device_count, planes, yz_local
    )
    link_recv, source_recv = (
        lax.all_to_all(link_send, "space", split_axis=1, concat_axis=3, tiled=True),
        lax.all_to_all(source_send, "space", split_axis=1, concat_axis=3, tiled=True),
    )
    gauge_local = link_recv.reshape(3, 3, 3, 2, planes, plane_sites)
    source_field = source_recv.reshape(vectors, 3, 2, planes, plane_sites)
    z_index = jnp.arange(plane_sites, dtype=jnp.int32) % LS
    x_top = gauge_local[0]
    x_rest = gauge_local[0][:, :, :, :-1]
    y_back = jnp.roll(gauge_local[1], LS, axis=-1)
    z_back = z_behind(gauge_local[2], LS, z_index)

    def fetch_lower(vector):
        return shifted(apply_dagger(x_top, vector), "space", NT)

    def hop_sum(vector):
        upper_face = shifted(vector, "space", -NT)
        lower_face = fetch_lower(vector)
        ahead = apply_link(
            gauge_local[0], jnp.concatenate([vector[:, :, :, 1:], upper_face], axis=3)
        )
        behind = jnp.concatenate([lower_face, apply_dagger(x_rest, vector[:, :, :, :-1])], axis=3)
        summed = ahead + behind
        summed = (
            summed
            + apply_link(gauge_local[1], jnp.roll(vector, -LS, axis=-1))
            + apply_dagger(y_back, jnp.roll(vector, LS, axis=-1))
        )
        summed = (
            summed
            + apply_link(gauge_local[2], z_ahead(vector, LS, z_index))
            + apply_dagger(z_back, z_behind(vector, LS, z_index))
        )
        return summed

    def scaled(vector):
        return hop_sum(vector) * (-1.0 / 6.0)

    previous = source_field
    current = scaled(previous)
    filtered = cheb_coeffs[0] * previous + cheb_coeffs[1] * current
    for degree in range(2, 5):
        following = 2.0 * scaled(current) - previous
        filtered = filtered + cheb_coeffs[degree] * following
        previous, current = (current, following)
    outgoing = filtered.reshape(vectors * 6, 1, planes, plane_sites)
    returned = lax.all_to_all(outgoing, "space", split_axis=3, concat_axis=1, tiled=True)
    ordered = jnp.transpose(
        returned.reshape(vectors * 6, slabs, NT, planes, yz_local), (0, 4, 2, 1, 3)
    )
    return ordered.reshape(vectors, 3, 2, yz_local, NT * slabs * planes)


def body(links, sources):
    sites, planes = sources.shape[3:]
    if sites == 2 * LS and planes == 2 * NT and sources.shape[0] % (4 * CHUNKS) == 0:
        return halo_body(links, sources)
    return plane_body(links, sources)


def solution(mesh):
    in_specs = (
        P(None, None, None, None, "space", "groups"),
        P(None, None, None, "space", "groups"),
    )
    out_specs = P(None, None, None, "space", "groups")
    return jax.shard_map(body, mesh=mesh, in_specs=in_specs, out_specs=out_specs, check_vma=False)
```

```python
import functools

import jax
import jax.numpy as jnp
from jax import lax
from jax.experimental import pallas as pl
from jax.experimental.pallas import tpu as pltpu
from jax.sharding import PartitionSpec as P

NT = 8
LS = 32

cheb_coeffs = (0.6, -0.5, 0.35, -0.25, 0.15)


def power_coeffs():
    c0, c1, c2, c3, c4 = cheb_coeffs
    return (c0 - c2 + c4, c1 - 3.0 * c3, 2.0 * c2 - 8.0 * c4, 4.0 * c3, 8.0 * c4)


def lane_ids():
    return lax.broadcasted_iota(jnp.int32, (8, 128), 1)


def sublane_ids():
    return lax.broadcasted_iota(jnp.int32, (8, 128), 0)


def low_half():
    return (lane_ids() // LS) % 2 == 0


def first_of(p, q, low):
    return jnp.where(low, p, pltpu.roll(q, LS, 1))


def second_of(p, q, low):
    return jnp.where(low, pltpu.roll(p, 128 - LS, 1), q)


def z_next(value, z):
    return jnp.where(z == LS - 1, pltpu.roll(value, LS - 1, 1), pltpu.roll(value, 127, 1))


def z_prev(value, z):
    return jnp.where(z == 0, pltpu.roll(value, 129 - LS, 1), pltpu.roll(value, 1, 1))


def x_other(value, even):
    return jnp.where(even, pltpu.roll(value, 7, 0), pltpu.roll(value, 1, 0))


def mat_vec(load, vectors, sums, dagger=False):
    for a in range(3):
        for b in range(3):
            w_re, w_im = load(b, a) if dagger else load(a, b)
            for vec, acc in zip(vectors, sums):
                v_re, v_im = vec[2 * b], vec[2 * b + 1]
                if dagger:
                    acc[2 * a] = acc[2 * a] + w_re * v_re + w_im * v_im
                    acc[2 * a + 1] = acc[2 * a + 1] + w_re * v_im - w_im * v_re
                else:
                    acc[2 * a] = acc[2 * a] + w_re * v_re - w_im * v_im
                    acc[2 * a + 1] = acc[2 * a + 1] + w_re * v_im + w_im * v_re


def zeros(count):
    return [[jnp.zeros((8, 128), jnp.float32) for _ in range(6)] for _ in range(count)]


def edge_link(edge):
    return lambda a, b: (edge[a, b, 0], edge[a, b, 1])


def tile(ref, index):
    return jnp.concatenate([ref[index + (slice(0, 8),)], ref[index + (slice(8, 16),)]], axis=1)


def pack_edge(links, edge):
    low = low_half()
    for a in range(3):
        for b in range(3):
            for part in range(2):
                y_link = tile(links, (a, b, part)) * (-1.0 / 6.0)
                edge[a, b, part] = second_of(y_link, y_link, low)


def by_parity(run, pair, other):
    odd = lax.axis_index("space") % 2 == 1

    @pl.when(odd)
    def _():
        run(pair, other)

    @pl.when(jnp.logical_not(odd))
    def _():
        run(other, pair)


def pack_sources(first, src, edge, row0, row1, pair_out, other_out, arrived, sems):
    low = low_half()
    pairs = row0.shape[0]

    def fetch(i):
        here = pl.ds(2 * i, 2)
        there = pl.ds(first + 2 * i, 2)
        return pltpu.make_async_copy(src.at[there], arrived.at[here], sems.at[i])

    for i in range(pairs):
        fetch(i).start()

    def finish(down, up):
        def step(i, carry):
            fetch(i).wait()
            upper = []
            for k in range(6):
                p = tile(arrived, (2 * i, k))
                q = tile(arrived, (2 * i + 1, k))
                row0[i, k] = down[i, k] = first_of(p, q, low)
                upper.append(second_of(p, q, low))
                row1[i, k] = upper[k]
            sums = zeros(1)
            mat_vec(edge_link(edge), [upper], sums, dagger=True)
            for k in range(6):
                up[i, k] = sums[0][k]
            return carry

        lax.fori_loop(0, pairs, step, 0)

    return lambda: by_parity(finish, pair_out, other_out)


def first_pack_kernel(
    first, src, links, edge, row0, row1, pair_out, other_out, arrived, y_links, sems, link_sem
):
    link_copy = pltpu.make_async_copy(links.at[1], y_links, link_sem)
    link_copy.start()
    finish = pack_sources(first, src, edge, row0, row1, pair_out, other_out, arrived, sems)
    link_copy.wait()
    pack_edge(y_links, edge)
    finish()


def pack_kernel(first, src, edge, row0, row1, pair_out, other_out, arrived, sems):
    pack_sources(first, src, edge, row0, row1, pair_out, other_out, arrived, sems)()


def link_kernel(links, inner):
    low = low_half()
    z = lane_ids() % LS
    even = sublane_ids() % 2 == 0
    for a in range(3):
        for b in range(3):
            for part in range(2):
                sign = 1.0 - 2.0 * part
                x_link = tile(links, (0, a, b, part)) * (-1.0 / 6.0)
                y_link = tile(links, (1, a, b, part)) * (-1.0 / 6.0)
                z_link = tile(links, (2, a, b, part)) * (-1.0 / 6.0)
                for row, pick in enumerate((first_of, second_of)):
                    inner[row, 0, a, b, part] = pick(x_link, x_link, low)
                    u_z = pick(z_link, z_link, low)
                    inner[row, 1, a, b, part] = u_z
                    inner[row, 2, b, a, part] = sign * z_prev(u_z, z)
                u_y = first_of(y_link, y_link, low)
                inner[0, 3, a, b, part] = u_y
                inner[1, 3, b, a, part] = sign * u_y
    for row in range(2):
        for part in range(2):
            sign = 1.0 - 2.0 * part
            own = [[inner[row, 0, a, b, part] for b in range(3)] for a in range(3)]
            for a in range(3):
                for b in range(3):
                    inner[row, 0, a, b, part] = own[a][b] + sign * x_other(own[b][a], even)


def inner_kernel(coeff, width, y0, y1, inner, v0, v1, sum0, sum1):
    z = lane_ids() % LS
    even = sublane_ids() % 2 == 0

    def step(i, carry):
        pairs = [i * width + w for w in range(width)]
        for row, (here, there, start, out) in enumerate(((y0, y1, v0, sum0), (y1, y0, v1, sum1))):
            sums = [[coeff * start[n, k] for k in range(6)] for n in pairs]

            def term(index, vectors):
                mat_vec(
                    lambda a, b: (inner[row, index, a, b, 0], inner[row, index, a, b, 1]),
                    vectors,
                    sums,
                )

            term(0, [[x_other(here[n, k], even) for k in range(6)] for n in pairs])
            term(1, [[z_next(here[n, k], z) for k in range(6)] for n in pairs])
            term(2, [[z_prev(here[n, k], z) for k in range(6)] for n in pairs])
            term(3, [[there[n, k] for k in range(6)] for n in pairs])
            for n, acc in zip(pairs, sums):
                for k in range(6):
                    out[n, k] = acc[k]
        return carry

    lax.fori_loop(0, y0.shape[0] // width, step, 0)


def edge_sums(pairs, below, above, edge, sum0, sum1):
    lower = [[sum0[n, k] + below[n, k] for k in range(6)] for n in pairs]
    upper = [[sum1[n, k] for k in range(6)] for n in pairs]
    mat_vec(edge_link(edge), [[above[n, k] for k in range(6)] for n in pairs], upper)
    return lower, upper


def edge_kernel(
    width, pair_in, other_in, edge, sum0, sum1, row0, row1, pair_out, other_out
):
    def run(lower_side, upper_side):
        below, down = lower_side
        above, up = upper_side

        def step(i, carry):
            pairs = [i * width + w for w in range(width)]
            lower, upper = edge_sums(pairs, below, above, edge, sum0, sum1)
            back = zeros(width)
            mat_vec(edge_link(edge), upper, back, dagger=True)
            for n, bottom, top, product in zip(pairs, lower, upper, back):
                for k in range(6):
                    row0[n, k] = down[n, k] = bottom[k]
                    row1[n, k] = top[k]
                    up[n, k] = product[k]
            return carry

        lax.fori_loop(0, row0.shape[0] // width, step, 0)

    by_parity(run, (pair_in, pair_out), (other_in, other_out))


def last_kernel(first, lead, pair_in, other_in, edge, sum0, sum1, *rest):
    out, filled, sems = rest[-3:]
    low = low_half()
    pairs = sum0.shape[0]

    def store(i):
        here = pl.ds(2 * i, 2)
        there = pl.ds(first + 2 * i, 2)
        return pltpu.make_async_copy(filled.at[here], out.at[there], sems.at[i])

    def run(below, above):
        def step(i, carry):
            (lower,), (upper,) = edge_sums([i], below, above, edge, sum0, sum1)
            for k in range(6):
                p = first_of(lower[k], upper[k], low) * lead
                q = second_of(lower[k], upper[k], low) * lead
                for m, value in ((2 * i, p), (2 * i + 1, q)):
                    filled[m, k, 0:8] = value[:, : 2 * LS]
                    filled[m, k, 8:16] = value[:, 2 * LS :]
            store(i).start()
            return carry

        lax.fori_loop(0, pairs, step, 0)

    def drain(i, carry):
        store(i).wait()
        return carry

    by_parity(run, pair_in, other_in)
    lax.fori_loop(0, pairs, drain, 0)


VMEM_LIMIT = 32 * 1024 * 1024
CHUNKS = 2


def call(kernel, outs, args, flops, scratch=(), in_hbm=(), out_hbm=False, aliases={}):
    moved = sum(4 * a.size for a in args) + sum(4 * o.size for o in outs)
    args = [
        pltpu.with_memory_space_constraint(a, pltpu.HBM) if i in in_hbm else a
        for i, a in enumerate(args)
    ]
    vmem = pl.BlockSpec(memory_space=pltpu.VMEM)
    hbm = pl.BlockSpec(memory_space=pltpu.HBM)
    return pl.pallas_call(
        kernel,
        out_shape=outs,
        in_specs=[hbm if i in in_hbm else vmem for i in range(len(args))],
        out_specs=[hbm if out_hbm else vmem] * len(outs),
        scratch_shapes=list(scratch),
        input_output_aliases=aliases,
        compiler_params=pltpu.CompilerParams(vmem_limit_bytes=VMEM_LIMIT),
        cost_estimate=pl.CostEstimate(flops=flops, bytes_accessed=moved, transcendentals=0),
    )(*args)


def halo_body(links, sources):
    vectors = sources.shape[0]
    share = vectors // CHUNKS
    pairs = share // 2
    width = 2
    sites, planes = links.shape[4:]
    f32 = functools.partial(jax.ShapeDtypeStruct, dtype=jnp.float32)
    field = f32((pairs, 6, 8, 128))
    inner_shape = f32((2, 4, 3, 3, 2, 8, 128))
    edge_shape = f32((3, 3, 2, 8, 128))
    source_view = jnp.swapaxes(sources, 3, 4).reshape(vectors, 6, planes, sites)
    link_view = jnp.swapaxes(links, 4, 5)
    powers = power_coeffs()
    lead = powers[4]
    work = 2 * pairs * 36 * 2 * 1024
    count = lax.axis_size("space")
    pairing = [(d, d ^ 1) for d in range(count)]
    others = [(d, (d + 1 if d % 2 else d - 1) % count) for d in range(count)]

    def exchange(to_pair, to_other):
        far = lax.ppermute(to_other, "space", others)
        return lax.ppermute(to_pair, "space", pairing), far

    arrived = pltpu.VMEM((share, 6, planes, sites), jnp.float32)
    sems = pltpu.SemaphoreType.DMA((pairs,))

    edge = None
    start, halo = [], []
    for chunk in range(CHUNKS):
        if chunk == 0:
            edge, row0, row1, *sends = call(
                functools.partial(first_pack_kernel, 0),
                [edge_shape, field, field, field, field],
                [source_view, link_view],
                work,
                [
                    arrived,
                    pltpu.VMEM(link_view.shape[1:], jnp.float32),
                    sems,
                    pltpu.SemaphoreType.DMA,
                ],
                (0, 1),
            )
        else:
            row0, row1, *sends = call(
                functools.partial(pack_kernel, chunk * share),
                [field, field, field, field],
                [source_view, edge],
                work,
                [arrived, sems],
                (0,),
            )
        start.append((row0, row1))
        halo.append(exchange(*sends))
    (inner,) = call(link_kernel, [inner_shape], [link_view], 8 * 18 * 1024)
    current = list(start)
    out = None
    for power in (3, 2, 1, 0):
        for chunk in range(CHUNKS):
            sum0, sum1 = call(
                functools.partial(inner_kernel, powers[power] / lead, width),
                [field, field],
                [*current[chunk], inner, *start[chunk]],
                4 * work,
            )
            args = [*halo[chunk], edge, sum0, sum1]
            if power:
                row0, row1, *sends = call(
                    functools.partial(edge_kernel, width), [field, field, field, field], args, work
                )
                current[chunk] = (row0, row1)
                halo[chunk] = exchange(*sends)
            else:
                (out,) = call(
                    functools.partial(last_kernel, chunk * share, lead),
                    [f32(source_view.shape)],
                    args if out is None else args + [out],
                    work,
                    [arrived, sems],
                    () if out is None else (len(args),),
                    True,
                    {} if out is None else {len(args): 0},
                )
    return jnp.swapaxes(out.reshape(vectors, 3, 2, planes, sites), 3, 4)


def shifted(value, axis, steps):
    count = lax.axis_size(axis)
    pairs = [(source, (source + steps) % count) for source in range(count)]
    return lax.ppermute(value, axis, pairs)


def apply_link(link, vector):
    real_part = 0.0
    imag_part = 0.0
    for column in range(3):
        link_re = link[:, column, 0][None]
        link_im = link[:, column, 1][None]
        vec_re = vector[:, column, 0][:, None]
        vec_im = vector[:, column, 1][:, None]
        real_part = real_part + link_re * vec_re - link_im * vec_im
        imag_part = imag_part + link_re * vec_im + link_im * vec_re
    return jnp.stack([real_part, imag_part], axis=2)


def apply_dagger(link, vector):
    real_part = 0.0
    imag_part = 0.0
    for column in range(3):
        link_re = link[column, :, 0][None]
        link_im = link[column, :, 1][None]
        vec_re = vector[:, column, 0][:, None]
        vec_im = vector[:, column, 1][:, None]
        real_part = real_part + link_re * vec_re + link_im * vec_im
        imag_part = imag_part + link_re * vec_im - link_im * vec_re
    return jnp.stack([real_part, imag_part], axis=2)


def z_ahead(array, extent, z_index):
    return jnp.where(
        z_index == extent - 1, jnp.roll(array, extent - 1, axis=-1), jnp.roll(array, -1, axis=-1)
    )


def z_behind(array, extent, z_index):
    return jnp.where(
        z_index == 0, jnp.roll(array, 1 - extent, axis=-1), jnp.roll(array, 1, axis=-1)
    )


def plane_body(links, sources):
    device_count = lax.axis_size("space")
    slabs = device_count // NT
    yz_local = links.shape[4]
    planes = links.shape[5] // device_count
    plane_sites = yz_local * device_count
    vectors = sources.shape[0]
    link_parts = links.reshape(54, yz_local, NT, slabs, planes)
    source_parts = sources.reshape(vectors * 6, yz_local, NT, slabs, planes)
    link_send = jnp.transpose(link_parts, (0, 3, 2, 4, 1)).reshape(
        54, device_count, planes, yz_local
    )
    source_send = jnp.transpose(source_parts, (0, 3, 2, 4, 1)).reshape(
        vectors * 6, device_count, planes, yz_local
    )
    link_recv, source_recv = (
        lax.all_to_all(link_send, "space", split_axis=1, concat_axis=3, tiled=True),
        lax.all_to_all(source_send, "space", split_axis=1, concat_axis=3, tiled=True),
    )
    gauge_local = link_recv.reshape(3, 3, 3, 2, planes, plane_sites)
    source_field = source_recv.reshape(vectors, 3, 2, planes, plane_sites)
    z_index = jnp.arange(plane_sites, dtype=jnp.int32) % LS
    x_top = gauge_local[0]
    x_rest = gauge_local[0][:, :, :, :-1]
    y_back = jnp.roll(gauge_local[1], LS, axis=-1)
    z_back = z_behind(gauge_local[2], LS, z_index)

    def fetch_lower(vector):
        return shifted(apply_dagger(x_top, vector), "space", NT)

    def hop_sum(vector):
        upper_face = shifted(vector, "space", -NT)
        lower_face = fetch_lower(vector)
        ahead = apply_link(
            gauge_local[0], jnp.concatenate([vector[:, :, :, 1:], upper_face], axis=3)
        )
        behind = jnp.concatenate([lower_face, apply_dagger(x_rest, vector[:, :, :, :-1])], axis=3)
        summed = ahead + behind
        summed = (
            summed
            + apply_link(gauge_local[1], jnp.roll(vector, -LS, axis=-1))
            + apply_dagger(y_back, jnp.roll(vector, LS, axis=-1))
        )
        summed = (
            summed
            + apply_link(gauge_local[2], z_ahead(vector, LS, z_index))
            + apply_dagger(z_back, z_behind(vector, LS, z_index))
        )
        return summed

    def scaled(vector):
        return hop_sum(vector) * (-1.0 / 6.0)

    previous = source_field
    current = scaled(previous)
    filtered = cheb_coeffs[0] * previous + cheb_coeffs[1] * current
    for degree in range(2, 5):
        following = 2.0 * scaled(current) - previous
        filtered = filtered + cheb_coeffs[degree] * following
        previous, current = (current, following)
    outgoing = filtered.reshape(vectors * 6, 1, planes, plane_sites)
    returned = lax.all_to_all(outgoing, "space", split_axis=3, concat_axis=1, tiled=True)
    ordered = jnp.transpose(
        returned.reshape(vectors * 6, slabs, NT, planes, yz_local), (0, 4, 2, 1, 3)
    )
    return ordered.reshape(vectors, 3, 2, yz_local, NT * slabs * planes)


def body(links, sources):
    sites, planes = sources.shape[3:]
    if sites == 2 * LS and planes == 2 * NT and sources.shape[0] % (4 * CHUNKS) == 0:
        return halo_body(links, sources)
    return plane_body(links, sources)


def solution(mesh):
    in_specs = (
        P(None, None, None, None, "space", "groups"),
        P(None, None, None, "space", "groups"),
    )
    out_specs = P(None, None, None, "space", "groups")
    return jax.shard_map(body, mesh=mesh, in_specs=in_specs, out_specs=out_specs, check_vma=False)
```

```python
import functools

import jax
import jax.numpy as jnp
from jax import lax
from jax.experimental import pallas as pl
from jax.experimental.pallas import tpu as pltpu
from jax.sharding import PartitionSpec as P

NT = 8
LS = 32

cheb_coeffs = (0.6, -0.5, 0.35, -0.25, 0.15)


def power_coeffs():
    c0, c1, c2, c3, c4 = cheb_coeffs
    return (c0 - c2 + c4, c1 - 3.0 * c3, 2.0 * c2 - 8.0 * c4, 4.0 * c3, 8.0 * c4)


def lane_ids():
    return lax.broadcasted_iota(jnp.int32, (8, 128), 1)


def sublane_ids():
    return lax.broadcasted_iota(jnp.int32, (8, 128), 0)


def low_half():
    return (lane_ids() // LS) % 2 == 0


def first_of(p, q, low):
    return jnp.where(low, p, pltpu.roll(q, LS, 1))


def second_of(p, q, low):
    return jnp.where(low, pltpu.roll(p, 128 - LS, 1), q)


def z_next(value, z):
    return jnp.where(z == LS - 1, pltpu.roll(value, LS - 1, 1), pltpu.roll(value, 127, 1))


def z_prev(value, z):
    return jnp.where(z == 0, pltpu.roll(value, 129 - LS, 1), pltpu.roll(value, 1, 1))


def x_other(value, even):
    return jnp.where(even, pltpu.roll(value, 7, 0), pltpu.roll(value, 1, 0))


def mat_vec(load, vectors, sums, dagger=False):
    for a in range(3):
        for b in range(3):
            w_re, w_im = load(b, a) if dagger else load(a, b)
            for vec, acc in zip(vectors, sums):
                v_re, v_im = vec[2 * b], vec[2 * b + 1]
                if dagger:
                    acc[2 * a] = acc[2 * a] + w_re * v_re + w_im * v_im
                    acc[2 * a + 1] = acc[2 * a + 1] + w_re * v_im - w_im * v_re
                else:
                    acc[2 * a] = acc[2 * a] + w_re * v_re - w_im * v_im
                    acc[2 * a + 1] = acc[2 * a + 1] + w_re * v_im + w_im * v_re


def zeros(count):
    return [[jnp.zeros((8, 128), jnp.float32) for _ in range(6)] for _ in range(count)]


def edge_link(edge):
    return lambda a, b: (edge[a, b, 0], edge[a, b, 1])


def tile(ref, index):
    return jnp.concatenate([ref[index + (slice(0, 8),)], ref[index + (slice(8, 16),)]], axis=1)


def pack_edge(links, edge):
    low = low_half()
    for a in range(3):
        for b in range(3):
            for part in range(2):
                y_link = tile(links, (a, b, part)) * (-1.0 / 6.0)
                edge[a, b, part] = second_of(y_link, y_link, low)


def by_parity(run, pair, other):
    odd = lax.axis_index("space") % 2 == 1

    @pl.when(odd)
    def _():
        run(pair, other)

    @pl.when(jnp.logical_not(odd))
    def _():
        run(other, pair)


def pack_sources(source, edge, row0, row1, pair_out, other_out):
    low = low_half()

    def run(down, up):
        for n in range(row0.shape[0]):
            upper = []
            for k in range(6):
                p, q = source(2 * n, k), source(2 * n + 1, k)
                row0[n, k] = down[n, k] = first_of(p, q, low)
                upper.append(second_of(p, q, low))
                row1[n, k] = upper[k]
            sums = zeros(1)
            mat_vec(edge_link(edge), [upper], sums, dagger=True)
            for k in range(6):
                up[n, k] = sums[0][k]

    by_parity(run, pair_out, other_out)


def first_pack_kernel(src, links, edge, row0, row1, other_out, pair_out, later, now, y_links, sems):
    count = now.shape[0]
    copies = [
        pltpu.make_async_copy(links.at[1], y_links, sems.at[0]),
        pltpu.make_async_copy(src.at[pl.ds(0, count)], now, sems.at[1]),
        pltpu.make_async_copy(src.at[pl.ds(count, later.shape[0])], later, sems.at[2]),
    ]
    for copy in copies:
        copy.start()
    copies[0].wait()
    pack_edge(y_links, edge)
    copies[1].wait()
    pack_sources(lambda n, k: tile(now, (n, k)), edge, row0, row1, pair_out, other_out)
    copies[2].wait()


def pack_kernel(first, later, edge, row0, row1, other_out, pair_out):
    pack_sources(lambda n, k: tile(later, (first + n, k)), edge, row0, row1, pair_out, other_out)


def link_kernel(links, inner):
    low = low_half()
    z = lane_ids() % LS
    even = sublane_ids() % 2 == 0
    for a in range(3):
        for b in range(3):
            for part in range(2):
                sign = 1.0 - 2.0 * part
                x_link = tile(links, (0, a, b, part)) * (-1.0 / 6.0)
                y_link = tile(links, (1, a, b, part)) * (-1.0 / 6.0)
                z_link = tile(links, (2, a, b, part)) * (-1.0 / 6.0)
                for row, pick in enumerate((first_of, second_of)):
                    inner[row, 0, a, b, part] = pick(x_link, x_link, low)
                    u_z = pick(z_link, z_link, low)
                    inner[row, 1, a, b, part] = u_z
                    inner[row, 2, b, a, part] = sign * z_prev(u_z, z)
                u_y = first_of(y_link, y_link, low)
                inner[0, 3, a, b, part] = u_y
                inner[1, 3, b, a, part] = sign * u_y
    for row in range(2):
        for part in range(2):
            sign = 1.0 - 2.0 * part
            own = [[inner[row, 0, a, b, part] for b in range(3)] for a in range(3)]
            for a in range(3):
                for b in range(3):
                    inner[row, 0, a, b, part] = own[a][b] + sign * x_other(own[b][a], even)


def inner_kernel(coeff, width, y0, y1, inner, v0, v1, sum0, sum1):
    z = lane_ids() % LS
    even = sublane_ids() % 2 == 0

    for i in range(y0.shape[0] // width):
        pairs = [i * width + w for w in range(width)]
        for row, (here, there, start, out) in enumerate(((y0, y1, v0, sum0), (y1, y0, v1, sum1))):
            sums = [[coeff * start[n, k] for k in range(6)] for n in pairs]

            def term(index, vectors):
                mat_vec(
                    lambda a, b: (inner[row, index, a, b, 0], inner[row, index, a, b, 1]),
                    vectors,
                    sums,
                )

            term(0, [[x_other(here[n, k], even) for k in range(6)] for n in pairs])
            term(1, [[z_next(here[n, k], z) for k in range(6)] for n in pairs])
            term(2, [[z_prev(here[n, k], z) for k in range(6)] for n in pairs])
            term(3, [[there[n, k] for k in range(6)] for n in pairs])
            for n, acc in zip(pairs, sums):
                for k in range(6):
                    out[n, k] = acc[k]


def edge_sums(pairs, below, above, edge, sum0, sum1):
    lower = [[sum0[n, k] + below[n, k] for k in range(6)] for n in pairs]
    upper = [[sum1[n, k] for k in range(6)] for n in pairs]
    mat_vec(edge_link(edge), [[above[n, k] for k in range(6)] for n in pairs], upper)
    return lower, upper


def edge_kernel(
    width, other_in, pair_in, edge, sum0, sum1, row0, row1, other_out, pair_out
):
    def run(lower_side, upper_side):
        below, down = lower_side
        above, up = upper_side

        for i in range(row0.shape[0] // width):
            pairs = [i * width + w for w in range(width)]
            lower, upper = edge_sums(pairs, below, above, edge, sum0, sum1)
            back = zeros(width)
            mat_vec(edge_link(edge), upper, back, dagger=True)
            for n, bottom, top, product in zip(pairs, lower, upper, back):
                for k in range(6):
                    row0[n, k] = down[n, k] = bottom[k]
                    row1[n, k] = top[k]
                    up[n, k] = product[k]

    by_parity(run, (pair_in, pair_out), (other_in, other_out))


def last_kernel(first, lead, other_in, pair_in, edge, sum0, sum1, *rest):
    out, filled, sems = rest[-3:]
    low = low_half()
    pairs = sum0.shape[0]

    def store(i):
        here = pl.ds(2 * i, 2)
        there = pl.ds(first + 2 * i, 2)
        return pltpu.make_async_copy(filled.at[here], out.at[there], sems.at[i])

    def run(below, above):
        for i in range(pairs):
            (lower,), (upper,) = edge_sums([i], below, above, edge, sum0, sum1)
            for k in range(6):
                p = first_of(lower[k], upper[k], low) * lead
                q = second_of(lower[k], upper[k], low) * lead
                for m, value in ((2 * i, p), (2 * i + 1, q)):
                    filled[m, k, 0:8] = value[:, : 2 * LS]
                    filled[m, k, 8:16] = value[:, 2 * LS :]
            store(i).start()

    by_parity(run, pair_in, other_in)
    for i in range(pairs):
        store(i).wait()


VMEM_LIMIT = 32 * 1024 * 1024
CHUNKS = 2


def call(kernel, outs, args, flops, scratch=(), in_hbm=(), out_hbm=False, aliases={}):
    moved = sum(4 * a.size for a in args) + sum(4 * o.size for o in outs)
    args = [
        pltpu.with_memory_space_constraint(a, pltpu.HBM) if i in in_hbm else a
        for i, a in enumerate(args)
    ]
    vmem = pl.BlockSpec(memory_space=pltpu.VMEM)
    hbm = pl.BlockSpec(memory_space=pltpu.HBM)
    return pl.pallas_call(
        kernel,
        out_shape=outs,
        in_specs=[hbm if i in in_hbm else vmem for i in range(len(args))],
        out_specs=[hbm if out_hbm else vmem] * len(outs),
        scratch_shapes=list(scratch),
        input_output_aliases=aliases,
        compiler_params=pltpu.CompilerParams(vmem_limit_bytes=VMEM_LIMIT),
        cost_estimate=pl.CostEstimate(flops=flops, bytes_accessed=moved, transcendentals=0),
    )(*args)


def halo_body(links, sources):
    vectors = sources.shape[0]
    share = vectors // CHUNKS
    pairs = share // 2
    width = 2
    sites, planes = links.shape[4:]
    f32 = functools.partial(jax.ShapeDtypeStruct, dtype=jnp.float32)
    field = f32((pairs, 6, 8, 128))
    inner_shape = f32((2, 4, 3, 3, 2, 8, 128))
    edge_shape = f32((3, 3, 2, 8, 128))
    source_view = jnp.swapaxes(sources, 3, 4).reshape(vectors, 6, planes, sites)
    link_view = jnp.swapaxes(links, 4, 5)
    powers = power_coeffs()
    lead = powers[4]
    work = 2 * pairs * 36 * 2 * 1024
    count = lax.axis_size("space")
    pairing = [(d, d ^ 1) for d in range(count)]
    others = [(d, (d + 1 if d % 2 else d - 1) % count) for d in range(count)]

    def exchange(to_other, to_pair):
        far = lax.ppermute(to_other, "space", others)
        return far, lax.ppermute(to_pair, "space", pairing)

    chunk_shape = (share, 6, planes, sites)

    edge, row0, row1, *sends, later = call(
        first_pack_kernel,
        [edge_shape, field, field, field, field, f32((vectors - share, 6, planes, sites))],
        [source_view, link_view],
        work,
        [
            pltpu.VMEM(chunk_shape, jnp.float32),
            pltpu.VMEM(link_view.shape[1:], jnp.float32),
            pltpu.SemaphoreType.DMA((3,)),
        ],
        (0, 1),
    )
    start, halo = [(row0, row1)], [exchange(*sends)]
    for chunk in range(1, CHUNKS):
        row0, row1, *sends = call(
            functools.partial(pack_kernel, (chunk - 1) * share),
            [field, field, field, field],
            [later, edge],
            work,
        )
        start.append((row0, row1))
        halo.append(exchange(*sends))
    (inner,) = call(link_kernel, [inner_shape], [link_view], 8 * 18 * 1024)
    current = list(start)
    out = None
    for power in (3, 2, 1, 0):
        for chunk in range(CHUNKS):
            sum0, sum1 = call(
                functools.partial(inner_kernel, powers[power] / lead, width),
                [field, field],
                [*current[chunk], inner, *start[chunk]],
                4 * work,
            )
            args = [*halo[chunk], edge, sum0, sum1]
            if power:
                row0, row1, *sends = call(
                    functools.partial(edge_kernel, width), [field, field, field, field], args, work
                )
                current[chunk] = (row0, row1)
                halo[chunk] = exchange(*sends)
            else:
                (out,) = call(
                    functools.partial(last_kernel, chunk * share, lead),
                    [f32(source_view.shape)],
                    args if out is None else args + [out],
                    work,
                    [pltpu.VMEM(chunk_shape, jnp.float32), pltpu.SemaphoreType.DMA((pairs,))],
                    () if out is None else (len(args),),
                    True,
                    {} if out is None else {len(args): 0},
                )
    return jnp.swapaxes(out.reshape(vectors, 3, 2, planes, sites), 3, 4)


def shifted(value, axis, steps):
    count = lax.axis_size(axis)
    pairs = [(source, (source + steps) % count) for source in range(count)]
    return lax.ppermute(value, axis, pairs)


def apply_link(link, vector):
    real_part = 0.0
    imag_part = 0.0
    for column in range(3):
        link_re = link[:, column, 0][None]
        link_im = link[:, column, 1][None]
        vec_re = vector[:, column, 0][:, None]
        vec_im = vector[:, column, 1][:, None]
        real_part = real_part + link_re * vec_re - link_im * vec_im
        imag_part = imag_part + link_re * vec_im + link_im * vec_re
    return jnp.stack([real_part, imag_part], axis=2)


def apply_dagger(link, vector):
    real_part = 0.0
    imag_part = 0.0
    for column in range(3):
        link_re = link[column, :, 0][None]
        link_im = link[column, :, 1][None]
        vec_re = vector[:, column, 0][:, None]
        vec_im = vector[:, column, 1][:, None]
        real_part = real_part + link_re * vec_re + link_im * vec_im
        imag_part = imag_part + link_re * vec_im - link_im * vec_re
    return jnp.stack([real_part, imag_part], axis=2)


def z_ahead(array, extent, z_index):
    return jnp.where(
        z_index == extent - 1, jnp.roll(array, extent - 1, axis=-1), jnp.roll(array, -1, axis=-1)
    )


def z_behind(array, extent, z_index):
    return jnp.where(
        z_index == 0, jnp.roll(array, 1 - extent, axis=-1), jnp.roll(array, 1, axis=-1)
    )


def plane_body(links, sources):
    device_count = lax.axis_size("space")
    slabs = device_count // NT
    yz_local = links.shape[4]
    planes = links.shape[5] // device_count
    plane_sites = yz_local * device_count
    vectors = sources.shape[0]
    link_parts = links.reshape(54, yz_local, NT, slabs, planes)
    source_parts = sources.reshape(vectors * 6, yz_local, NT, slabs, planes)
    link_send = jnp.transpose(link_parts, (0, 3, 2, 4, 1)).reshape(
        54, device_count, planes, yz_local
    )
    source_send = jnp.transpose(source_parts, (0, 3, 2, 4, 1)).reshape(
        vectors * 6, device_count, planes, yz_local
    )
    link_recv, source_recv = (
        lax.all_to_all(link_send, "space", split_axis=1, concat_axis=3, tiled=True),
        lax.all_to_all(source_send, "space", split_axis=1, concat_axis=3, tiled=True),
    )
    gauge_local = link_recv.reshape(3, 3, 3, 2, planes, plane_sites)
    source_field = source_recv.reshape(vectors, 3, 2, planes, plane_sites)
    z_index = jnp.arange(plane_sites, dtype=jnp.int32) % LS
    x_top = gauge_local[0]
    x_rest = gauge_local[0][:, :, :, :-1]
    y_back = jnp.roll(gauge_local[1], LS, axis=-1)
    z_back = z_behind(gauge_local[2], LS, z_index)

    def fetch_lower(vector):
        return shifted(apply_dagger(x_top, vector), "space", NT)

    def hop_sum(vector):
        upper_face = shifted(vector, "space", -NT)
        lower_face = fetch_lower(vector)
        ahead = apply_link(
            gauge_local[0], jnp.concatenate([vector[:, :, :, 1:], upper_face], axis=3)
        )
        behind = jnp.concatenate([lower_face, apply_dagger(x_rest, vector[:, :, :, :-1])], axis=3)
        summed = ahead + behind
        summed = (
            summed
            + apply_link(gauge_local[1], jnp.roll(vector, -LS, axis=-1))
            + apply_dagger(y_back, jnp.roll(vector, LS, axis=-1))
        )
        summed = (
            summed
            + apply_link(gauge_local[2], z_ahead(vector, LS, z_index))
            + apply_dagger(z_back, z_behind(vector, LS, z_index))
        )
        return summed

    def scaled(vector):
        return hop_sum(vector) * (-1.0 / 6.0)

    previous = source_field
    current = scaled(previous)
    filtered = cheb_coeffs[0] * previous + cheb_coeffs[1] * current
    for degree in range(2, 5):
        following = 2.0 * scaled(current) - previous
        filtered = filtered + cheb_coeffs[degree] * following
        previous, current = (current, following)
    outgoing = filtered.reshape(vectors * 6, 1, planes, plane_sites)
    returned = lax.all_to_all(outgoing, "space", split_axis=3, concat_axis=1, tiled=True)
    ordered = jnp.transpose(
        returned.reshape(vectors * 6, slabs, NT, planes, yz_local), (0, 4, 2, 1, 3)
    )
    return ordered.reshape(vectors, 3, 2, yz_local, NT * slabs * planes)


def body(links, sources):
    sites, planes = sources.shape[3:]
    if sites == 2 * LS and planes == 2 * NT and sources.shape[0] % (4 * CHUNKS) == 0:
        return halo_body(links, sources)
    return plane_body(links, sources)


def solution(mesh):
    in_specs = (
        P(None, None, None, None, "space", "groups"),
        P(None, None, None, "space", "groups"),
    )
    out_specs = P(None, None, None, "space", "groups")
    return jax.shard_map(body, mesh=mesh, in_specs=in_specs, out_specs=out_specs, check_vma=False)
```

```python
import functools

import jax
import jax.numpy as jnp
from jax import lax
from jax.experimental import pallas as pl
from jax.experimental.pallas import tpu as pltpu
from jax.sharding import PartitionSpec as P

NT = 8
LS = 32

cheb_coeffs = (0.6, -0.5, 0.35, -0.25, 0.15)


def power_coeffs():
    c0, c1, c2, c3, c4 = cheb_coeffs
    return (c0 - c2 + c4, c1 - 3.0 * c3, 2.0 * c2 - 8.0 * c4, 4.0 * c3, 8.0 * c4)


def lane_ids():
    return lax.broadcasted_iota(jnp.int32, (8, 128), 1)


def sublane_ids():
    return lax.broadcasted_iota(jnp.int32, (8, 128), 0)


def low_half():
    return (lane_ids() // LS) % 2 == 0


def first_of(p, q, low):
    return jnp.where(low, p, pltpu.roll(q, LS, 1))


def second_of(p, q, low):
    return jnp.where(low, pltpu.roll(p, 128 - LS, 1), q)


def z_next(value, z):
    return jnp.where(z == LS - 1, pltpu.roll(value, LS - 1, 1), pltpu.roll(value, 127, 1))


def z_prev(value, z):
    return jnp.where(z == 0, pltpu.roll(value, 129 - LS, 1), pltpu.roll(value, 1, 1))


def x_other(value, even):
    return jnp.where(even, pltpu.roll(value, 7, 0), pltpu.roll(value, 1, 0))


def mat_vec(load, vectors, sums, dagger=False):
    for a in range(3):
        for b in range(3):
            w_re, w_im = load(b, a) if dagger else load(a, b)
            for vec, acc in zip(vectors, sums):
                v_re, v_im = vec[2 * b], vec[2 * b + 1]
                if dagger:
                    acc[2 * a] = acc[2 * a] + w_re * v_re + w_im * v_im
                    acc[2 * a + 1] = acc[2 * a + 1] + w_re * v_im - w_im * v_re
                else:
                    acc[2 * a] = acc[2 * a] + w_re * v_re - w_im * v_im
                    acc[2 * a + 1] = acc[2 * a + 1] + w_re * v_im + w_im * v_re


def zeros(count):
    return [[jnp.zeros((8, 128), jnp.float32) for _ in range(6)] for _ in range(count)]


def link_at(ref, *index):
    return lambda a, b: (ref[index + (a, b, 0)], ref[index + (a, b, 1)])


def tile(ref, index):
    return jnp.concatenate([ref[index + (slice(0, 8),)], ref[index + (slice(8, 16),)]], axis=1)


def by_parity(run, near, far):
    odd = lax.axis_index("space") % 2 == 1

    @pl.when(odd)
    def _():
        run(near, far)

    @pl.when(jnp.logical_not(odd))
    def _():
        run(far, near)


def groups(ref):
    width = 2 if ref.shape[1] % 2 == 0 else 1
    return [range(i, i + width) for i in range(0, ref.shape[1], width)]


def take(ref, row, pairs):
    return [[ref[row, n, k] for k in range(6)] for n in pairs]


def put(ref, row, pairs, vectors):
    for n, vec in zip(pairs, vectors):
        for k in range(6):
            ref[row, n, k] = vec[k]


def pack_links(links, inner, edge):
    low = low_half()
    z = lane_ids() % LS
    even = sublane_ids() % 2 == 0
    for a in range(3):
        for b in range(3):
            for part in range(2):
                sign = 1.0 - 2.0 * part
                x_link, y_link, z_link = (
                    tile(links, (mu, a, b, part)) * (-1.0 / 6.0) for mu in range(3)
                )
                for row, pick in enumerate((first_of, second_of)):
                    inner[row, 0, a, b, part] = pick(x_link, x_link, low)
                    u_z = pick(z_link, z_link, low)
                    inner[row, 1, a, b, part] = u_z
                    inner[row, 2, b, a, part] = sign * z_prev(u_z, z)
                u_y = first_of(y_link, y_link, low)
                inner[0, 3, a, b, part] = u_y
                inner[1, 3, b, a, part] = sign * u_y
                edge[a, b, part] = second_of(y_link, y_link, low)
    for row in range(2):
        for part in range(2):
            sign = 1.0 - 2.0 * part
            own = [[inner[row, 0, a, b, part] for b in range(3)] for a in range(3)]
            for a in range(3):
                for b in range(3):
                    inner[row, 0, a, b, part] = own[a][b] + sign * x_other(own[b][a], even)


def add_inner(inner, row, pairs, field, sums):
    z = lane_ids() % LS
    even = sublane_ids() % 2 == 0
    here = take(field, row, pairs)
    mat_vec(link_at(inner, row, 0), [[x_other(c, even) for c in vec] for vec in here], sums)
    mat_vec(link_at(inner, row, 1), [[z_next(c, z) for c in vec] for vec in here], sums)
    mat_vec(link_at(inner, row, 2), [[z_prev(c, z) for c in vec] for vec in here], sums)
    mat_vec(link_at(inner, row, 3), take(field, 1 - row, pairs), sums)


def scaled_rows(coeff, start, row, pairs):
    return [[coeff * c for c in vec] for vec in take(start, row, pairs)]


def open_round(coeff, pairs, rows, start, inner, edge, sums_out, down, up):
    for row in range(2):
        sums = scaled_rows(coeff, start, row, pairs)
        add_inner(inner, row, pairs, rows, sums)
        put(sums_out, row, pairs, sums)
        if row == 0:
            put(down, 0, pairs, take(rows, 0, pairs))
            put(down, 1, pairs, sums)
        else:
            for i, vectors in enumerate((take(rows, 1, pairs), sums)):
                back = zeros(len(pairs))
                mat_vec(link_at(edge), vectors, back, dagger=True)
                put(up, i, pairs, back)


def close_round(coeff, pairs, below, above, rows, sums_in, start, inner, edge, middle):
    lower = [
        [s + u for s, u in zip(*both)]
        for both in zip(take(sums_in, 0, pairs), take(below, 0, pairs))
    ]
    put(middle, 0, pairs, lower)
    upper = take(sums_in, 1, pairs)
    mat_vec(link_at(edge), take(above, 0, pairs), upper)
    put(middle, 1, pairs, upper)
    result = []
    for row in range(2):
        sums = [
            [c + (1.0 / 36.0) * r for c, r in zip(*both)]
            for both in zip(scaled_rows(coeff, start, row, pairs), take(rows, row, pairs))
        ]
        add_inner(inner, row, pairs, middle, sums)
        if row == 0:
            sums = [
                [s + u for s, u in zip(*both)] for both in zip(sums, take(below, 1, pairs))
            ]
        else:
            mat_vec(link_at(edge), take(above, 1, pairs), sums)
        result.append(sums)
    return result


def pack_rows(source, rows):
    low = low_half()
    for n in range(rows.shape[1]):
        for k in range(6):
            p, q = source(2 * n, k), source(2 * n + 1, k)
            rows[0, n, k] = first_of(p, q, low)
            rows[1, n, k] = second_of(p, q, low)


def start_chunk(coeff, rows, inner, edge, sums, far_out, near_out):
    def run(down, up):
        for pairs in groups(rows):
            open_round(coeff, pairs, rows, rows, inner, edge, sums, down, up)

    by_parity(run, near_out, far_out)


def first_kernel(
    coeff, src, links, inner, edge, rows, sums, far_out, near_out, later, now, held, sems
):
    count = now.shape[0]
    copies = [
        pltpu.make_async_copy(links, held, sems.at[0]),
        pltpu.make_async_copy(src.at[pl.ds(0, count)], now, sems.at[1]),
        pltpu.make_async_copy(src.at[pl.ds(count, later.shape[0])], later, sems.at[2]),
    ]
    for copy in copies:
        copy.start()
    copies[0].wait()
    pack_links(held, inner, edge)
    copies[1].wait()
    pack_rows(lambda n, k: tile(now, (n, k)), rows)
    start_chunk(coeff, rows, inner, edge, sums, far_out, near_out)
    copies[2].wait()


def start_kernel(coeff, first, later, inner, edge, rows, sums, far_out, near_out):
    pack_rows(lambda n, k: tile(later, (first + n, k)), rows)
    start_chunk(coeff, rows, inner, edge, sums, far_out, near_out)


def round_kernel(
    coeff,
    next_coeff,
    far_in,
    near_in,
    rows,
    sums_in,
    start,
    inner,
    edge,
    rows_out,
    sums_out,
    far_out,
    near_out,
    middle,
):
    def run(lower_side, upper_side):
        below, down = lower_side
        above, up = upper_side
        for pairs in groups(rows):
            result = close_round(
                coeff, pairs, below, above, rows, sums_in, start, inner, edge, middle
            )
            for row in range(2):
                put(rows_out, row, pairs, result[row])
            open_round(next_coeff, pairs, rows_out, start, inner, edge, sums_out, down, up)

    by_parity(run, (near_in, near_out), (far_in, far_out))


def last_kernel(coeff, first, lead, far_in, near_in, rows, sums_in, start, inner, edge, *rest):
    out, middle, filled, sems = rest[-4:]
    low = low_half()

    def store(n):
        here = pl.ds(2 * n, 2)
        there = pl.ds(first + 2 * n, 2)
        return pltpu.make_async_copy(filled.at[here], out.at[there], sems.at[n])

    def run(below, above):
        for pairs in groups(rows):
            lower, upper = close_round(
                coeff, pairs, below, above, rows, sums_in, start, inner, edge, middle
            )
            for n, bottom, top in zip(pairs, lower, upper):
                for k in range(6):
                    p = first_of(bottom[k], top[k], low) * lead
                    q = second_of(bottom[k], top[k], low) * lead
                    for m, value in ((2 * n, p), (2 * n + 1, q)):
                        filled[m, k, 0:8] = value[:, : 2 * LS]
                        filled[m, k, 8:16] = value[:, 2 * LS :]
                store(n).start()

    by_parity(run, near_in, far_in)
    for n in range(rows.shape[1]):
        store(n).wait()


VMEM_LIMIT = 32 * 1024 * 1024
CHUNKS = 2


def call(kernel, outs, args, flops, scratch=(), in_hbm=(), out_hbm=False, aliases={}):
    moved = sum(4 * a.size for a in args) + sum(4 * o.size for o in outs)
    args = [
        pltpu.with_memory_space_constraint(a, pltpu.HBM) if i in in_hbm else a
        for i, a in enumerate(args)
    ]
    vmem = pl.BlockSpec(memory_space=pltpu.VMEM)
    hbm = pl.BlockSpec(memory_space=pltpu.HBM)
    return pl.pallas_call(
        kernel,
        out_shape=outs,
        in_specs=[hbm if i in in_hbm else vmem for i in range(len(args))],
        out_specs=[hbm if out_hbm else vmem] * len(outs),
        scratch_shapes=list(scratch),
        input_output_aliases=aliases,
        compiler_params=pltpu.CompilerParams(vmem_limit_bytes=VMEM_LIMIT),
        cost_estimate=pl.CostEstimate(flops=flops, bytes_accessed=moved, transcendentals=0),
    )(*args)


def halo_body(links, sources):
    vectors = sources.shape[0]
    share = vectors // CHUNKS
    pairs = share // 2
    sites, planes = links.shape[4:]
    f32 = functools.partial(jax.ShapeDtypeStruct, dtype=jnp.float32)
    both = f32((2, pairs, 6, 8, 128))
    middle = pltpu.VMEM(both.shape, jnp.float32)
    source_view = jnp.swapaxes(sources, 3, 4).reshape(vectors, 6, planes, sites)
    link_view = jnp.swapaxes(links, 4, 5)
    chunk_shape = (share, 6, planes, sites)
    powers = power_coeffs()
    lead = powers[4]
    steps = [powers[power] / lead for power in (3, 2, 1, 0)]
    work = 2 * pairs * 36 * 2 * 1024
    count = lax.axis_size("space")
    near_pairs = [(d, d ^ 1) for d in range(count)]
    far_pairs = [(d, (d + 1 if d % 2 else d - 1) % count) for d in range(count)]

    def exchange(far_out, near_out):
        far = lax.ppermute(far_out, "space", far_pairs)
        return far, lax.ppermute(near_out, "space", near_pairs)

    inner, edge, rows, sums, *sends, later = call(
        functools.partial(first_kernel, steps[0]),
        [
            f32((2, 4, 3, 3, 2, 8, 128)),
            f32((3, 3, 2, 8, 128)),
            *[both] * 4,
            f32((vectors - share, 6, planes, sites)),
        ],
        [source_view, link_view],
        6 * work,
        [
            pltpu.VMEM(chunk_shape, jnp.float32),
            pltpu.VMEM(link_view.shape, jnp.float32),
            pltpu.SemaphoreType.DMA((3,)),
        ],
        (0, 1),
    )
    start, fields, halos = [rows], [(rows, sums)], [exchange(*sends)]
    for chunk in range(1, CHUNKS):
        rows, sums, *sends = call(
            functools.partial(start_kernel, steps[0], (chunk - 1) * share),
            [both] * 4,
            [later, inner, edge],
            6 * work,
        )
        start.append(rows)
        fields.append((rows, sums))
        halos.append(exchange(*sends))
    for chunk in range(CHUNKS):
        rows, sums, *sends = call(
            functools.partial(round_kernel, steps[1], steps[2]),
            [both] * 4,
            [*halos[chunk], *fields[chunk], start[chunk], inner, edge],
            12 * work,
            [middle],
        )
        fields[chunk] = (rows, sums)
        halos[chunk] = exchange(*sends)
    out = None
    for chunk in range(CHUNKS):
        args = [*halos[chunk], *fields[chunk], start[chunk], inner, edge]
        (out,) = call(
            functools.partial(last_kernel, steps[3], chunk * share, lead),
            [f32(source_view.shape)],
            args if out is None else args + [out],
            6 * work,
            [middle, pltpu.VMEM(chunk_shape, jnp.float32), pltpu.SemaphoreType.DMA((pairs,))],
            () if out is None else (len(args),),
            True,
            {} if out is None else {len(args): 0},
        )
    return jnp.swapaxes(out.reshape(vectors, 3, 2, planes, sites), 3, 4)


def shifted(value, axis, steps):
    count = lax.axis_size(axis)
    pairs = [(source, (source + steps) % count) for source in range(count)]
    return lax.ppermute(value, axis, pairs)


def apply_link(link, vector):
    real_part = 0.0
    imag_part = 0.0
    for column in range(3):
        link_re = link[:, column, 0][None]
        link_im = link[:, column, 1][None]
        vec_re = vector[:, column, 0][:, None]
        vec_im = vector[:, column, 1][:, None]
        real_part = real_part + link_re * vec_re - link_im * vec_im
        imag_part = imag_part + link_re * vec_im + link_im * vec_re
    return jnp.stack([real_part, imag_part], axis=2)


def apply_dagger(link, vector):
    real_part = 0.0
    imag_part = 0.0
    for column in range(3):
        link_re = link[column, :, 0][None]
        link_im = link[column, :, 1][None]
        vec_re = vector[:, column, 0][:, None]
        vec_im = vector[:, column, 1][:, None]
        real_part = real_part + link_re * vec_re + link_im * vec_im
        imag_part = imag_part + link_re * vec_im - link_im * vec_re
    return jnp.stack([real_part, imag_part], axis=2)


def z_ahead(array, extent, z_index):
    return jnp.where(
        z_index == extent - 1, jnp.roll(array, extent - 1, axis=-1), jnp.roll(array, -1, axis=-1)
    )


def z_behind(array, extent, z_index):
    return jnp.where(
        z_index == 0, jnp.roll(array, 1 - extent, axis=-1), jnp.roll(array, 1, axis=-1)
    )


def plane_body(links, sources):
    device_count = lax.axis_size("space")
    slabs = device_count // NT
    yz_local = links.shape[4]
    planes = links.shape[5] // device_count
    plane_sites = yz_local * device_count
    vectors = sources.shape[0]
    link_parts = links.reshape(54, yz_local, NT, slabs, planes)
    source_parts = sources.reshape(vectors * 6, yz_local, NT, slabs, planes)
    link_send = jnp.transpose(link_parts, (0, 3, 2, 4, 1)).reshape(
        54, device_count, planes, yz_local
    )
    source_send = jnp.transpose(source_parts, (0, 3, 2, 4, 1)).reshape(
        vectors * 6, device_count, planes, yz_local
    )
    link_recv, source_recv = (
        lax.all_to_all(link_send, "space", split_axis=1, concat_axis=3, tiled=True),
        lax.all_to_all(source_send, "space", split_axis=1, concat_axis=3, tiled=True),
    )
    gauge_local = link_recv.reshape(3, 3, 3, 2, planes, plane_sites)
    source_field = source_recv.reshape(vectors, 3, 2, planes, plane_sites)
    z_index = jnp.arange(plane_sites, dtype=jnp.int32) % LS
    x_top = gauge_local[0]
    x_rest = gauge_local[0][:, :, :, :-1]
    y_back = jnp.roll(gauge_local[1], LS, axis=-1)
    z_back = z_behind(gauge_local[2], LS, z_index)

    def fetch_lower(vector):
        return shifted(apply_dagger(x_top, vector), "space", NT)

    def hop_sum(vector):
        upper_face = shifted(vector, "space", -NT)
        lower_face = fetch_lower(vector)
        ahead = apply_link(
            gauge_local[0], jnp.concatenate([vector[:, :, :, 1:], upper_face], axis=3)
        )
        behind = jnp.concatenate([lower_face, apply_dagger(x_rest, vector[:, :, :, :-1])], axis=3)
        summed = ahead + behind
        summed = (
            summed
            + apply_link(gauge_local[1], jnp.roll(vector, -LS, axis=-1))
            + apply_dagger(y_back, jnp.roll(vector, LS, axis=-1))
        )
        summed = (
            summed
            + apply_link(gauge_local[2], z_ahead(vector, LS, z_index))
            + apply_dagger(z_back, z_behind(vector, LS, z_index))
        )
        return summed

    def scaled(vector):
        return hop_sum(vector) * (-1.0 / 6.0)

    previous = source_field
    current = scaled(previous)
    filtered = cheb_coeffs[0] * previous + cheb_coeffs[1] * current
    for degree in range(2, 5):
        following = 2.0 * scaled(current) - previous
        filtered = filtered + cheb_coeffs[degree] * following
        previous, current = (current, following)
    outgoing = filtered.reshape(vectors * 6, 1, planes, plane_sites)
    returned = lax.all_to_all(outgoing, "space", split_axis=3, concat_axis=1, tiled=True)
    ordered = jnp.transpose(
        returned.reshape(vectors * 6, slabs, NT, planes, yz_local), (0, 4, 2, 1, 3)
    )
    return ordered.reshape(vectors, 3, 2, yz_local, NT * slabs * planes)


def body(links, sources):
    sites, planes = sources.shape[3:]
    if sites == 2 * LS and planes == 2 * NT and sources.shape[0] % (2 * CHUNKS) == 0:
        return halo_body(links, sources)
    return plane_body(links, sources)


def solution(mesh):
    in_specs = (
        P(None, None, None, None, "space", "groups"),
        P(None, None, None, "space", "groups"),
    )
    out_specs = P(None, None, None, "space", "groups")
    return jax.shard_map(body, mesh=mesh, in_specs=in_specs, out_specs=out_specs, check_vma=False)
```

```python
import functools

import jax
import jax.numpy as jnp
from jax import lax
from jax.experimental import pallas as pl
from jax.experimental.pallas import tpu as pltpu
from jax.sharding import PartitionSpec as P

NT = 8
LS = 32

cheb_coeffs = (0.6, -0.5, 0.35, -0.25, 0.15)


def power_coeffs():
    c0, c1, c2, c3, c4 = cheb_coeffs
    return (c0 - c2 + c4, c1 - 3.0 * c3, 2.0 * c2 - 8.0 * c4, 4.0 * c3, 8.0 * c4)


def lane_ids():
    return lax.broadcasted_iota(jnp.int32, (8, 128), 1)


def sublane_ids():
    return lax.broadcasted_iota(jnp.int32, (8, 128), 0)


def low_half():
    return (lane_ids() // LS) % 2 == 0


def first_of(p, q, low):
    return jnp.where(low, p, pltpu.roll(q, LS, 1))


def second_of(p, q, low):
    return jnp.where(low, pltpu.roll(p, 128 - LS, 1), q)


def z_next(value, z):
    return jnp.where(z == LS - 1, pltpu.roll(value, LS - 1, 1), pltpu.roll(value, 127, 1))


def z_prev(value, z):
    return jnp.where(z == 0, pltpu.roll(value, 129 - LS, 1), pltpu.roll(value, 1, 1))


def x_other(value, even):
    return jnp.where(even, pltpu.roll(value, 7, 0), pltpu.roll(value, 1, 0))


def mat_vec(load, vectors, sums, dagger=False):
    for a in range(3):
        for b in range(3):
            w_re, w_im = load(b, a) if dagger else load(a, b)
            for vec, acc in zip(vectors, sums):
                v_re, v_im = vec[2 * b], vec[2 * b + 1]
                if dagger:
                    acc[2 * a] = acc[2 * a] + w_re * v_re + w_im * v_im
                    acc[2 * a + 1] = acc[2 * a + 1] + w_re * v_im - w_im * v_re
                else:
                    acc[2 * a] = acc[2 * a] + w_re * v_re - w_im * v_im
                    acc[2 * a + 1] = acc[2 * a + 1] + w_re * v_im + w_im * v_re


def zeros(count):
    return [[jnp.zeros((8, 128), jnp.float32) for _ in range(6)] for _ in range(count)]


def link_at(ref, *index):
    return lambda a, b: (ref[index + (a, b, 0)], ref[index + (a, b, 1)])


def tile(ref, index):
    return jnp.concatenate([ref[index + (slice(0, 8),)], ref[index + (slice(8, 16),)]], axis=1)


def by_parity(run, near, far):
    odd = lax.axis_index("space") % 2 == 1

    @pl.when(odd)
    def _():
        run(near, far)

    @pl.when(jnp.logical_not(odd))
    def _():
        run(far, near)


def groups(ref):
    width = 2 if ref.shape[1] % 2 == 0 else 1
    return [range(i, i + width) for i in range(0, ref.shape[1], width)]


def take(ref, row, pairs):
    return [[ref[row, n, k] for k in range(6)] for n in pairs]


def put(ref, row, pairs, vectors):
    for n, vec in zip(pairs, vectors):
        for k in range(6):
            ref[row, n, k] = vec[k]


def pack_links(links, inner, edge):
    low = low_half()
    z = lane_ids() % LS
    even = sublane_ids() % 2 == 0
    for a in range(3):
        for b in range(3):
            for part in range(2):
                sign = 1.0 - 2.0 * part
                x_link, y_link, z_link = (
                    tile(links, (mu, a, b, part)) * (-1.0 / 6.0) for mu in range(3)
                )
                for row, pick in enumerate((first_of, second_of)):
                    inner[row, 0, a, b, part] = pick(x_link, x_link, low)
                    u_z = pick(z_link, z_link, low)
                    inner[row, 1, a, b, part] = u_z
                    inner[row, 2, b, a, part] = sign * z_prev(u_z, z)
                u_y = first_of(y_link, y_link, low)
                inner[0, 3, a, b, part] = u_y
                inner[1, 3, b, a, part] = sign * u_y
                edge[a, b, part] = second_of(y_link, y_link, low)
    for row in range(2):
        for part in range(2):
            sign = 1.0 - 2.0 * part
            own = [[inner[row, 0, a, b, part] for b in range(3)] for a in range(3)]
            for a in range(3):
                for b in range(3):
                    inner[row, 0, a, b, part] = own[a][b] + sign * x_other(own[b][a], even)


def add_inner(inner, row, pairs, field, sums):
    z = lane_ids() % LS
    even = sublane_ids() % 2 == 0
    here = take(field, row, pairs)
    mat_vec(link_at(inner, row, 0), [[x_other(c, even) for c in vec] for vec in here], sums)
    mat_vec(link_at(inner, row, 1), [[z_next(c, z) for c in vec] for vec in here], sums)
    mat_vec(link_at(inner, row, 2), [[z_prev(c, z) for c in vec] for vec in here], sums)
    mat_vec(link_at(inner, row, 3), take(field, 1 - row, pairs), sums)


def scaled_rows(coeff, start, row, pairs):
    return [[coeff * c for c in vec] for vec in take(start, row, pairs)]


def open_round(coeff, pairs, rows, start, inner, edge, sums_out, down, up):
    for row in range(2):
        sums = scaled_rows(coeff, start, row, pairs)
        add_inner(inner, row, pairs, rows, sums)
        put(sums_out, row, pairs, sums)
        if row == 0:
            put(down, 0, pairs, take(rows, 0, pairs))
            put(down, 1, pairs, sums)
        else:
            for i, vectors in enumerate((take(rows, 1, pairs), sums)):
                back = zeros(len(pairs))
                mat_vec(link_at(edge), vectors, back, dagger=True)
                put(up, i, pairs, back)


def close_round(coeff, pairs, below, above, rows, sums_in, start, inner, edge, middle):
    lower = [
        [s + u for s, u in zip(*both)]
        for both in zip(take(sums_in, 0, pairs), take(below, 0, pairs))
    ]
    put(middle, 0, pairs, lower)
    upper = take(sums_in, 1, pairs)
    mat_vec(link_at(edge), take(above, 0, pairs), upper)
    put(middle, 1, pairs, upper)
    result = []
    for row in range(2):
        sums = [
            [c + (1.0 / 36.0) * r for c, r in zip(*both)]
            for both in zip(scaled_rows(coeff, start, row, pairs), take(rows, row, pairs))
        ]
        add_inner(inner, row, pairs, middle, sums)
        if row == 0:
            sums = [
                [s + u for s, u in zip(*both)] for both in zip(sums, take(below, 1, pairs))
            ]
        else:
            mat_vec(link_at(edge), take(above, 1, pairs), sums)
        result.append(sums)
    return result


def pack_rows(source, rows):
    low = low_half()
    for n in range(rows.shape[1]):
        for k in range(6):
            p, q = source(2 * n, k), source(2 * n + 1, k)
            rows[0, n, k] = first_of(p, q, low)
            rows[1, n, k] = second_of(p, q, low)


def start_chunk(coeff, rows, inner, edge, sums, far_out, near_out):
    def run(down, up):
        for pairs in groups(rows):
            open_round(coeff, pairs, rows, rows, inner, edge, sums, down, up)

    by_parity(run, near_out, far_out)


def first_kernel(
    coeff, src, links, inner, edge, rows, sums, far_out, near_out, later, now, held, sems
):
    count = now.shape[0]
    copies = [
        pltpu.make_async_copy(links, held, sems.at[0]),
        pltpu.make_async_copy(src.at[pl.ds(0, count)], now, sems.at[1]),
        pltpu.make_async_copy(src.at[pl.ds(count, later.shape[0])], later, sems.at[2]),
    ]
    for copy in copies:
        copy.start()
    copies[0].wait()
    pack_links(held, inner, edge)
    copies[1].wait()
    pack_rows(lambda n, k: tile(now, (n, k)), rows)
    start_chunk(coeff, rows, inner, edge, sums, far_out, near_out)
    copies[2].wait()


def start_kernel(coeff, first, later, inner, edge, rows, sums, far_out, near_out):
    pack_rows(lambda n, k: tile(later, (first + n, k)), rows)
    start_chunk(coeff, rows, inner, edge, sums, far_out, near_out)


def round_kernel(
    coeff,
    next_coeff,
    far_in,
    near_in,
    rows,
    sums_in,
    start,
    inner,
    edge,
    rows_out,
    sums_out,
    far_out,
    near_out,
    middle,
):
    def run(lower_side, upper_side):
        below, down = lower_side
        above, up = upper_side
        for pairs in groups(rows):
            result = close_round(
                coeff, pairs, below, above, rows, sums_in, start, inner, edge, middle
            )
            for row in range(2):
                put(rows_out, row, pairs, result[row])
            open_round(next_coeff, pairs, rows_out, start, inner, edge, sums_out, down, up)

    by_parity(run, (near_in, near_out), (far_in, far_out))


def last_kernel(coeff, first, lead, far_in, near_in, rows, sums_in, start, inner, edge, *rest):
    out, middle, filled, sems = rest[-4:]
    low = low_half()

    def store(n):
        here = pl.ds(2 * n, 2)
        there = pl.ds(first + 2 * n, 2)
        return pltpu.make_async_copy(filled.at[here], out.at[there], sems.at[n])

    def run(below, above):
        for pairs in groups(rows):
            lower, upper = close_round(
                coeff, pairs, below, above, rows, sums_in, start, inner, edge, middle
            )
            for n, bottom, top in zip(pairs, lower, upper):
                for k in range(6):
                    p = first_of(bottom[k], top[k], low) * lead
                    q = second_of(bottom[k], top[k], low) * lead
                    for m, value in ((2 * n, p), (2 * n + 1, q)):
                        filled[m, k, 0:8] = value[:, : 2 * LS]
                        filled[m, k, 8:16] = value[:, 2 * LS :]
                store(n).start()

    by_parity(run, near_in, far_in)
    for n in range(rows.shape[1]):
        store(n).wait()


VMEM_LIMIT = 32 * 1024 * 1024
CHUNKS = 3


def call(kernel, outs, args, flops, scratch=(), in_hbm=(), out_hbm=False, aliases={}):
    moved = sum(4 * a.size for a in args) + sum(4 * o.size for o in outs)
    args = [
        pltpu.with_memory_space_constraint(a, pltpu.HBM) if i in in_hbm else a
        for i, a in enumerate(args)
    ]
    vmem = pl.BlockSpec(memory_space=pltpu.VMEM)
    hbm = pl.BlockSpec(memory_space=pltpu.HBM)
    return pl.pallas_call(
        kernel,
        out_shape=outs,
        in_specs=[hbm if i in in_hbm else vmem for i in range(len(args))],
        out_specs=[hbm if out_hbm else vmem] * len(outs),
        scratch_shapes=list(scratch),
        input_output_aliases=aliases,
        compiler_params=pltpu.CompilerParams(vmem_limit_bytes=VMEM_LIMIT),
        cost_estimate=pl.CostEstimate(flops=flops, bytes_accessed=moved, transcendentals=0),
    )(*args)


def halo_body(links, sources):
    vectors = sources.shape[0]
    share = vectors // CHUNKS
    pairs = share // 2
    sites, planes = links.shape[4:]
    f32 = functools.partial(jax.ShapeDtypeStruct, dtype=jnp.float32)
    both = f32((2, pairs, 6, 8, 128))
    middle = pltpu.VMEM(both.shape, jnp.float32)
    source_view = jnp.swapaxes(sources, 3, 4).reshape(vectors, 6, planes, sites)
    link_view = jnp.swapaxes(links, 4, 5)
    chunk_shape = (share, 6, planes, sites)
    powers = power_coeffs()
    lead = powers[4]
    steps = [powers[power] / lead for power in (3, 2, 1, 0)]
    work = 2 * pairs * 36 * 2 * 1024
    count = lax.axis_size("space")
    near_pairs = [(d, d ^ 1) for d in range(count)]
    far_pairs = [(d, (d + 1 if d % 2 else d - 1) % count) for d in range(count)]

    def exchange(far_out, near_out):
        far = lax.ppermute(far_out, "space", far_pairs)
        return far, lax.ppermute(near_out, "space", near_pairs)

    inner, edge, rows, sums, *sends, later = call(
        functools.partial(first_kernel, steps[0]),
        [
            f32((2, 4, 3, 3, 2, 8, 128)),
            f32((3, 3, 2, 8, 128)),
            *[both] * 4,
            f32((vectors - share, 6, planes, sites)),
        ],
        [source_view, link_view],
        6 * work,
        [
            pltpu.VMEM(chunk_shape, jnp.float32),
            pltpu.VMEM(link_view.shape, jnp.float32),
            pltpu.SemaphoreType.DMA((3,)),
        ],
        (0, 1),
    )
    start, fields, halos = [rows], [(rows, sums)], [exchange(*sends)]
    for chunk in range(1, CHUNKS):
        rows, sums, *sends = call(
            functools.partial(start_kernel, steps[0], (chunk - 1) * share),
            [both] * 4,
            [later, inner, edge],
            6 * work,
        )
        start.append(rows)
        fields.append((rows, sums))
        halos.append(exchange(*sends))
    for chunk in range(CHUNKS):
        rows, sums, *sends = call(
            functools.partial(round_kernel, steps[1], steps[2]),
            [both] * 4,
            [*halos[chunk], *fields[chunk], start[chunk], inner, edge],
            12 * work,
            [middle],
        )
        fields[chunk] = (rows, sums)
        halos[chunk] = exchange(*sends)
    out = None
    for chunk in range(CHUNKS):
        args = [*halos[chunk], *fields[chunk], start[chunk], inner, edge]
        (out,) = call(
            functools.partial(last_kernel, steps[3], chunk * share, lead),
            [f32(source_view.shape)],
            args if out is None else args + [out],
            6 * work,
            [middle, pltpu.VMEM(chunk_shape, jnp.float32), pltpu.SemaphoreType.DMA((pairs,))],
            () if out is None else (len(args),),
            True,
            {} if out is None else {len(args): 0},
        )
    return jnp.swapaxes(out.reshape(vectors, 3, 2, planes, sites), 3, 4)


def shifted(value, axis, steps):
    count = lax.axis_size(axis)
    pairs = [(source, (source + steps) % count) for source in range(count)]
    return lax.ppermute(value, axis, pairs)


def apply_link(link, vector):
    real_part = 0.0
    imag_part = 0.0
    for column in range(3):
        link_re = link[:, column, 0][None]
        link_im = link[:, column, 1][None]
        vec_re = vector[:, column, 0][:, None]
        vec_im = vector[:, column, 1][:, None]
        real_part = real_part + link_re * vec_re - link_im * vec_im
        imag_part = imag_part + link_re * vec_im + link_im * vec_re
    return jnp.stack([real_part, imag_part], axis=2)


def apply_dagger(link, vector):
    real_part = 0.0
    imag_part = 0.0
    for column in range(3):
        link_re = link[column, :, 0][None]
        link_im = link[column, :, 1][None]
        vec_re = vector[:, column, 0][:, None]
        vec_im = vector[:, column, 1][:, None]
        real_part = real_part + link_re * vec_re + link_im * vec_im
        imag_part = imag_part + link_re * vec_im - link_im * vec_re
    return jnp.stack([real_part, imag_part], axis=2)


def z_ahead(array, extent, z_index):
    return jnp.where(
        z_index == extent - 1, jnp.roll(array, extent - 1, axis=-1), jnp.roll(array, -1, axis=-1)
    )


def z_behind(array, extent, z_index):
    return jnp.where(
        z_index == 0, jnp.roll(array, 1 - extent, axis=-1), jnp.roll(array, 1, axis=-1)
    )


def plane_body(links, sources):
    device_count = lax.axis_size("space")
    slabs = device_count // NT
    yz_local = links.shape[4]
    planes = links.shape[5] // device_count
    plane_sites = yz_local * device_count
    vectors = sources.shape[0]
    link_parts = links.reshape(54, yz_local, NT, slabs, planes)
    source_parts = sources.reshape(vectors * 6, yz_local, NT, slabs, planes)
    link_send = jnp.transpose(link_parts, (0, 3, 2, 4, 1)).reshape(
        54, device_count, planes, yz_local
    )
    source_send = jnp.transpose(source_parts, (0, 3, 2, 4, 1)).reshape(
        vectors * 6, device_count, planes, yz_local
    )
    link_recv, source_recv = (
        lax.all_to_all(link_send, "space", split_axis=1, concat_axis=3, tiled=True),
        lax.all_to_all(source_send, "space", split_axis=1, concat_axis=3, tiled=True),
    )
    gauge_local = link_recv.reshape(3, 3, 3, 2, planes, plane_sites)
    source_field = source_recv.reshape(vectors, 3, 2, planes, plane_sites)
    z_index = jnp.arange(plane_sites, dtype=jnp.int32) % LS
    x_top = gauge_local[0]
    x_rest = gauge_local[0][:, :, :, :-1]
    y_back = jnp.roll(gauge_local[1], LS, axis=-1)
    z_back = z_behind(gauge_local[2], LS, z_index)

    def fetch_lower(vector):
        return shifted(apply_dagger(x_top, vector), "space", NT)

    def hop_sum(vector):
        upper_face = shifted(vector, "space", -NT)
        lower_face = fetch_lower(vector)
        ahead = apply_link(
            gauge_local[0], jnp.concatenate([vector[:, :, :, 1:], upper_face], axis=3)
        )
        behind = jnp.concatenate([lower_face, apply_dagger(x_rest, vector[:, :, :, :-1])], axis=3)
        summed = ahead + behind
        summed = (
            summed
            + apply_link(gauge_local[1], jnp.roll(vector, -LS, axis=-1))
            + apply_dagger(y_back, jnp.roll(vector, LS, axis=-1))
        )
        summed = (
            summed
            + apply_link(gauge_local[2], z_ahead(vector, LS, z_index))
            + apply_dagger(z_back, z_behind(vector, LS, z_index))
        )
        return summed

    def scaled(vector):
        return hop_sum(vector) * (-1.0 / 6.0)

    previous = source_field
    current = scaled(previous)
    filtered = cheb_coeffs[0] * previous + cheb_coeffs[1] * current
    for degree in range(2, 5):
        following = 2.0 * scaled(current) - previous
        filtered = filtered + cheb_coeffs[degree] * following
        previous, current = (current, following)
    outgoing = filtered.reshape(vectors * 6, 1, planes, plane_sites)
    returned = lax.all_to_all(outgoing, "space", split_axis=3, concat_axis=1, tiled=True)
    ordered = jnp.transpose(
        returned.reshape(vectors * 6, slabs, NT, planes, yz_local), (0, 4, 2, 1, 3)
    )
    return ordered.reshape(vectors, 3, 2, yz_local, NT * slabs * planes)


def body(links, sources):
    sites, planes = sources.shape[3:]
    if sites == 2 * LS and planes == 2 * NT and sources.shape[0] % (2 * CHUNKS) == 0:
        return halo_body(links, sources)
    return plane_body(links, sources)


def solution(mesh):
    in_specs = (
        P(None, None, None, None, "space", "groups"),
        P(None, None, None, "space", "groups"),
    )
    out_specs = P(None, None, None, "space", "groups")
    return jax.shard_map(body, mesh=mesh, in_specs=in_specs, out_specs=out_specs, check_vma=False)
```

```python
import functools

import jax
import jax.numpy as jnp
from jax import lax
from jax.experimental import pallas as pl
from jax.experimental.pallas import tpu as pltpu
from jax.sharding import PartitionSpec as P

NT = 8
LS = 32

cheb_coeffs = (0.6, -0.5, 0.35, -0.25, 0.15)


def power_coeffs():
    c0, c1, c2, c3, c4 = cheb_coeffs
    return (c0 - c2 + c4, c1 - 3.0 * c3, 2.0 * c2 - 8.0 * c4, 4.0 * c3, 8.0 * c4)


def lane_ids():
    return lax.broadcasted_iota(jnp.int32, (8, 128), 1)


def sublane_ids():
    return lax.broadcasted_iota(jnp.int32, (8, 128), 0)


def low_half():
    return (lane_ids() // LS) % 2 == 0


def first_of(p, q, low):
    return jnp.where(low, p, pltpu.roll(q, LS, 1))


def second_of(p, q, low):
    return jnp.where(low, pltpu.roll(p, 128 - LS, 1), q)


def z_next(value, z):
    return jnp.where(z == LS - 1, pltpu.roll(value, LS - 1, 1), pltpu.roll(value, 127, 1))


def z_prev(value, z):
    return jnp.where(z == 0, pltpu.roll(value, 129 - LS, 1), pltpu.roll(value, 1, 1))


def x_other(value, even):
    return jnp.where(even, pltpu.roll(value, 7, 0), pltpu.roll(value, 1, 0))


def mat_vec(load, vectors, sums, dagger=False):
    for a in range(3):
        for b in range(3):
            w_re, w_im = load(b, a) if dagger else load(a, b)
            for vec, acc in zip(vectors, sums):
                v_re, v_im = vec[2 * b], vec[2 * b + 1]
                if dagger:
                    acc[2 * a] = acc[2 * a] + w_re * v_re + w_im * v_im
                    acc[2 * a + 1] = acc[2 * a + 1] + w_re * v_im - w_im * v_re
                else:
                    acc[2 * a] = acc[2 * a] + w_re * v_re - w_im * v_im
                    acc[2 * a + 1] = acc[2 * a + 1] + w_re * v_im + w_im * v_re


def zeros(count):
    return [[jnp.zeros((8, 128), jnp.float32) for _ in range(6)] for _ in range(count)]


def link_at(ref, *index):
    return lambda a, b: (ref[index + (a, b, 0)], ref[index + (a, b, 1)])


def tile(ref, index):
    return jnp.concatenate([ref[index + (slice(0, 8),)], ref[index + (slice(8, 16),)]], axis=1)


def by_parity(run, near, far):
    odd = lax.axis_index("space") % 2 == 1

    @pl.when(odd)
    def _():
        run(near, far)

    @pl.when(jnp.logical_not(odd))
    def _():
        run(far, near)


def groups(ref):
    count = ref.shape[1]
    return [range(i, min(i + 2, count)) for i in range(0, count, 2)]


def take(ref, row, pairs):
    return [[ref[row, n, k] for k in range(6)] for n in pairs]


def put(ref, row, pairs, vectors):
    for n, vec in zip(pairs, vectors):
        for k in range(6):
            ref[row, n, k] = vec[k]


def pack_links(links, inner, edge, arrive):
    low = low_half()
    z = lane_ids() % LS
    even = sublane_ids() % 2 == 0
    entries = [(a, b, part) for a in range(3) for b in range(3) for part in range(2)]
    rows = tuple(enumerate((first_of, second_of)))

    arrive(1)
    for a, b, part in entries:
        y_link = tile(links, (1, a, b, part)) * (-1.0 / 6.0)
        u_y = first_of(y_link, y_link, low)
        inner[0, 3, a, b, part] = u_y
        inner[1, 3, b, a, part] = u_y if part == 0 else -u_y
        edge[a, b, part] = second_of(y_link, y_link, low)
    arrive(2)
    for a, b, part in entries:
        z_link = tile(links, (2, a, b, part)) * (-1.0 / 6.0)
        for row, pick in rows:
            u_z = pick(z_link, z_link, low)
            inner[row, 1, a, b, part] = u_z
            u_z = z_prev(u_z, z)
            inner[row, 2, b, a, part] = u_z if part == 0 else -u_z
    arrive(0)
    for part in range(2):
        x_link = [
            [tile(links, (0, a, b, part)) * (-1.0 / 6.0) for b in range(3)] for a in range(3)
        ]
        for row, pick in rows:
            own = [[pick(entry, entry, low) for entry in line] for line in x_link]
            for a in range(3):
                for b in range(3):
                    other = x_other(own[b][a], even)
                    inner[row, 0, a, b, part] = own[a][b] + (other if part == 0 else -other)


def add_inner(inner, row, pairs, field, sums):
    z = lane_ids() % LS
    even = sublane_ids() % 2 == 0
    here = take(field, row, pairs)
    mat_vec(link_at(inner, row, 0), [[x_other(c, even) for c in vec] for vec in here], sums)
    mat_vec(link_at(inner, row, 1), [[z_next(c, z) for c in vec] for vec in here], sums)
    mat_vec(link_at(inner, row, 2), [[z_prev(c, z) for c in vec] for vec in here], sums)
    mat_vec(link_at(inner, row, 3), take(field, 1 - row, pairs), sums)


def scaled_rows(coeff, start, row, pairs):
    return [[coeff * c for c in vec] for vec in take(start, row, pairs)]


def open_round(coeff, pairs, rows, start, inner, edge, sums_out, down, up):
    for row in range(2):
        sums = scaled_rows(coeff, start, row, pairs)
        add_inner(inner, row, pairs, rows, sums)
        put(sums_out, row, pairs, sums)
        if row == 0:
            put(down, 0, pairs, take(rows, 0, pairs))
            put(down, 1, pairs, sums)
        else:
            for i, vectors in enumerate((take(rows, 1, pairs), sums)):
                back = zeros(len(pairs))
                mat_vec(link_at(edge), vectors, back, dagger=True)
                put(up, i, pairs, back)


def close_round(coeff, pairs, below, above, rows, sums_in, start, inner, edge, middle):
    lower = [
        [s + u for s, u in zip(*both)]
        for both in zip(take(sums_in, 0, pairs), take(below, 0, pairs))
    ]
    put(middle, 0, pairs, lower)
    upper = take(sums_in, 1, pairs)
    mat_vec(link_at(edge), take(above, 0, pairs), upper)
    put(middle, 1, pairs, upper)
    result = []
    for row in range(2):
        sums = [
            [c + (1.0 / 36.0) * r for c, r in zip(*both)]
            for both in zip(scaled_rows(coeff, start, row, pairs), take(rows, row, pairs))
        ]
        add_inner(inner, row, pairs, middle, sums)
        if row == 0:
            sums = [
                [s + u for s, u in zip(*both)] for both in zip(sums, take(below, 1, pairs))
            ]
        else:
            mat_vec(link_at(edge), take(above, 1, pairs), sums)
        result.append(sums)
    return result


def pack_rows(source, rows):
    low = low_half()
    for n in range(rows.shape[1]):
        for k in range(6):
            p, q = source(2 * n, k), source(2 * n + 1, k)
            rows[0, n, k] = first_of(p, q, low)
            rows[1, n, k] = second_of(p, q, low)


def start_chunk(coeff, rows, inner, edge, sums, far_out, near_out):
    def run(down, up):
        for pairs in groups(rows):
            open_round(coeff, pairs, rows, rows, inner, edge, sums, down, up)

    by_parity(run, near_out, far_out)


def first_kernel(
    coeff, src, links, inner, edge, rows, sums, far_out, near_out, later, now, held, sems
):
    count = now.shape[0]
    link_copies = [
        pltpu.make_async_copy(links.at[mu], held.at[mu], sems.at[mu]) for mu in range(3)
    ]
    first_copy = pltpu.make_async_copy(src.at[pl.ds(0, count)], now, sems.at[3])
    rest = src.at[pl.ds(count, later.shape[0])]
    later_copy = pltpu.make_async_copy(rest, later, sems.at[4])
    link_copies[1].start()
    first_copy.start()
    link_copies[2].start()
    link_copies[0].start()
    later_copy.start()
    pack_links(held, inner, edge, lambda mu: link_copies[mu].wait())
    first_copy.wait()
    pack_rows(lambda n, k: tile(now, (n, k)), rows)
    start_chunk(coeff, rows, inner, edge, sums, far_out, near_out)
    later_copy.wait()


def start_kernel(coeff, first, later, inner, edge, rows, sums, far_out, near_out):
    pack_rows(lambda n, k: tile(later, (first + n, k)), rows)
    start_chunk(coeff, rows, inner, edge, sums, far_out, near_out)


def round_kernel(
    coeff,
    next_coeff,
    far_in,
    near_in,
    rows,
    sums_in,
    start,
    inner,
    edge,
    all_started,
    rows_out,
    sums_out,
    far_out,
    near_out,
    middle,
):
    del all_started

    def run(lower_side, upper_side):
        below, down = lower_side
        above, up = upper_side
        for pairs in groups(rows):
            result = close_round(
                coeff, pairs, below, above, rows, sums_in, start, inner, edge, middle
            )
            for row in range(2):
                put(rows_out, row, pairs, result[row])
            open_round(next_coeff, pairs, rows_out, start, inner, edge, sums_out, down, up)

    by_parity(run, (near_in, near_out), (far_in, far_out))


def last_kernel(coeff, first, lead, far_in, near_in, rows, sums_in, start, inner, edge, *rest):
    out, middle, filled, sems = rest[-4:]
    low = low_half()

    def store(n):
        here = pl.ds(2 * n, 2)
        there = pl.ds(first + 2 * n, 2)
        return pltpu.make_async_copy(filled.at[here], out.at[there], sems.at[n])

    def run(below, above):
        for pairs in groups(rows):
            lower, upper = close_round(
                coeff, pairs, below, above, rows, sums_in, start, inner, edge, middle
            )
            for n, bottom, top in zip(pairs, lower, upper):
                for k in range(6):
                    p = first_of(bottom[k], top[k], low) * lead
                    q = second_of(bottom[k], top[k], low) * lead
                    for m, value in ((2 * n, p), (2 * n + 1, q)):
                        filled[m, k, 0:8] = value[:, : 2 * LS]
                        filled[m, k, 8:16] = value[:, 2 * LS :]
                store(n).start()

    by_parity(run, near_in, far_in)
    for n in range(rows.shape[1]):
        store(n).wait()


VMEM_LIMIT = 32 * 1024 * 1024


def call(
    kernel, outs, args, flops, scratch=(), in_hbm=(), out_hbm=False, aliases={}, unread=()
):
    moved = sum(4 * a.size for a in args) + sum(4 * o.size for o in outs)
    args = [
        pltpu.with_memory_space_constraint(a, pltpu.HBM) if i in in_hbm else a
        for i, a in enumerate(args)
    ]
    vmem = pl.BlockSpec(memory_space=pltpu.VMEM)
    hbm = pl.BlockSpec(memory_space=pltpu.HBM)
    anywhere = pl.BlockSpec(memory_space=pl.ANY)
    return pl.pallas_call(
        kernel,
        out_shape=outs,
        in_specs=[
            hbm if i in in_hbm else anywhere if i in unread else vmem for i in range(len(args))
        ],
        out_specs=[hbm if out_hbm else vmem] * len(outs),
        scratch_shapes=list(scratch),
        input_output_aliases=aliases,
        compiler_params=pltpu.CompilerParams(vmem_limit_bytes=VMEM_LIMIT),
        cost_estimate=pl.CostEstimate(flops=flops, bytes_accessed=moved, transcendentals=0),
    )(*args)


def chunk_sizes(pairs):
    last = pairs // 4
    second = pairs // 3
    return (pairs - second - last, second, last)


def halo_body(links, sources):
    vectors = sources.shape[0]
    sizes = chunk_sizes(vectors // 2)
    chunks = range(len(sizes))
    first = [2 * sum(sizes[:chunk]) for chunk in chunks]
    sites, planes = links.shape[4:]
    f32 = functools.partial(jax.ShapeDtypeStruct, dtype=jnp.float32)
    both = [f32((2, pairs, 6, 8, 128)) for pairs in sizes]
    middle = [pltpu.VMEM(shape.shape, jnp.float32) for shape in both]
    raw = [(2 * pairs, 6, planes, sites) for pairs in sizes]
    source_view = jnp.swapaxes(sources, 3, 4).reshape(vectors, 6, planes, sites)
    link_view = jnp.swapaxes(links, 4, 5)
    powers = power_coeffs()
    lead = powers[4]
    steps = [powers[power] / lead for power in (3, 2, 1, 0)]
    work = [2 * pairs * 36 * 2 * 1024 for pairs in sizes]
    count = lax.axis_size("space")
    near_pairs = [(d, d ^ 1) for d in range(count)]
    far_pairs = [(d, (d + 1 if d % 2 else d - 1) % count) for d in range(count)]

    def exchange(far_out, near_out):
        far = lax.ppermute(far_out, "space", far_pairs)
        return far, lax.ppermute(near_out, "space", near_pairs)

    inner, edge, rows, sums, *sends, later = call(
        functools.partial(first_kernel, steps[0]),
        [
            f32((2, 4, 3, 3, 2, 8, 128)),
            f32((3, 3, 2, 8, 128)),
            *[both[0]] * 4,
            f32((vectors - first[1], 6, planes, sites)),
        ],
        [source_view, link_view],
        6 * work[0],
        [
            pltpu.VMEM(raw[0], jnp.float32),
            pltpu.VMEM(link_view.shape, jnp.float32),
            pltpu.SemaphoreType.DMA((5,)),
        ],
        (0, 1),
    )
    start, fields, halos = [rows], [(rows, sums)], [exchange(*sends)]
    for chunk in chunks[1:]:
        rows, sums, *sends = call(
            functools.partial(start_kernel, steps[0], first[chunk] - first[1]),
            [both[chunk]] * 4,
            [later, inner, edge],
            6 * work[chunk],
        )
        start.append(rows)
        fields.append((rows, sums))
        halos.append(exchange(*sends))
    for chunk in chunks:
        rows, sums, *sends = call(
            functools.partial(round_kernel, steps[1], steps[2]),
            [both[chunk]] * 4,
            [*halos[chunk], *fields[chunk], start[chunk], inner, edge, start[-1]],
            12 * work[chunk],
            [middle[chunk]],
            unread=(7,),
        )
        fields[chunk] = (rows, sums)
        halos[chunk] = exchange(*sends)
    out = None
    for chunk in chunks:
        args = [*halos[chunk], *fields[chunk], start[chunk], inner, edge]
        (out,) = call(
            functools.partial(last_kernel, steps[3], first[chunk], lead),
            [f32(source_view.shape)],
            args if out is None else args + [out],
            6 * work[chunk],
            [
                middle[chunk],
                pltpu.VMEM(raw[chunk], jnp.float32),
                pltpu.SemaphoreType.DMA((sizes[chunk],)),
            ],
            () if out is None else (len(args),),
            True,
            {} if out is None else {len(args): 0},
        )
    return jnp.swapaxes(out.reshape(vectors, 3, 2, planes, sites), 3, 4)


def shifted(value, axis, steps):
    count = lax.axis_size(axis)
    pairs = [(source, (source + steps) % count) for source in range(count)]
    return lax.ppermute(value, axis, pairs)


def apply_link(link, vector):
    real_part = 0.0
    imag_part = 0.0
    for column in range(3):
        link_re = link[:, column, 0][None]
        link_im = link[:, column, 1][None]
        vec_re = vector[:, column, 0][:, None]
        vec_im = vector[:, column, 1][:, None]
        real_part = real_part + link_re * vec_re - link_im * vec_im
        imag_part = imag_part + link_re * vec_im + link_im * vec_re
    return jnp.stack([real_part, imag_part], axis=2)


def apply_dagger(link, vector):
    real_part = 0.0
    imag_part = 0.0
    for column in range(3):
        link_re = link[column, :, 0][None]
        link_im = link[column, :, 1][None]
        vec_re = vector[:, column, 0][:, None]
        vec_im = vector[:, column, 1][:, None]
        real_part = real_part + link_re * vec_re + link_im * vec_im
        imag_part = imag_part + link_re * vec_im - link_im * vec_re
    return jnp.stack([real_part, imag_part], axis=2)


def z_ahead(array, extent, z_index):
    return jnp.where(
        z_index == extent - 1, jnp.roll(array, extent - 1, axis=-1), jnp.roll(array, -1, axis=-1)
    )


def z_behind(array, extent, z_index):
    return jnp.where(
        z_index == 0, jnp.roll(array, 1 - extent, axis=-1), jnp.roll(array, 1, axis=-1)
    )


def plane_body(links, sources):
    device_count = lax.axis_size("space")
    slabs = device_count // NT
    yz_local = links.shape[4]
    planes = links.shape[5] // device_count
    plane_sites = yz_local * device_count
    vectors = sources.shape[0]
    link_parts = links.reshape(54, yz_local, NT, slabs, planes)
    source_parts = sources.reshape(vectors * 6, yz_local, NT, slabs, planes)
    link_send = jnp.transpose(link_parts, (0, 3, 2, 4, 1)).reshape(
        54, device_count, planes, yz_local
    )
    source_send = jnp.transpose(source_parts, (0, 3, 2, 4, 1)).reshape(
        vectors * 6, device_count, planes, yz_local
    )
    link_recv, source_recv = (
        lax.all_to_all(link_send, "space", split_axis=1, concat_axis=3, tiled=True),
        lax.all_to_all(source_send, "space", split_axis=1, concat_axis=3, tiled=True),
    )
    gauge_local = link_recv.reshape(3, 3, 3, 2, planes, plane_sites)
    source_field = source_recv.reshape(vectors, 3, 2, planes, plane_sites)
    z_index = jnp.arange(plane_sites, dtype=jnp.int32) % LS
    x_top = gauge_local[0]
    x_rest = gauge_local[0][:, :, :, :-1]
    y_back = jnp.roll(gauge_local[1], LS, axis=-1)
    z_back = z_behind(gauge_local[2], LS, z_index)

    def fetch_lower(vector):
        return shifted(apply_dagger(x_top, vector), "space", NT)

    def hop_sum(vector):
        upper_face = shifted(vector, "space", -NT)
        lower_face = fetch_lower(vector)
        ahead = apply_link(
            gauge_local[0], jnp.concatenate([vector[:, :, :, 1:], upper_face], axis=3)
        )
        behind = jnp.concatenate([lower_face, apply_dagger(x_rest, vector[:, :, :, :-1])], axis=3)
        summed = ahead + behind
        summed = (
            summed
            + apply_link(gauge_local[1], jnp.roll(vector, -LS, axis=-1))
            + apply_dagger(y_back, jnp.roll(vector, LS, axis=-1))
        )
        summed = (
            summed
            + apply_link(gauge_local[2], z_ahead(vector, LS, z_index))
            + apply_dagger(z_back, z_behind(vector, LS, z_index))
        )
        return summed

    def scaled(vector):
        return hop_sum(vector) * (-1.0 / 6.0)

    previous = source_field
    current = scaled(previous)
    filtered = cheb_coeffs[0] * previous + cheb_coeffs[1] * current
    for degree in range(2, 5):
        following = 2.0 * scaled(current) - previous
        filtered = filtered + cheb_coeffs[degree] * following
        previous, current = (current, following)
    outgoing = filtered.reshape(vectors * 6, 1, planes, plane_sites)
    returned = lax.all_to_all(outgoing, "space", split_axis=3, concat_axis=1, tiled=True)
    ordered = jnp.transpose(
        returned.reshape(vectors * 6, slabs, NT, planes, yz_local), (0, 4, 2, 1, 3)
    )
    return ordered.reshape(vectors, 3, 2, yz_local, NT * slabs * planes)


def body(links, sources):
    sites, planes = sources.shape[3:]
    if sites == 2 * LS and planes == 2 * NT and sources.shape[0] % 8 == 0:
        return halo_body(links, sources)
    return plane_body(links, sources)


def solution(mesh):
    in_specs = (
        P(None, None, None, None, "space", "groups"),
        P(None, None, None, "space", "groups"),
    )
    out_specs = P(None, None, None, "space", "groups")
    return jax.shard_map(body, mesh=mesh, in_specs=in_specs, out_specs=out_specs, check_vma=False)
```

```python
import functools

import jax
import jax.numpy as jnp
from jax import lax
from jax.experimental import pallas as pl
from jax.experimental.pallas import tpu as pltpu
from jax.sharding import PartitionSpec as P

NT = 8
LS = 32

cheb_coeffs = (0.6, -0.5, 0.35, -0.25, 0.15)


def power_coeffs():
    c0, c1, c2, c3, c4 = cheb_coeffs
    return (c0 - c2 + c4, c1 - 3.0 * c3, 2.0 * c2 - 8.0 * c4, 4.0 * c3, 8.0 * c4)


def lane_ids():
    return lax.broadcasted_iota(jnp.int32, (8, 128), 1)


def sublane_ids():
    return lax.broadcasted_iota(jnp.int32, (8, 128), 0)


def low_half():
    return (lane_ids() // LS) % 2 == 0


def first_of(p, q, low):
    return jnp.where(low, p, pltpu.roll(q, LS, 1))


def second_of(p, q, low):
    return jnp.where(low, pltpu.roll(p, 128 - LS, 1), q)


def z_next(value, z):
    return jnp.where(z == LS - 1, pltpu.roll(value, LS - 1, 1), pltpu.roll(value, 127, 1))


def z_prev(value, z):
    return jnp.where(z == 0, pltpu.roll(value, 129 - LS, 1), pltpu.roll(value, 1, 1))


def x_other(value, even):
    return jnp.where(even, pltpu.roll(value, 7, 0), pltpu.roll(value, 1, 0))


def mat_vec(load, vectors, sums, dagger=False):
    for a in range(3):
        for b in range(3):
            w_re, w_im = load(b, a) if dagger else load(a, b)
            for vec, acc in zip(vectors, sums):
                v_re, v_im = vec[2 * b], vec[2 * b + 1]
                if dagger:
                    acc[2 * a] = acc[2 * a] + w_re * v_re + w_im * v_im
                    acc[2 * a + 1] = acc[2 * a + 1] + w_re * v_im - w_im * v_re
                else:
                    acc[2 * a] = acc[2 * a] + w_re * v_re - w_im * v_im
                    acc[2 * a + 1] = acc[2 * a + 1] + w_re * v_im + w_im * v_re


def zeros(count):
    return [[jnp.zeros((8, 128), jnp.float32) for _ in range(6)] for _ in range(count)]


def link_at(ref, *index):
    return lambda a, b: (ref[index + (a, b, 0)], ref[index + (a, b, 1)])


def tile(ref, index):
    return jnp.concatenate([ref[index + (slice(0, 8),)], ref[index + (slice(8, 16),)]], axis=1)


def by_parity(run, near, far):
    odd = lax.axis_index("space") % 2 == 1

    @pl.when(odd)
    def _():
        run(near, far)

    @pl.when(jnp.logical_not(odd))
    def _():
        run(far, near)


def groups(ref):
    count = ref.shape[1]
    return [range(i, min(i + 2, count)) for i in range(0, count, 2)]


def take(ref, row, pairs):
    return [[ref[row, n, k] for k in range(6)] for n in pairs]


def put(ref, row, pairs, vectors):
    for n, vec in zip(pairs, vectors):
        for k in range(6):
            ref[row, n, k] = vec[k]


def pack_links(links, inner, edge, arrive):
    low = low_half()
    z = lane_ids() % LS
    even = sublane_ids() % 2 == 0
    entries = [(a, b, part) for a in range(3) for b in range(3) for part in range(2)]
    rows = tuple(enumerate((first_of, second_of)))

    arrive(1)
    for a, b, part in entries:
        y_link = tile(links, (1, a, b, part)) * (-1.0 / 6.0)
        u_y = first_of(y_link, y_link, low)
        inner[0, 3, a, b, part] = u_y
        inner[1, 3, b, a, part] = u_y if part == 0 else -u_y
        edge[a, b, part] = second_of(y_link, y_link, low)
    arrive(2)
    for a, b, part in entries:
        z_link = tile(links, (2, a, b, part)) * (-1.0 / 6.0)
        for row, pick in rows:
            u_z = pick(z_link, z_link, low)
            inner[row, 1, a, b, part] = u_z
            u_z = z_prev(u_z, z)
            inner[row, 2, b, a, part] = u_z if part == 0 else -u_z
    arrive(0)
    for part in range(2):
        x_link = [
            [tile(links, (0, a, b, part)) * (-1.0 / 6.0) for b in range(3)] for a in range(3)
        ]
        for a in range(3):
            for b in range(3):
                other = x_other(x_link[b][a], even)
                both = x_link[a][b] + (other if part == 0 else -other)
                for row, pick in rows:
                    inner[row, 0, a, b, part] = pick(both, both, low)


def add_inner(inner, row, pairs, field, sums):
    z = lane_ids() % LS
    even = sublane_ids() % 2 == 0
    here = take(field, row, pairs)
    mat_vec(link_at(inner, row, 0), [[x_other(c, even) for c in vec] for vec in here], sums)
    mat_vec(link_at(inner, row, 1), [[z_next(c, z) for c in vec] for vec in here], sums)
    mat_vec(link_at(inner, row, 2), [[z_prev(c, z) for c in vec] for vec in here], sums)
    mat_vec(link_at(inner, row, 3), take(field, 1 - row, pairs), sums)


def scaled_rows(coeff, start, row, pairs):
    return [[coeff * c for c in vec] for vec in take(start, row, pairs)]


def open_round(coeff, pairs, rows, start, inner, edge, sums_out, down, up):
    for row in range(2):
        sums = scaled_rows(coeff, start, row, pairs)
        add_inner(inner, row, pairs, rows, sums)
        put(sums_out, row, pairs, sums)
        if row == 0:
            put(down, 0, pairs, take(rows, 0, pairs))
            put(down, 1, pairs, sums)
        else:
            for i, vectors in enumerate((take(rows, 1, pairs), sums)):
                back = zeros(len(pairs))
                mat_vec(link_at(edge), vectors, back, dagger=True)
                put(up, i, pairs, back)


def close_round(coeff, pairs, below, above, rows, sums_in, start, inner, edge, middle):
    lower = [
        [s + u for s, u in zip(*both)]
        for both in zip(take(sums_in, 0, pairs), take(below, 0, pairs))
    ]
    put(middle, 0, pairs, lower)
    upper = take(sums_in, 1, pairs)
    mat_vec(link_at(edge), take(above, 0, pairs), upper)
    put(middle, 1, pairs, upper)
    result = []
    for row in range(2):
        sums = [
            [c + (1.0 / 36.0) * r for c, r in zip(*both)]
            for both in zip(scaled_rows(coeff, start, row, pairs), take(rows, row, pairs))
        ]
        add_inner(inner, row, pairs, middle, sums)
        if row == 0:
            sums = [
                [s + u for s, u in zip(*both)] for both in zip(sums, take(below, 1, pairs))
            ]
        else:
            mat_vec(link_at(edge), take(above, 1, pairs), sums)
        result.append(sums)
    return result


def pack_rows(source, rows):
    low = low_half()
    for n in range(rows.shape[1]):
        for k in range(6):
            p, q = source(2 * n, k), source(2 * n + 1, k)
            rows[0, n, k] = first_of(p, q, low)
            rows[1, n, k] = second_of(p, q, low)


def start_chunk(coeff, rows, inner, edge, sums, far_out, near_out):
    def run(down, up):
        for pairs in groups(rows):
            open_round(coeff, pairs, rows, rows, inner, edge, sums, down, up)

    by_parity(run, near_out, far_out)


def first_kernel(
    coeff, src, links, inner, edge, rows, sums, far_out, near_out, later, now, held, sems
):
    count = now.shape[0]
    link_copies = [
        pltpu.make_async_copy(links.at[mu], held.at[mu], sems.at[mu]) for mu in range(3)
    ]
    first_copy = pltpu.make_async_copy(src.at[pl.ds(0, count)], now, sems.at[3])
    rest = src.at[pl.ds(count, later.shape[0])]
    later_copy = pltpu.make_async_copy(rest, later, sems.at[4])
    link_copies[1].start()
    first_copy.start()
    link_copies[2].start()
    link_copies[0].start()
    later_copy.start()
    pack_links(held, inner, edge, lambda mu: link_copies[mu].wait())
    first_copy.wait()
    pack_rows(lambda n, k: tile(now, (n, k)), rows)
    start_chunk(coeff, rows, inner, edge, sums, far_out, near_out)
    later_copy.wait()


def start_kernel(coeff, first, later, inner, edge, rows, sums, far_out, near_out):
    pack_rows(lambda n, k: tile(later, (first + n, k)), rows)
    start_chunk(coeff, rows, inner, edge, sums, far_out, near_out)


def round_kernel(
    coeff,
    next_coeff,
    far_in,
    near_in,
    rows,
    sums_in,
    start,
    inner,
    edge,
    rows_out,
    sums_out,
    far_out,
    near_out,
    middle,
):
    def run(lower_side, upper_side):
        below, down = lower_side
        above, up = upper_side
        for pairs in groups(rows):
            result = close_round(
                coeff, pairs, below, above, rows, sums_in, start, inner, edge, middle
            )
            for row in range(2):
                put(rows_out, row, pairs, result[row])
            open_round(next_coeff, pairs, rows_out, start, inner, edge, sums_out, down, up)

    by_parity(run, (near_in, near_out), (far_in, far_out))


def last_kernel(coeff, first, lead, far_in, near_in, rows, sums_in, start, inner, edge, *rest):
    out, middle, filled, sems = rest[-4:]
    low = low_half()

    def store(n):
        here = pl.ds(2 * n, 2)
        there = pl.ds(first + 2 * n, 2)
        return pltpu.make_async_copy(filled.at[here], out.at[there], sems.at[n])

    def run(below, above):
        for pairs in groups(rows):
            lower, upper = close_round(
                coeff, pairs, below, above, rows, sums_in, start, inner, edge, middle
            )
            for n, bottom, top in zip(pairs, lower, upper):
                for k in range(6):
                    p = first_of(bottom[k], top[k], low) * lead
                    q = second_of(bottom[k], top[k], low) * lead
                    for m, value in ((2 * n, p), (2 * n + 1, q)):
                        filled[m, k, 0:8] = value[:, : 2 * LS]
                        filled[m, k, 8:16] = value[:, 2 * LS :]
                store(n).start()

    by_parity(run, near_in, far_in)
    for n in range(rows.shape[1]):
        store(n).wait()


VMEM_LIMIT = 32 * 1024 * 1024
CHUNKS = 3


def call(kernel, outs, args, flops, scratch=(), in_hbm=(), out_hbm=False, aliases={}):
    moved = sum(4 * a.size for a in args) + sum(4 * o.size for o in outs)
    args = [
        pltpu.with_memory_space_constraint(a, pltpu.HBM) if i in in_hbm else a
        for i, a in enumerate(args)
    ]
    vmem = pl.BlockSpec(memory_space=pltpu.VMEM)
    hbm = pl.BlockSpec(memory_space=pltpu.HBM)
    return pl.pallas_call(
        kernel,
        out_shape=outs,
        in_specs=[hbm if i in in_hbm else vmem for i in range(len(args))],
        out_specs=[hbm if out_hbm else vmem] * len(outs),
        scratch_shapes=list(scratch),
        input_output_aliases=aliases,
        compiler_params=pltpu.CompilerParams(vmem_limit_bytes=VMEM_LIMIT),
        cost_estimate=pl.CostEstimate(flops=flops, bytes_accessed=moved, transcendentals=0),
    )(*args)


def halo_body(links, sources):
    vectors = sources.shape[0]
    share = vectors // CHUNKS
    pairs = share // 2
    sites, planes = links.shape[4:]
    f32 = functools.partial(jax.ShapeDtypeStruct, dtype=jnp.float32)
    both = f32((2, pairs, 6, 8, 128))
    middle = pltpu.VMEM(both.shape, jnp.float32)
    source_view = jnp.swapaxes(sources, 3, 4).reshape(vectors, 6, planes, sites)
    link_view = jnp.swapaxes(links, 4, 5)
    chunk_shape = (share, 6, planes, sites)
    powers = power_coeffs()
    lead = powers[4]
    steps = [powers[power] / lead for power in (3, 2, 1, 0)]
    work = 2 * pairs * 36 * 2 * 1024
    count = lax.axis_size("space")
    near_pairs = [(d, d ^ 1) for d in range(count)]
    far_pairs = [(d, (d + 1 if d % 2 else d - 1) % count) for d in range(count)]

    def exchange(far_out, near_out):
        far = lax.ppermute(far_out, "space", far_pairs)
        return far, lax.ppermute(near_out, "space", near_pairs)

    inner, edge, rows, sums, *sends, later = call(
        functools.partial(first_kernel, steps[0]),
        [
            f32((2, 4, 3, 3, 2, 8, 128)),
            f32((3, 3, 2, 8, 128)),
            *[both] * 4,
            f32((vectors - share, 6, planes, sites)),
        ],
        [source_view, link_view],
        6 * work,
        [
            pltpu.VMEM(chunk_shape, jnp.float32),
            pltpu.VMEM(link_view.shape, jnp.float32),
            pltpu.SemaphoreType.DMA((5,)),
        ],
        (0, 1),
    )
    start, fields, halos = [rows], [(rows, sums)], [exchange(*sends)]
    for chunk in range(1, CHUNKS):
        rows, sums, *sends = call(
            functools.partial(start_kernel, steps[0], (chunk - 1) * share),
            [both] * 4,
            [later, inner, edge],
            6 * work,
        )
        start.append(rows)
        fields.append((rows, sums))
        halos.append(exchange(*sends))
    for chunk in range(CHUNKS):
        rows, sums, *sends = call(
            functools.partial(round_kernel, steps[1], steps[2]),
            [both] * 4,
            [*halos[chunk], *fields[chunk], start[chunk], inner, edge],
            12 * work,
            [middle],
        )
        fields[chunk] = (rows, sums)
        halos[chunk] = exchange(*sends)
    out = None
    for chunk in range(CHUNKS):
        args = [*halos[chunk], *fields[chunk], start[chunk], inner, edge]
        (out,) = call(
            functools.partial(last_kernel, steps[3], chunk * share, lead),
            [f32(source_view.shape)],
            args if out is None else args + [out],
            6 * work,
            [middle, pltpu.VMEM(chunk_shape, jnp.float32), pltpu.SemaphoreType.DMA((pairs,))],
            () if out is None else (len(args),),
            True,
            {} if out is None else {len(args): 0},
        )
    return jnp.swapaxes(out.reshape(vectors, 3, 2, planes, sites), 3, 4)


def shifted(value, axis, steps):
    count = lax.axis_size(axis)
    pairs = [(source, (source + steps) % count) for source in range(count)]
    return lax.ppermute(value, axis, pairs)


def apply_link(link, vector):
    real_part = 0.0
    imag_part = 0.0
    for column in range(3):
        link_re = link[:, column, 0][None]
        link_im = link[:, column, 1][None]
        vec_re = vector[:, column, 0][:, None]
        vec_im = vector[:, column, 1][:, None]
        real_part = real_part + link_re * vec_re - link_im * vec_im
        imag_part = imag_part + link_re * vec_im + link_im * vec_re
    return jnp.stack([real_part, imag_part], axis=2)


def apply_dagger(link, vector):
    real_part = 0.0
    imag_part = 0.0
    for column in range(3):
        link_re = link[column, :, 0][None]
        link_im = link[column, :, 1][None]
        vec_re = vector[:, column, 0][:, None]
        vec_im = vector[:, column, 1][:, None]
        real_part = real_part + link_re * vec_re + link_im * vec_im
        imag_part = imag_part + link_re * vec_im - link_im * vec_re
    return jnp.stack([real_part, imag_part], axis=2)


def z_ahead(array, extent, z_index):
    return jnp.where(
        z_index == extent - 1, jnp.roll(array, extent - 1, axis=-1), jnp.roll(array, -1, axis=-1)
    )


def z_behind(array, extent, z_index):
    return jnp.where(
        z_index == 0, jnp.roll(array, 1 - extent, axis=-1), jnp.roll(array, 1, axis=-1)
    )


def plane_body(links, sources):
    device_count = lax.axis_size("space")
    slabs = device_count // NT
    yz_local = links.shape[4]
    planes = links.shape[5] // device_count
    plane_sites = yz_local * device_count
    vectors = sources.shape[0]
    link_parts = links.reshape(54, yz_local, NT, slabs, planes)
    source_parts = sources.reshape(vectors * 6, yz_local, NT, slabs, planes)
    link_send = jnp.transpose(link_parts, (0, 3, 2, 4, 1)).reshape(
        54, device_count, planes, yz_local
    )
    source_send = jnp.transpose(source_parts, (0, 3, 2, 4, 1)).reshape(
        vectors * 6, device_count, planes, yz_local
    )
    link_recv, source_recv = (
        lax.all_to_all(link_send, "space", split_axis=1, concat_axis=3, tiled=True),
        lax.all_to_all(source_send, "space", split_axis=1, concat_axis=3, tiled=True),
    )
    gauge_local = link_recv.reshape(3, 3, 3, 2, planes, plane_sites)
    source_field = source_recv.reshape(vectors, 3, 2, planes, plane_sites)
    z_index = jnp.arange(plane_sites, dtype=jnp.int32) % LS
    x_top = gauge_local[0]
    x_rest = gauge_local[0][:, :, :, :-1]
    y_back = jnp.roll(gauge_local[1], LS, axis=-1)
    z_back = z_behind(gauge_local[2], LS, z_index)

    def fetch_lower(vector):
        return shifted(apply_dagger(x_top, vector), "space", NT)

    def hop_sum(vector):
        upper_face = shifted(vector, "space", -NT)
        lower_face = fetch_lower(vector)
        ahead = apply_link(
            gauge_local[0], jnp.concatenate([vector[:, :, :, 1:], upper_face], axis=3)
        )
        behind = jnp.concatenate([lower_face, apply_dagger(x_rest, vector[:, :, :, :-1])], axis=3)
        summed = ahead + behind
        summed = (
            summed
            + apply_link(gauge_local[1], jnp.roll(vector, -LS, axis=-1))
            + apply_dagger(y_back, jnp.roll(vector, LS, axis=-1))
        )
        summed = (
            summed
            + apply_link(gauge_local[2], z_ahead(vector, LS, z_index))
            + apply_dagger(z_back, z_behind(vector, LS, z_index))
        )
        return summed

    def scaled(vector):
        return hop_sum(vector) * (-1.0 / 6.0)

    previous = source_field
    current = scaled(previous)
    filtered = cheb_coeffs[0] * previous + cheb_coeffs[1] * current
    for degree in range(2, 5):
        following = 2.0 * scaled(current) - previous
        filtered = filtered + cheb_coeffs[degree] * following
        previous, current = (current, following)
    outgoing = filtered.reshape(vectors * 6, 1, planes, plane_sites)
    returned = lax.all_to_all(outgoing, "space", split_axis=3, concat_axis=1, tiled=True)
    ordered = jnp.transpose(
        returned.reshape(vectors * 6, slabs, NT, planes, yz_local), (0, 4, 2, 1, 3)
    )
    return ordered.reshape(vectors, 3, 2, yz_local, NT * slabs * planes)


def body(links, sources):
    sites, planes = sources.shape[3:]
    if sites == 2 * LS and planes == 2 * NT and sources.shape[0] % (2 * CHUNKS) == 0:
        return halo_body(links, sources)
    return plane_body(links, sources)


def solution(mesh):
    in_specs = (
        P(None, None, None, None, "space", "groups"),
        P(None, None, None, "space", "groups"),
    )
    out_specs = P(None, None, None, "space", "groups")
    return jax.shard_map(body, mesh=mesh, in_specs=in_specs, out_specs=out_specs, check_vma=False)
```

```python
import functools

import jax
import jax.numpy as jnp
from jax import lax
from jax.experimental import pallas as pl
from jax.experimental.pallas import tpu as pltpu
from jax.sharding import PartitionSpec as P

NT = 8
LS = 32

cheb_coeffs = (0.6, -0.5, 0.35, -0.25, 0.15)


def power_coeffs():
    c0, c1, c2, c3, c4 = cheb_coeffs
    return (c0 - c2 + c4, c1 - 3.0 * c3, 2.0 * c2 - 8.0 * c4, 4.0 * c3, 8.0 * c4)


def lane_ids():
    return lax.broadcasted_iota(jnp.int32, (8, 128), 1)


def sublane_ids():
    return lax.broadcasted_iota(jnp.int32, (8, 128), 0)


def low_half():
    return (lane_ids() // LS) % 2 == 0


def first_of(p, q, low):
    return jnp.where(low, p, pltpu.roll(q, LS, 1))


def second_of(p, q, low):
    return jnp.where(low, pltpu.roll(p, 128 - LS, 1), q)


def z_next(value, z):
    return jnp.where(z == LS - 1, pltpu.roll(value, LS - 1, 1), pltpu.roll(value, 127, 1))


def z_prev(value, z):
    return jnp.where(z == 0, pltpu.roll(value, 129 - LS, 1), pltpu.roll(value, 1, 1))


def x_other(value, even):
    return jnp.where(even, pltpu.roll(value, 7, 0), pltpu.roll(value, 1, 0))


def mat_vec(load, vectors, sums, dagger=False):
    for a in range(3):
        for b in range(3):
            w_re, w_im = load(b, a) if dagger else load(a, b)
            for vec, acc in zip(vectors, sums):
                v_re, v_im = vec[2 * b], vec[2 * b + 1]
                if dagger:
                    acc[2 * a] = acc[2 * a] + w_re * v_re + w_im * v_im
                    acc[2 * a + 1] = acc[2 * a + 1] + w_re * v_im - w_im * v_re
                else:
                    acc[2 * a] = acc[2 * a] + w_re * v_re - w_im * v_im
                    acc[2 * a + 1] = acc[2 * a + 1] + w_re * v_im + w_im * v_re


def zeros(count):
    return [[jnp.zeros((8, 128), jnp.float32) for _ in range(6)] for _ in range(count)]


def link_at(ref, *index):
    return lambda a, b: (ref[index + (a, b, 0)], ref[index + (a, b, 1)])


def tile(ref, index):
    return jnp.concatenate([ref[index + (slice(0, 8),)], ref[index + (slice(8, 16),)]], axis=1)


def by_parity(run, near, far):
    odd = lax.axis_index("space") % 2 == 1

    @pl.when(odd)
    def _():
        run(near, far)

    @pl.when(jnp.logical_not(odd))
    def _():
        run(far, near)


def groups(ref):
    count = ref.shape[1]
    return [range(i, min(i + 2, count)) for i in range(0, count, 2)]


def take(ref, row, pairs):
    return [[ref[row, n, k] for k in range(6)] for n in pairs]


def put(ref, row, pairs, vectors):
    for n, vec in zip(pairs, vectors):
        for k in range(6):
            ref[row, n, k] = vec[k]


def pack_links(links, inner, edge, arrive):
    low = low_half()
    z = lane_ids() % LS
    even = sublane_ids() % 2 == 0
    entries = [(a, b, part) for a in range(3) for b in range(3) for part in range(2)]
    rows = tuple(enumerate((first_of, second_of)))

    arrive(1)
    for a, b, part in entries:
        y_link = tile(links, (1, a, b, part)) * (-1.0 / 6.0)
        u_y = first_of(y_link, y_link, low)
        inner[0, 3, a, b, part] = u_y
        inner[1, 3, b, a, part] = u_y if part == 0 else -u_y
        edge[a, b, part] = second_of(y_link, y_link, low)
    arrive(2)
    for a, b, part in entries:
        z_link = tile(links, (2, a, b, part)) * (-1.0 / 6.0)
        for row, pick in rows:
            u_z = pick(z_link, z_link, low)
            inner[row, 1, a, b, part] = u_z
            u_z = z_prev(u_z, z)
            inner[row, 2, b, a, part] = u_z if part == 0 else -u_z
    arrive(0)
    for part in range(2):
        x_link = [
            [tile(links, (0, a, b, part)) * (-1.0 / 6.0) for b in range(3)] for a in range(3)
        ]
        for a in range(3):
            for b in range(3):
                other = x_other(x_link[b][a], even)
                both = x_link[a][b] + (other if part == 0 else -other)
                for row, pick in rows:
                    inner[row, 0, a, b, part] = pick(both, both, low)


def add_inner(inner, row, pairs, field, sums):
    z = lane_ids() % LS
    even = sublane_ids() % 2 == 0
    here = take(field, row, pairs)
    mat_vec(link_at(inner, row, 0), [[x_other(c, even) for c in vec] for vec in here], sums)
    mat_vec(link_at(inner, row, 1), [[z_next(c, z) for c in vec] for vec in here], sums)
    mat_vec(link_at(inner, row, 2), [[z_prev(c, z) for c in vec] for vec in here], sums)
    mat_vec(link_at(inner, row, 3), take(field, 1 - row, pairs), sums)


def scaled_rows(coeff, start, row, pairs):
    return [[coeff * c for c in vec] for vec in take(start, row, pairs)]


def open_round(coeff, pairs, rows, start, inner, edge, sums_out, down, up):
    for row in range(2):
        sums = scaled_rows(coeff, start, row, pairs)
        add_inner(inner, row, pairs, rows, sums)
        put(sums_out, row, pairs, sums)
        if row == 0:
            put(down, 0, pairs, take(rows, 0, pairs))
            put(down, 1, pairs, sums)
        else:
            for i, vectors in enumerate((take(rows, 1, pairs), sums)):
                back = zeros(len(pairs))
                mat_vec(link_at(edge), vectors, back, dagger=True)
                put(up, i, pairs, back)


def close_round(coeff, pairs, below, above, rows, sums_in, start, inner, edge, middle):
    lower = [
        [s + u for s, u in zip(*both)]
        for both in zip(take(sums_in, 0, pairs), take(below, 0, pairs))
    ]
    put(middle, 0, pairs, lower)
    upper = take(sums_in, 1, pairs)
    mat_vec(link_at(edge), take(above, 0, pairs), upper)
    put(middle, 1, pairs, upper)
    result = []
    for row in range(2):
        sums = [
            [c + (1.0 / 36.0) * r for c, r in zip(*both)]
            for both in zip(scaled_rows(coeff, start, row, pairs), take(rows, row, pairs))
        ]
        add_inner(inner, row, pairs, middle, sums)
        if row == 0:
            sums = [
                [s + u for s, u in zip(*both)] for both in zip(sums, take(below, 1, pairs))
            ]
        else:
            mat_vec(link_at(edge), take(above, 1, pairs), sums)
        result.append(sums)
    return result


def pack_rows(source, rows):
    low = low_half()
    for n in range(rows.shape[1]):
        for k in range(6):
            p, q = source(2 * n, k), source(2 * n + 1, k)
            rows[0, n, k] = first_of(p, q, low)
            rows[1, n, k] = second_of(p, q, low)


def start_chunk(coeff, rows, inner, edge, sums, far_out, near_out):
    def run(down, up):
        for pairs in groups(rows):
            open_round(coeff, pairs, rows, rows, inner, edge, sums, down, up)

    by_parity(run, near_out, far_out)


def first_kernel(
    coeff, src, links, inner, edge, rows, sums, far_out, near_out, later, now, held, sems
):
    count = now.shape[0]
    link_copies = [
        pltpu.make_async_copy(links.at[mu], held.at[mu], sems.at[mu]) for mu in range(3)
    ]
    first_copy = pltpu.make_async_copy(src.at[pl.ds(0, count)], now, sems.at[3])
    rest = src.at[pl.ds(count, later.shape[0])]
    later_copy = pltpu.make_async_copy(rest, later, sems.at[4])
    link_copies[1].start()
    first_copy.start()
    link_copies[2].start()
    link_copies[0].start()
    later_copy.start()
    pack_links(held, inner, edge, lambda mu: link_copies[mu].wait())
    first_copy.wait()
    pack_rows(lambda n, k: tile(now, (n, k)), rows)
    start_chunk(coeff, rows, inner, edge, sums, far_out, near_out)
    later_copy.wait()


def start_kernel(coeff, first, later, inner, edge, *refs):
    before, (rows, sums, far_out, near_out) = refs[:-4], refs[-4:]
    pack_rows(lambda n, k: tile(later, (first + n, k)), rows)
    held = 0
    for ref in before:
        held = ref.shape[1]
        for row in range(2):
            for n in range(held):
                put(near_out, row, [n], take(ref, row, [n]))
    own = near_out.at[:, pl.ds(held, rows.shape[1])]
    start_chunk(coeff, rows, inner, edge, sums, far_out, own)


def round_kernel(
    coeff,
    next_coeff,
    place,
    far_in,
    near_in,
    rows,
    sums_in,
    start,
    inner,
    edge,
    rows_out,
    sums_out,
    far_out,
    near_out,
    middle,
):
    near_in = near_in.at[:, pl.ds(place, rows.shape[1])]

    def run(lower_side, upper_side):
        below, down = lower_side
        above, up = upper_side
        for pairs in groups(rows):
            result = close_round(
                coeff, pairs, below, above, rows, sums_in, start, inner, edge, middle
            )
            for row in range(2):
                put(rows_out, row, pairs, result[row])
            open_round(next_coeff, pairs, rows_out, start, inner, edge, sums_out, down, up)

    by_parity(run, (near_in, near_out), (far_in, far_out))


def last_kernel(coeff, first, lead, far_in, near_in, rows, sums_in, start, inner, edge, *rest):
    out, middle, filled, sems = rest[-4:]
    low = low_half()

    def store(n):
        here = pl.ds(2 * n, 2)
        there = pl.ds(first + 2 * n, 2)
        return pltpu.make_async_copy(filled.at[here], out.at[there], sems.at[n])

    def run(below, above):
        for pairs in groups(rows):
            lower, upper = close_round(
                coeff, pairs, below, above, rows, sums_in, start, inner, edge, middle
            )
            for n, bottom, top in zip(pairs, lower, upper):
                for k in range(6):
                    p = first_of(bottom[k], top[k], low) * lead
                    q = second_of(bottom[k], top[k], low) * lead
                    for m, value in ((2 * n, p), (2 * n + 1, q)):
                        filled[m, k, 0:8] = value[:, : 2 * LS]
                        filled[m, k, 8:16] = value[:, 2 * LS :]
                store(n).start()

    by_parity(run, near_in, far_in)
    for n in range(rows.shape[1]):
        store(n).wait()


VMEM_LIMIT = 32 * 1024 * 1024


def call(
    kernel, outs, args, flops, scratch=(), in_hbm=(), out_hbm=False, aliases={}, unread=()
):
    moved = sum(4 * a.size for a in args) + sum(4 * o.size for o in outs)
    args = [
        pltpu.with_memory_space_constraint(a, pltpu.HBM) if i in in_hbm else a
        for i, a in enumerate(args)
    ]
    vmem = pl.BlockSpec(memory_space=pltpu.VMEM)
    hbm = pl.BlockSpec(memory_space=pltpu.HBM)
    anywhere = pl.BlockSpec(memory_space=pl.ANY)
    return pl.pallas_call(
        kernel,
        out_shape=outs,
        in_specs=[
            hbm if i in in_hbm else anywhere if i in unread else vmem for i in range(len(args))
        ],
        out_specs=[hbm if out_hbm else vmem] * len(outs),
        scratch_shapes=list(scratch),
        input_output_aliases=aliases,
        compiler_params=pltpu.CompilerParams(vmem_limit_bytes=VMEM_LIMIT),
        cost_estimate=pl.CostEstimate(flops=flops, bytes_accessed=moved, transcendentals=0),
    )(*args)


def chunk_sizes(pairs):
    return tuple(pairs * part // 12 for part in (6, 4, 2))


def halo_body(links, sources):
    vectors = sources.shape[0]
    sizes = chunk_sizes(vectors // 2)
    chunks = range(len(sizes))
    first = [2 * sum(sizes[:chunk]) for chunk in chunks]
    sites, planes = links.shape[4:]
    f32 = functools.partial(jax.ShapeDtypeStruct, dtype=jnp.float32)
    both = [f32((2, pairs, 6, 8, 128)) for pairs in sizes]
    middle = [pltpu.VMEM(shape.shape, jnp.float32) for shape in both]
    raw = [(2 * pairs, 6, planes, sites) for pairs in sizes]
    source_view = jnp.swapaxes(sources, 3, 4).reshape(vectors, 6, planes, sites)
    link_view = jnp.swapaxes(links, 4, 5)
    powers = power_coeffs()
    lead = powers[4]
    steps = [powers[power] / lead for power in (3, 2, 1, 0)]
    work = [2 * pairs * 36 * 2 * 1024 for pairs in sizes]
    count = lax.axis_size("space")
    near_pairs = [(d, d ^ 1) for d in range(count)]
    far_pairs = [(d, (d + 1 if d % 2 else d - 1) % count) for d in range(count)]

    def exchange(far_out, near_out):
        far = lax.ppermute(far_out, "space", far_pairs)
        return far, lax.ppermute(near_out, "space", near_pairs)

    inner, edge, rows, sums, *sends, later = call(
        functools.partial(first_kernel, steps[0]),
        [
            f32((2, 4, 3, 3, 2, 8, 128)),
            f32((3, 3, 2, 8, 128)),
            *[both[0]] * 4,
            f32((vectors - first[1], 6, planes, sites)),
        ],
        [source_view, link_view],
        6 * work[0],
        [
            pltpu.VMEM(raw[0], jnp.float32),
            pltpu.VMEM(link_view.shape, jnp.float32),
            pltpu.SemaphoreType.DMA((5,)),
        ],
        (0, 1),
    )
    start, fields, halos = [rows], [(rows, sums)], [exchange(*sends)]
    fars, before, places = [], [], [0, 0]
    for chunk in chunks[1:]:
        near_shape = f32((2, places[-1] + sizes[chunk], *both[chunk].shape[2:]))
        rows, sums, far_out, near_out = call(
            functools.partial(start_kernel, steps[0], first[chunk] - first[1]),
            [both[chunk]] * 3 + [near_shape],
            [later, inner, edge, *before],
            6 * work[chunk],
        )
        start.append(rows)
        fields.append((rows, sums))
        fars.append(lax.ppermute(far_out, "space", far_pairs))
        before = [near_out]
        places.append(places[-1] + sizes[chunk])
    near = lax.ppermute(near_out, "space", near_pairs)
    halos += [(far, near) for far in fars]
    for chunk in chunks:
        rows, sums, *sends = call(
            functools.partial(round_kernel, steps[1], steps[2], places[chunk]),
            [both[chunk]] * 4,
            [*halos[chunk], *fields[chunk], start[chunk], inner, edge],
            12 * work[chunk],
            [middle[chunk]],
        )
        fields[chunk] = (rows, sums)
        halos[chunk] = exchange(*sends)
    out = None
    for chunk in chunks:
        args = [*halos[chunk], *fields[chunk], start[chunk], inner, edge]
        (out,) = call(
            functools.partial(last_kernel, steps[3], first[chunk], lead),
            [f32(source_view.shape)],
            args if out is None else args + [out],
            6 * work[chunk],
            [
                middle[chunk],
                pltpu.VMEM(raw[chunk], jnp.float32),
                pltpu.SemaphoreType.DMA((sizes[chunk],)),
            ],
            () if out is None else (len(args),),
            True,
            {} if out is None else {len(args): 0},
        )
    return jnp.swapaxes(out.reshape(vectors, 3, 2, planes, sites), 3, 4)


def shifted(value, axis, steps):
    count = lax.axis_size(axis)
    pairs = [(source, (source + steps) % count) for source in range(count)]
    return lax.ppermute(value, axis, pairs)


def apply_link(link, vector):
    real_part = 0.0
    imag_part = 0.0
    for column in range(3):
        link_re = link[:, column, 0][None]
        link_im = link[:, column, 1][None]
        vec_re = vector[:, column, 0][:, None]
        vec_im = vector[:, column, 1][:, None]
        real_part = real_part + link_re * vec_re - link_im * vec_im
        imag_part = imag_part + link_re * vec_im + link_im * vec_re
    return jnp.stack([real_part, imag_part], axis=2)


def apply_dagger(link, vector):
    real_part = 0.0
    imag_part = 0.0
    for column in range(3):
        link_re = link[column, :, 0][None]
        link_im = link[column, :, 1][None]
        vec_re = vector[:, column, 0][:, None]
        vec_im = vector[:, column, 1][:, None]
        real_part = real_part + link_re * vec_re + link_im * vec_im
        imag_part = imag_part + link_re * vec_im - link_im * vec_re
    return jnp.stack([real_part, imag_part], axis=2)


def z_ahead(array, extent, z_index):
    return jnp.where(
        z_index == extent - 1, jnp.roll(array, extent - 1, axis=-1), jnp.roll(array, -1, axis=-1)
    )


def z_behind(array, extent, z_index):
    return jnp.where(
        z_index == 0, jnp.roll(array, 1 - extent, axis=-1), jnp.roll(array, 1, axis=-1)
    )


def plane_body(links, sources):
    device_count = lax.axis_size("space")
    slabs = device_count // NT
    yz_local = links.shape[4]
    planes = links.shape[5] // device_count
    plane_sites = yz_local * device_count
    vectors = sources.shape[0]
    link_parts = links.reshape(54, yz_local, NT, slabs, planes)
    source_parts = sources.reshape(vectors * 6, yz_local, NT, slabs, planes)
    link_send = jnp.transpose(link_parts, (0, 3, 2, 4, 1)).reshape(
        54, device_count, planes, yz_local
    )
    source_send = jnp.transpose(source_parts, (0, 3, 2, 4, 1)).reshape(
        vectors * 6, device_count, planes, yz_local
    )
    link_recv, source_recv = (
        lax.all_to_all(link_send, "space", split_axis=1, concat_axis=3, tiled=True),
        lax.all_to_all(source_send, "space", split_axis=1, concat_axis=3, tiled=True),
    )
    gauge_local = link_recv.reshape(3, 3, 3, 2, planes, plane_sites)
    source_field = source_recv.reshape(vectors, 3, 2, planes, plane_sites)
    z_index = jnp.arange(plane_sites, dtype=jnp.int32) % LS
    x_top = gauge_local[0]
    x_rest = gauge_local[0][:, :, :, :-1]
    y_back = jnp.roll(gauge_local[1], LS, axis=-1)
    z_back = z_behind(gauge_local[2], LS, z_index)

    def fetch_lower(vector):
        return shifted(apply_dagger(x_top, vector), "space", NT)

    def hop_sum(vector):
        upper_face = shifted(vector, "space", -NT)
        lower_face = fetch_lower(vector)
        ahead = apply_link(
            gauge_local[0], jnp.concatenate([vector[:, :, :, 1:], upper_face], axis=3)
        )
        behind = jnp.concatenate([lower_face, apply_dagger(x_rest, vector[:, :, :, :-1])], axis=3)
        summed = ahead + behind
        summed = (
            summed
            + apply_link(gauge_local[1], jnp.roll(vector, -LS, axis=-1))
            + apply_dagger(y_back, jnp.roll(vector, LS, axis=-1))
        )
        summed = (
            summed
            + apply_link(gauge_local[2], z_ahead(vector, LS, z_index))
            + apply_dagger(z_back, z_behind(vector, LS, z_index))
        )
        return summed

    def scaled(vector):
        return hop_sum(vector) * (-1.0 / 6.0)

    previous = source_field
    current = scaled(previous)
    filtered = cheb_coeffs[0] * previous + cheb_coeffs[1] * current
    for degree in range(2, 5):
        following = 2.0 * scaled(current) - previous
        filtered = filtered + cheb_coeffs[degree] * following
        previous, current = (current, following)
    outgoing = filtered.reshape(vectors * 6, 1, planes, plane_sites)
    returned = lax.all_to_all(outgoing, "space", split_axis=3, concat_axis=1, tiled=True)
    ordered = jnp.transpose(
        returned.reshape(vectors * 6, slabs, NT, planes, yz_local), (0, 4, 2, 1, 3)
    )
    return ordered.reshape(vectors, 3, 2, yz_local, NT * slabs * planes)


def body(links, sources):
    sites, planes = sources.shape[3:]
    if sites == 2 * LS and planes == 2 * NT and sources.shape[0] % 8 == 0:
        return halo_body(links, sources)
    return plane_body(links, sources)


def solution(mesh):
    in_specs = (
        P(None, None, None, None, "space", "groups"),
        P(None, None, None, "space", "groups"),
    )
    out_specs = P(None, None, None, "space", "groups")
    return jax.shard_map(body, mesh=mesh, in_specs=in_specs, out_specs=out_specs, check_vma=False)
```

```python
import functools

import jax
import jax.numpy as jnp
from jax import lax
from jax.experimental import pallas as pl
from jax.experimental.pallas import tpu as pltpu
from jax.sharding import PartitionSpec as P

NT = 8
LS = 32

cheb_coeffs = (0.6, -0.5, 0.35, -0.25, 0.15)


def power_coeffs():
    c0, c1, c2, c3, c4 = cheb_coeffs
    return (c0 - c2 + c4, c1 - 3.0 * c3, 2.0 * c2 - 8.0 * c4, 4.0 * c3, 8.0 * c4)


def lane_ids():
    return lax.broadcasted_iota(jnp.int32, (8, 128), 1)


def sublane_ids():
    return lax.broadcasted_iota(jnp.int32, (8, 128), 0)


def low_half():
    return (lane_ids() // LS) % 2 == 0


def first_of(p, q, low):
    return jnp.where(low, p, pltpu.roll(q, LS, 1))


def second_of(p, q, low):
    return jnp.where(low, pltpu.roll(p, 128 - LS, 1), q)


def z_next(value, z):
    return jnp.where(z == LS - 1, pltpu.roll(value, LS - 1, 1), pltpu.roll(value, 127, 1))


def z_prev(value, z):
    return jnp.where(z == 0, pltpu.roll(value, 129 - LS, 1), pltpu.roll(value, 1, 1))


def x_other(value, even):
    return jnp.where(even, pltpu.roll(value, 7, 0), pltpu.roll(value, 1, 0))


def mat_vec(load, vectors, sums, dagger=False):
    for a in range(3):
        for b in range(3):
            w_re, w_im = load(b, a) if dagger else load(a, b)
            for vec, acc in zip(vectors, sums):
                v_re, v_im = vec[2 * b], vec[2 * b + 1]
                if dagger:
                    acc[2 * a] = acc[2 * a] + w_re * v_re + w_im * v_im
                    acc[2 * a + 1] = acc[2 * a + 1] + w_re * v_im - w_im * v_re
                else:
                    acc[2 * a] = acc[2 * a] + w_re * v_re - w_im * v_im
                    acc[2 * a + 1] = acc[2 * a + 1] + w_re * v_im + w_im * v_re


def zeros(count):
    return [[jnp.zeros((8, 128), jnp.float32) for _ in range(6)] for _ in range(count)]


def link_at(ref, *index):
    return lambda a, b: (ref[index + (a, b, 0)], ref[index + (a, b, 1)])


def tile(ref, index):
    return jnp.concatenate([ref[index + (slice(0, 8),)], ref[index + (slice(8, 16),)]], axis=1)


def by_parity(run, near, far):
    odd = lax.axis_index("space") % 2 == 1

    @pl.when(odd)
    def _():
        run(near, far)

    @pl.when(jnp.logical_not(odd))
    def _():
        run(far, near)


def groups(ref):
    count = ref.shape[1]
    return [range(i, min(i + 2, count)) for i in range(0, count, 2)]


def take(ref, row, pairs):
    return [[ref[row, n, k] for k in range(6)] for n in pairs]


def put(ref, row, pairs, vectors):
    for n, vec in zip(pairs, vectors):
        for k in range(6):
            ref[row, n, k] = vec[k]


def pack_links(links, inner, edge, arrive):
    low = low_half()
    z = lane_ids() % LS
    even = sublane_ids() % 2 == 0
    entries = [(a, b, part) for a in range(3) for b in range(3) for part in range(2)]
    rows = tuple(enumerate((first_of, second_of)))

    arrive(1)
    for a, b, part in entries:
        y_link = tile(links, (1, a, b, part)) * (-1.0 / 6.0)
        u_y = first_of(y_link, y_link, low)
        inner[0, 3, a, b, part] = u_y
        inner[1, 3, b, a, part] = u_y if part == 0 else -u_y
        edge[a, b, part] = second_of(y_link, y_link, low)
    arrive(2)
    for a, b, part in entries:
        z_link = tile(links, (2, a, b, part)) * (-1.0 / 6.0)
        for row, pick in rows:
            u_z = pick(z_link, z_link, low)
            inner[row, 1, a, b, part] = u_z
            u_z = z_prev(u_z, z)
            inner[row, 2, b, a, part] = u_z if part == 0 else -u_z
    arrive(0)
    for part in range(2):
        x_link = [
            [tile(links, (0, a, b, part)) * (-1.0 / 6.0) for b in range(3)] for a in range(3)
        ]
        for a in range(3):
            for b in range(3):
                other = x_other(x_link[b][a], even)
                both = x_link[a][b] + (other if part == 0 else -other)
                for row, pick in rows:
                    inner[row, 0, a, b, part] = pick(both, both, low)


def add_inner(inner, row, pairs, field, sums):
    z = lane_ids() % LS
    even = sublane_ids() % 2 == 0
    here = take(field, row, pairs)
    mat_vec(link_at(inner, row, 0), [[x_other(c, even) for c in vec] for vec in here], sums)
    mat_vec(link_at(inner, row, 1), [[z_next(c, z) for c in vec] for vec in here], sums)
    mat_vec(link_at(inner, row, 2), [[z_prev(c, z) for c in vec] for vec in here], sums)
    mat_vec(link_at(inner, row, 3), take(field, 1 - row, pairs), sums)


def scaled_rows(coeff, start, row, pairs):
    return [[coeff * c for c in vec] for vec in take(start, row, pairs)]


def open_round(coeff, pairs, rows, start, inner, edge, sums_out, down, up):
    for row in range(2):
        sums = scaled_rows(coeff, start, row, pairs)
        add_inner(inner, row, pairs, rows, sums)
        put(sums_out, row, pairs, sums)
        if row == 0:
            put(down, 0, pairs, take(rows, 0, pairs))
            put(down, 1, pairs, sums)
        else:
            for i, vectors in enumerate((take(rows, 1, pairs), sums)):
                back = zeros(len(pairs))
                mat_vec(link_at(edge), vectors, back, dagger=True)
                put(up, i, pairs, back)


def close_round(coeff, pairs, below, above, rows, sums_in, start, inner, edge, middle):
    lower = [
        [s + u for s, u in zip(*both)]
        for both in zip(take(sums_in, 0, pairs), take(below, 0, pairs))
    ]
    put(middle, 0, pairs, lower)
    upper = take(sums_in, 1, pairs)
    mat_vec(link_at(edge), take(above, 0, pairs), upper)
    put(middle, 1, pairs, upper)
    result = []
    for row in range(2):
        sums = [
            [c + (1.0 / 36.0) * r for c, r in zip(*both)]
            for both in zip(scaled_rows(coeff, start, row, pairs), take(rows, row, pairs))
        ]
        add_inner(inner, row, pairs, middle, sums)
        if row == 0:
            sums = [
                [s + u for s, u in zip(*both)] for both in zip(sums, take(below, 1, pairs))
            ]
        else:
            mat_vec(link_at(edge), take(above, 1, pairs), sums)
        result.append(sums)
    return result


def pack_rows(source, rows):
    low = low_half()
    for n in range(rows.shape[1]):
        for k in range(6):
            p, q = source(2 * n, k), source(2 * n + 1, k)
            rows[0, n, k] = first_of(p, q, low)
            rows[1, n, k] = second_of(p, q, low)


def start_chunk(coeff, rows, inner, edge, sums, far_out, near_out):
    def run(down, up):
        for pairs in groups(rows):
            open_round(coeff, pairs, rows, rows, inner, edge, sums, down, up)

    by_parity(run, near_out, far_out)


def first_kernel(
    coeff, src, links, inner, edge, rows, sums, far_out, near_out, later, now, held, sems
):
    count = now.shape[0]
    link_copies = [
        pltpu.make_async_copy(links.at[mu], held.at[mu], sems.at[mu]) for mu in range(3)
    ]
    first_copy = pltpu.make_async_copy(src.at[pl.ds(0, count)], now, sems.at[3])
    rest = src.at[pl.ds(count, later.shape[0])]
    later_copy = pltpu.make_async_copy(rest, later, sems.at[4])
    link_copies[1].start()
    first_copy.start()
    link_copies[2].start()
    link_copies[0].start()
    later_copy.start()
    pack_links(held, inner, edge, lambda mu: link_copies[mu].wait())
    first_copy.wait()
    pack_rows(lambda n, k: tile(now, (n, k)), rows)
    start_chunk(coeff, rows, inner, edge, sums, far_out, near_out)
    later_copy.wait()


def start_kernel(coeff, first, later, inner, edge, *refs):
    before, (rows, sums, far_out, near_out) = refs[:-4], refs[-4:]
    pack_rows(lambda n, k: tile(later, (first + n, k)), rows)
    held = 0
    for ref in before:
        held = ref.shape[1]
        for row in range(2):
            for n in range(held):
                put(near_out, row, [n], take(ref, row, [n]))
    own = near_out.at[:, pl.ds(held, rows.shape[1])]
    start_chunk(coeff, rows, inner, edge, sums, far_out, own)


def round_kernel(
    coeff,
    next_coeff,
    place,
    far_in,
    near_in,
    rows,
    sums_in,
    start,
    inner,
    edge,
    rows_out,
    sums_out,
    far_out,
    near_out,
    middle,
):
    near_in = near_in.at[:, pl.ds(place, rows.shape[1])]

    def run(lower_side, upper_side):
        below, down = lower_side
        above, up = upper_side
        for pairs in groups(rows):
            result = close_round(
                coeff, pairs, below, above, rows, sums_in, start, inner, edge, middle
            )
            for row in range(2):
                put(rows_out, row, pairs, result[row])
            open_round(next_coeff, pairs, rows_out, start, inner, edge, sums_out, down, up)

    by_parity(run, (near_in, near_out), (far_in, far_out))


def last_kernel(coeff, first, lead, far_in, near_in, rows, sums_in, start, inner, edge, *rest):
    out, middle, filled, sems = rest[-4:]
    low = low_half()

    def store(n):
        here = pl.ds(2 * n, 2)
        there = pl.ds(first + 2 * n, 2)
        return pltpu.make_async_copy(filled.at[here], out.at[there], sems.at[n])

    def run(below, above):
        for pairs in groups(rows):
            lower, upper = close_round(
                coeff, pairs, below, above, rows, sums_in, start, inner, edge, middle
            )
            for n, bottom, top in zip(pairs, lower, upper):
                for k in range(6):
                    p = first_of(bottom[k], top[k], low) * lead
                    q = second_of(bottom[k], top[k], low) * lead
                    for m, value in ((2 * n, p), (2 * n + 1, q)):
                        filled[m, k, 0:8] = value[:, : 2 * LS]
                        filled[m, k, 8:16] = value[:, 2 * LS :]
                store(n).start()

    by_parity(run, near_in, far_in)
    for n in range(rows.shape[1]):
        store(n).wait()


VMEM_LIMIT = 32 * 1024 * 1024


def call(
    kernel, outs, args, flops, scratch=(), in_hbm=(), out_hbm=False, aliases={}, unread=()
):
    moved = sum(4 * a.size for a in args) + sum(4 * o.size for o in outs)
    args = [
        pltpu.with_memory_space_constraint(a, pltpu.HBM) if i in in_hbm else a
        for i, a in enumerate(args)
    ]
    vmem = pl.BlockSpec(memory_space=pltpu.VMEM)
    hbm = pl.BlockSpec(memory_space=pltpu.HBM)
    anywhere = pl.BlockSpec(memory_space=pl.ANY)
    return pl.pallas_call(
        kernel,
        out_shape=outs,
        in_specs=[
            hbm if i in in_hbm else anywhere if i in unread else vmem for i in range(len(args))
        ],
        out_specs=[hbm if out_hbm else vmem] * len(outs),
        scratch_shapes=list(scratch),
        input_output_aliases=aliases,
        compiler_params=pltpu.CompilerParams(vmem_limit_bytes=VMEM_LIMIT),
        cost_estimate=pl.CostEstimate(flops=flops, bytes_accessed=moved, transcendentals=0),
    )(*args)


def chunk_sizes(pairs):
    return tuple(pairs * part // 12 for part in (7, 5))


def halo_body(links, sources):
    vectors = sources.shape[0]
    sizes = chunk_sizes(vectors // 2)
    chunks = range(len(sizes))
    first = [2 * sum(sizes[:chunk]) for chunk in chunks]
    sites, planes = links.shape[4:]
    f32 = functools.partial(jax.ShapeDtypeStruct, dtype=jnp.float32)
    both = [f32((2, pairs, 6, 8, 128)) for pairs in sizes]
    middle = [pltpu.VMEM(shape.shape, jnp.float32) for shape in both]
    raw = [(2 * pairs, 6, planes, sites) for pairs in sizes]
    source_view = jnp.swapaxes(sources, 3, 4).reshape(vectors, 6, planes, sites)
    link_view = jnp.swapaxes(links, 4, 5)
    powers = power_coeffs()
    lead = powers[4]
    steps = [powers[power] / lead for power in (3, 2, 1, 0)]
    work = [2 * pairs * 36 * 2 * 1024 for pairs in sizes]
    count = lax.axis_size("space")
    near_pairs = [(d, d ^ 1) for d in range(count)]
    far_pairs = [(d, (d + 1 if d % 2 else d - 1) % count) for d in range(count)]

    def exchange(far_out, near_out):
        far = lax.ppermute(far_out, "space", far_pairs)
        return far, lax.ppermute(near_out, "space", near_pairs)

    inner, edge, rows, sums, *sends, later = call(
        functools.partial(first_kernel, steps[0]),
        [
            f32((2, 4, 3, 3, 2, 8, 128)),
            f32((3, 3, 2, 8, 128)),
            *[both[0]] * 4,
            f32((vectors - first[1], 6, planes, sites)),
        ],
        [source_view, link_view],
        6 * work[0],
        [
            pltpu.VMEM(raw[0], jnp.float32),
            pltpu.VMEM(link_view.shape, jnp.float32),
            pltpu.SemaphoreType.DMA((5,)),
        ],
        (0, 1),
    )
    start, fields, halos = [rows], [(rows, sums)], [exchange(*sends)]
    fars, before, places = [], [], [0, 0]
    for chunk in chunks[1:]:
        near_shape = f32((2, places[-1] + sizes[chunk], *both[chunk].shape[2:]))
        rows, sums, far_out, near_out = call(
            functools.partial(start_kernel, steps[0], first[chunk] - first[1]),
            [both[chunk]] * 3 + [near_shape],
            [later, inner, edge, *before],
            6 * work[chunk],
        )
        start.append(rows)
        fields.append((rows, sums))
        fars.append(lax.ppermute(far_out, "space", far_pairs))
        before = [near_out]
        places.append(places[-1] + sizes[chunk])
    near = lax.ppermute(near_out, "space", near_pairs)
    halos += [(far, near) for far in fars]
    for chunk in chunks:
        rows, sums, *sends = call(
            functools.partial(round_kernel, steps[1], steps[2], places[chunk]),
            [both[chunk]] * 4,
            [*halos[chunk], *fields[chunk], start[chunk], inner, edge],
            12 * work[chunk],
            [middle[chunk]],
        )
        fields[chunk] = (rows, sums)
        halos[chunk] = exchange(*sends)
    out = None
    for chunk in chunks:
        args = [*halos[chunk], *fields[chunk], start[chunk], inner, edge]
        (out,) = call(
            functools.partial(last_kernel, steps[3], first[chunk], lead),
            [f32(source_view.shape)],
            args if out is None else args + [out],
            6 * work[chunk],
            [
                middle[chunk],
                pltpu.VMEM(raw[chunk], jnp.float32),
                pltpu.SemaphoreType.DMA((sizes[chunk],)),
            ],
            () if out is None else (len(args),),
            True,
            {} if out is None else {len(args): 0},
        )
    return jnp.swapaxes(out.reshape(vectors, 3, 2, planes, sites), 3, 4)


def shifted(value, axis, steps):
    count = lax.axis_size(axis)
    pairs = [(source, (source + steps) % count) for source in range(count)]
    return lax.ppermute(value, axis, pairs)


def apply_link(link, vector):
    real_part = 0.0
    imag_part = 0.0
    for column in range(3):
        link_re = link[:, column, 0][None]
        link_im = link[:, column, 1][None]
        vec_re = vector[:, column, 0][:, None]
        vec_im = vector[:, column, 1][:, None]
        real_part = real_part + link_re * vec_re - link_im * vec_im
        imag_part = imag_part + link_re * vec_im + link_im * vec_re
    return jnp.stack([real_part, imag_part], axis=2)


def apply_dagger(link, vector):
    real_part = 0.0
    imag_part = 0.0
    for column in range(3):
        link_re = link[column, :, 0][None]
        link_im = link[column, :, 1][None]
        vec_re = vector[:, column, 0][:, None]
        vec_im = vector[:, column, 1][:, None]
        real_part = real_part + link_re * vec_re + link_im * vec_im
        imag_part = imag_part + link_re * vec_im - link_im * vec_re
    return jnp.stack([real_part, imag_part], axis=2)


def z_ahead(array, extent, z_index):
    return jnp.where(
        z_index == extent - 1, jnp.roll(array, extent - 1, axis=-1), jnp.roll(array, -1, axis=-1)
    )


def z_behind(array, extent, z_index):
    return jnp.where(
        z_index == 0, jnp.roll(array, 1 - extent, axis=-1), jnp.roll(array, 1, axis=-1)
    )


def plane_body(links, sources):
    device_count = lax.axis_size("space")
    slabs = device_count // NT
    yz_local = links.shape[4]
    planes = links.shape[5] // device_count
    plane_sites = yz_local * device_count
    vectors = sources.shape[0]
    link_parts = links.reshape(54, yz_local, NT, slabs, planes)
    source_parts = sources.reshape(vectors * 6, yz_local, NT, slabs, planes)
    link_send = jnp.transpose(link_parts, (0, 3, 2, 4, 1)).reshape(
        54, device_count, planes, yz_local
    )
    source_send = jnp.transpose(source_parts, (0, 3, 2, 4, 1)).reshape(
        vectors * 6, device_count, planes, yz_local
    )
    link_recv, source_recv = (
        lax.all_to_all(link_send, "space", split_axis=1, concat_axis=3, tiled=True),
        lax.all_to_all(source_send, "space", split_axis=1, concat_axis=3, tiled=True),
    )
    gauge_local = link_recv.reshape(3, 3, 3, 2, planes, plane_sites)
    source_field = source_recv.reshape(vectors, 3, 2, planes, plane_sites)
    z_index = jnp.arange(plane_sites, dtype=jnp.int32) % LS
    x_top = gauge_local[0]
    x_rest = gauge_local[0][:, :, :, :-1]
    y_back = jnp.roll(gauge_local[1], LS, axis=-1)
    z_back = z_behind(gauge_local[2], LS, z_index)

    def fetch_lower(vector):
        return shifted(apply_dagger(x_top, vector), "space", NT)

    def hop_sum(vector):
        upper_face = shifted(vector, "space", -NT)
        lower_face = fetch_lower(vector)
        ahead = apply_link(
            gauge_local[0], jnp.concatenate([vector[:, :, :, 1:], upper_face], axis=3)
        )
        behind = jnp.concatenate([lower_face, apply_dagger(x_rest, vector[:, :, :, :-1])], axis=3)
        summed = ahead + behind
        summed = (
            summed
            + apply_link(gauge_local[1], jnp.roll(vector, -LS, axis=-1))
            + apply_dagger(y_back, jnp.roll(vector, LS, axis=-1))
        )
        summed = (
            summed
            + apply_link(gauge_local[2], z_ahead(vector, LS, z_index))
            + apply_dagger(z_back, z_behind(vector, LS, z_index))
        )
        return summed

    def scaled(vector):
        return hop_sum(vector) * (-1.0 / 6.0)

    previous = source_field
    current = scaled(previous)
    filtered = cheb_coeffs[0] * previous + cheb_coeffs[1] * current
    for degree in range(2, 5):
        following = 2.0 * scaled(current) - previous
        filtered = filtered + cheb_coeffs[degree] * following
        previous, current = (current, following)
    outgoing = filtered.reshape(vectors * 6, 1, planes, plane_sites)
    returned = lax.all_to_all(outgoing, "space", split_axis=3, concat_axis=1, tiled=True)
    ordered = jnp.transpose(
        returned.reshape(vectors * 6, slabs, NT, planes, yz_local), (0, 4, 2, 1, 3)
    )
    return ordered.reshape(vectors, 3, 2, yz_local, NT * slabs * planes)


def body(links, sources):
    sites, planes = sources.shape[3:]
    if sites == 2 * LS and planes == 2 * NT and sources.shape[0] % 8 == 0:
        return halo_body(links, sources)
    return plane_body(links, sources)


def solution(mesh):
    in_specs = (
        P(None, None, None, None, "space", "groups"),
        P(None, None, None, "space", "groups"),
    )
    out_specs = P(None, None, None, "space", "groups")
    return jax.shard_map(body, mesh=mesh, in_specs=in_specs, out_specs=out_specs, check_vma=False)
```

```python
import functools

import jax
import jax.numpy as jnp
from jax import lax
from jax.experimental import pallas as pl
from jax.experimental.pallas import tpu as pltpu
from jax.sharding import PartitionSpec as P

NT = 8
LS = 32

cheb_coeffs = (0.6, -0.5, 0.35, -0.25, 0.15)


def power_coeffs():
    c0, c1, c2, c3, c4 = cheb_coeffs
    return (c0 - c2 + c4, c1 - 3.0 * c3, 2.0 * c2 - 8.0 * c4, 4.0 * c3, 8.0 * c4)


def lane_ids():
    return lax.broadcasted_iota(jnp.int32, (8, 128), 1)


def sublane_ids():
    return lax.broadcasted_iota(jnp.int32, (8, 128), 0)


def low_half():
    return (lane_ids() // LS) % 2 == 0


def first_of(p, q, low):
    return jnp.where(low, p, pltpu.roll(q, LS, 1))


def second_of(p, q, low):
    return jnp.where(low, pltpu.roll(p, 128 - LS, 1), q)


def z_next(value, z):
    return jnp.where(z == LS - 1, pltpu.roll(value, LS - 1, 1), pltpu.roll(value, 127, 1))


def z_prev(value, z):
    return jnp.where(z == 0, pltpu.roll(value, 129 - LS, 1), pltpu.roll(value, 1, 1))


def x_other(value, even):
    return jnp.where(even, pltpu.roll(value, 7, 0), pltpu.roll(value, 1, 0))


def mat_vec(load, vectors, sums, dagger=False):
    for a in range(3):
        for b in range(3):
            w_re, w_im = load(b, a) if dagger else load(a, b)
            for vec, acc in zip(vectors, sums):
                v_re, v_im = vec[2 * b], vec[2 * b + 1]
                if dagger:
                    acc[2 * a] = acc[2 * a] + w_re * v_re + w_im * v_im
                    acc[2 * a + 1] = acc[2 * a + 1] + w_re * v_im - w_im * v_re
                else:
                    acc[2 * a] = acc[2 * a] + w_re * v_re - w_im * v_im
                    acc[2 * a + 1] = acc[2 * a + 1] + w_re * v_im + w_im * v_re


def zeros(count):
    return [[jnp.zeros((8, 128), jnp.float32) for _ in range(6)] for _ in range(count)]


def link_at(ref, *index):
    return lambda a, b: (ref[index + (a, b, 0)], ref[index + (a, b, 1)])


def tile(ref, index):
    return jnp.concatenate([ref[index + (slice(0, 8),)], ref[index + (slice(8, 16),)]], axis=1)


def by_parity(run, near, far):
    odd = lax.axis_index("space") % 2 == 1

    @pl.when(odd)
    def _():
        run(near, far)

    @pl.when(jnp.logical_not(odd))
    def _():
        run(far, near)


def each_group(ref, body):
    count = ref.shape[1]

    def step(i, carry):
        body([2 * i, 2 * i + 1])
        return carry

    lax.fori_loop(0, count // 2, step, 0)
    if count % 2:
        body([count - 1])


def take(ref, row, pairs):
    return [[ref[row, n, k] for k in range(6)] for n in pairs]


def put(ref, row, pairs, vectors):
    for n, vec in zip(pairs, vectors):
        for k in range(6):
            ref[row, n, k] = vec[k]


def pack_links(links, inner, edge, arrive):
    low = low_half()
    z = lane_ids() % LS
    even = sublane_ids() % 2 == 0
    entries = [(a, b, part) for a in range(3) for b in range(3) for part in range(2)]
    rows = tuple(enumerate((first_of, second_of)))

    arrive(1)
    for a, b, part in entries:
        y_link = tile(links, (1, a, b, part)) * (-1.0 / 6.0)
        u_y = first_of(y_link, y_link, low)
        inner[0, 3, a, b, part] = u_y
        inner[1, 3, b, a, part] = u_y if part == 0 else -u_y
        edge[a, b, part] = second_of(y_link, y_link, low)
    arrive(2)
    for a, b, part in entries:
        z_link = tile(links, (2, a, b, part)) * (-1.0 / 6.0)
        for row, pick in rows:
            u_z = pick(z_link, z_link, low)
            inner[row, 1, a, b, part] = u_z
            u_z = z_prev(u_z, z)
            inner[row, 2, b, a, part] = u_z if part == 0 else -u_z
    arrive(0)
    for part in range(2):
        x_link = [
            [tile(links, (0, a, b, part)) * (-1.0 / 6.0) for b in range(3)] for a in range(3)
        ]
        for a in range(3):
            for b in range(3):
                other = x_other(x_link[b][a], even)
                both = x_link[a][b] + (other if part == 0 else -other)
                for row, pick in rows:
                    inner[row, 0, a, b, part] = pick(both, both, low)


def add_inner(inner, row, pairs, field, sums):
    z = lane_ids() % LS
    even = sublane_ids() % 2 == 0
    here = take(field, row, pairs)
    mat_vec(link_at(inner, row, 0), [[x_other(c, even) for c in vec] for vec in here], sums)
    mat_vec(link_at(inner, row, 1), [[z_next(c, z) for c in vec] for vec in here], sums)
    mat_vec(link_at(inner, row, 2), [[z_prev(c, z) for c in vec] for vec in here], sums)
    mat_vec(link_at(inner, row, 3), take(field, 1 - row, pairs), sums)


def scaled_rows(coeff, start, row, pairs):
    return [[coeff * c for c in vec] for vec in take(start, row, pairs)]


def open_round(coeff, pairs, rows, start, inner, edge, sums_out, down, up):
    for row in range(2):
        sums = scaled_rows(coeff, start, row, pairs)
        add_inner(inner, row, pairs, rows, sums)
        put(sums_out, row, pairs, sums)
        if row == 0:
            put(down, 0, pairs, take(rows, 0, pairs))
            put(down, 1, pairs, sums)
        else:
            for i, vectors in enumerate((take(rows, 1, pairs), sums)):
                back = zeros(len(pairs))
                mat_vec(link_at(edge), vectors, back, dagger=True)
                put(up, i, pairs, back)


def close_round(coeff, pairs, below, above, rows, sums_in, start, inner, edge, middle):
    lower = [
        [s + u for s, u in zip(*both)]
        for both in zip(take(sums_in, 0, pairs), take(below, 0, pairs))
    ]
    put(middle, 0, pairs, lower)
    upper = take(sums_in, 1, pairs)
    mat_vec(link_at(edge), take(above, 0, pairs), upper)
    put(middle, 1, pairs, upper)
    result = []
    for row in range(2):
        sums = [
            [c + (1.0 / 36.0) * r for c, r in zip(*both)]
            for both in zip(scaled_rows(coeff, start, row, pairs), take(rows, row, pairs))
        ]
        add_inner(inner, row, pairs, middle, sums)
        if row == 0:
            sums = [
                [s + u for s, u in zip(*both)] for both in zip(sums, take(below, 1, pairs))
            ]
        else:
            mat_vec(link_at(edge), take(above, 1, pairs), sums)
        result.append(sums)
    return result


def pack_rows(source, rows, arrive=lambda n: None):
    low = low_half()

    def body(pairs):
        for n in pairs:
            arrive(n)
        for n in pairs:
            for k in range(6):
                p, q = source(2 * n, k), source(2 * n + 1, k)
                rows[0, n, k] = first_of(p, q, low)
                rows[1, n, k] = second_of(p, q, low)

    each_group(rows, body)


def start_chunk(coeff, rows, inner, edge, sums, far_out, near_out):
    def run(down, up):
        each_group(
            rows,
            lambda pairs: open_round(coeff, pairs, rows, rows, inner, edge, sums, down, up),
        )

    by_parity(run, near_out, far_out)


def first_kernel(
    coeff, src, links, inner, edge, rows, sums, far_out, near_out, later, now, held, sems
):
    count = now.shape[0]
    link_copies = [
        pltpu.make_async_copy(links.at[mu], held.at[mu], sems.at[mu]) for mu in range(3)
    ]

    def first_copy(n):
        here = pl.ds(2 * n, 2)
        return pltpu.make_async_copy(src.at[here], now.at[here], sems.at[4 + n])

    rest = src.at[pl.ds(count, later.shape[0])]
    later_copy = pltpu.make_async_copy(rest, later, sems.at[3])
    for mu in (1, 2, 0):
        link_copies[mu].start()
    for n in range(count // 2):
        first_copy(n).start()
    later_copy.start()
    pack_links(held, inner, edge, lambda mu: link_copies[mu].wait())
    pack_rows(lambda n, k: tile(now, (n, k)), rows, lambda n: first_copy(n).wait())
    start_chunk(coeff, rows, inner, edge, sums, far_out, near_out)
    later_copy.wait()


def start_kernel(coeff, first, later, inner, edge, *refs):
    before, (rows, sums, far_out, near_out) = refs[:-4], refs[-4:]
    pack_rows(lambda n, k: tile(later, (first + n, k)), rows)
    held = 0
    for ref in before:
        held = ref.shape[1]
        for row in range(2):
            for n in range(held):
                put(near_out, row, [n], take(ref, row, [n]))
    own = near_out.at[:, pl.ds(held, rows.shape[1])]
    start_chunk(coeff, rows, inner, edge, sums, far_out, own)


def round_kernel(
    coeff,
    next_coeff,
    place,
    far_in,
    near_in,
    rows,
    sums_in,
    start,
    inner,
    edge,
    rows_out,
    sums_out,
    far_out,
    near_out,
    middle,
):
    near_in = near_in.at[:, pl.ds(place, rows.shape[1])]

    def run(lower_side, upper_side):
        below, down = lower_side
        above, up = upper_side

        def body(pairs):
            result = close_round(
                coeff, pairs, below, above, rows, sums_in, start, inner, edge, middle
            )
            for row in range(2):
                put(rows_out, row, pairs, result[row])
            open_round(next_coeff, pairs, rows_out, start, inner, edge, sums_out, down, up)

        each_group(rows, body)

    by_parity(run, (near_in, near_out), (far_in, far_out))


def last_kernel(coeff, first, lead, far_in, near_in, rows, sums_in, start, inner, edge, *rest):
    out, middle, filled, sems = rest[-4:]
    low = low_half()

    def store(n):
        here = pl.ds(2 * n, 2)
        there = pl.ds(first + 2 * n, 2)
        return pltpu.make_async_copy(filled.at[here], out.at[there], sems.at[n])

    def run(below, above):
        def body(pairs):
            lower, upper = close_round(
                coeff, pairs, below, above, rows, sums_in, start, inner, edge, middle
            )
            for n, bottom, top in zip(pairs, lower, upper):
                for k in range(6):
                    p = first_of(bottom[k], top[k], low) * lead
                    q = second_of(bottom[k], top[k], low) * lead
                    for m, value in ((2 * n, p), (2 * n + 1, q)):
                        filled[m, k, 0:8] = value[:, : 2 * LS]
                        filled[m, k, 8:16] = value[:, 2 * LS :]
                store(n).start()

        each_group(rows, body)

    by_parity(run, near_in, far_in)
    for n in range(rows.shape[1]):
        store(n).wait()


VMEM_LIMIT = 32 * 1024 * 1024


def call(
    kernel, outs, args, flops, scratch=(), in_hbm=(), out_hbm=False, aliases={}, unread=()
):
    moved = sum(4 * a.size for a in args) + sum(4 * o.size for o in outs)
    args = [
        pltpu.with_memory_space_constraint(a, pltpu.HBM) if i in in_hbm else a
        for i, a in enumerate(args)
    ]
    vmem = pl.BlockSpec(memory_space=pltpu.VMEM)
    hbm = pl.BlockSpec(memory_space=pltpu.HBM)
    anywhere = pl.BlockSpec(memory_space=pl.ANY)
    return pl.pallas_call(
        kernel,
        out_shape=outs,
        in_specs=[
            hbm if i in in_hbm else anywhere if i in unread else vmem for i in range(len(args))
        ],
        out_specs=[hbm if out_hbm else vmem] * len(outs),
        scratch_shapes=list(scratch),
        input_output_aliases=aliases,
        compiler_params=pltpu.CompilerParams(vmem_limit_bytes=VMEM_LIMIT),
        cost_estimate=pl.CostEstimate(flops=flops, bytes_accessed=moved, transcendentals=0),
    )(*args)


def chunk_sizes(pairs):
    first = pairs * 7 // 12
    return (first, pairs - first)


def halo_body(links, sources):
    vectors = sources.shape[0]
    sizes = chunk_sizes(vectors // 2)
    chunks = range(len(sizes))
    first = [2 * sum(sizes[:chunk]) for chunk in chunks]
    sites, planes = links.shape[4:]
    f32 = functools.partial(jax.ShapeDtypeStruct, dtype=jnp.float32)
    both = [f32((2, pairs, 6, 8, 128)) for pairs in sizes]
    middle = [pltpu.VMEM(shape.shape, jnp.float32) for shape in both]
    raw = [(2 * pairs, 6, planes, sites) for pairs in sizes]
    source_view = jnp.swapaxes(sources, 3, 4).reshape(vectors, 6, planes, sites)
    link_view = jnp.swapaxes(links, 4, 5)
    powers = power_coeffs()
    lead = powers[4]
    steps = [powers[power] / lead for power in (3, 2, 1, 0)]
    work = [2 * pairs * 36 * 2 * 1024 for pairs in sizes]
    count = lax.axis_size("space")
    near_pairs = [(d, d ^ 1) for d in range(count)]
    far_pairs = [(d, (d + 1 if d % 2 else d - 1) % count) for d in range(count)]

    def exchange(far_out, near_out):
        far = lax.ppermute(far_out, "space", far_pairs)
        return far, lax.ppermute(near_out, "space", near_pairs)

    inner, edge, rows, sums, *sends, later = call(
        functools.partial(first_kernel, steps[0]),
        [
            f32((2, 4, 3, 3, 2, 8, 128)),
            f32((3, 3, 2, 8, 128)),
            *[both[0]] * 4,
            f32((vectors - first[1], 6, planes, sites)),
        ],
        [source_view, link_view],
        6 * work[0],
        [
            pltpu.VMEM(raw[0], jnp.float32),
            pltpu.VMEM(link_view.shape, jnp.float32),
            pltpu.SemaphoreType.DMA((4 + sizes[0],)),
        ],
        (0, 1),
    )
    start, fields, halos = [rows], [(rows, sums)], [exchange(*sends)]
    fars, before, places = [], [], [0, 0]
    for chunk in chunks[1:]:
        near_shape = f32((2, places[-1] + sizes[chunk], *both[chunk].shape[2:]))
        rows, sums, far_out, near_out = call(
            functools.partial(start_kernel, steps[0], first[chunk] - first[1]),
            [both[chunk]] * 3 + [near_shape],
            [later, inner, edge, *before],
            6 * work[chunk],
        )
        start.append(rows)
        fields.append((rows, sums))
        fars.append(lax.ppermute(far_out, "space", far_pairs))
        before = [near_out]
        places.append(places[-1] + sizes[chunk])
    near = lax.ppermute(near_out, "space", near_pairs)
    halos += [(far, near) for far in fars]
    for chunk in chunks:
        rows, sums, *sends = call(
            functools.partial(round_kernel, steps[1], steps[2], places[chunk]),
            [both[chunk]] * 4,
            [*halos[chunk], *fields[chunk], start[chunk], inner, edge],
            12 * work[chunk],
            [middle[chunk]],
        )
        fields[chunk] = (rows, sums)
        halos[chunk] = exchange(*sends)
    out = None
    for chunk in chunks:
        args = [*halos[chunk], *fields[chunk], start[chunk], inner, edge]
        (out,) = call(
            functools.partial(last_kernel, steps[3], first[chunk], lead),
            [f32(source_view.shape)],
            args if out is None else args + [out],
            6 * work[chunk],
            [
                middle[chunk],
                pltpu.VMEM(raw[chunk], jnp.float32),
                pltpu.SemaphoreType.DMA((sizes[chunk],)),
            ],
            () if out is None else (len(args),),
            True,
            {} if out is None else {len(args): 0},
        )
    return jnp.swapaxes(out.reshape(vectors, 3, 2, planes, sites), 3, 4)


def shifted(value, axis, steps):
    count = lax.axis_size(axis)
    pairs = [(source, (source + steps) % count) for source in range(count)]
    return lax.ppermute(value, axis, pairs)


def apply_link(link, vector):
    real_part = 0.0
    imag_part = 0.0
    for column in range(3):
        link_re = link[:, column, 0][None]
        link_im = link[:, column, 1][None]
        vec_re = vector[:, column, 0][:, None]
        vec_im = vector[:, column, 1][:, None]
        real_part = real_part + link_re * vec_re - link_im * vec_im
        imag_part = imag_part + link_re * vec_im + link_im * vec_re
    return jnp.stack([real_part, imag_part], axis=2)


def apply_dagger(link, vector):
    real_part = 0.0
    imag_part = 0.0
    for column in range(3):
        link_re = link[column, :, 0][None]
        link_im = link[column, :, 1][None]
        vec_re = vector[:, column, 0][:, None]
        vec_im = vector[:, column, 1][:, None]
        real_part = real_part + link_re * vec_re + link_im * vec_im
        imag_part = imag_part + link_re * vec_im - link_im * vec_re
    return jnp.stack([real_part, imag_part], axis=2)


def z_ahead(array, extent, z_index):
    return jnp.where(
        z_index == extent - 1, jnp.roll(array, extent - 1, axis=-1), jnp.roll(array, -1, axis=-1)
    )


def z_behind(array, extent, z_index):
    return jnp.where(
        z_index == 0, jnp.roll(array, 1 - extent, axis=-1), jnp.roll(array, 1, axis=-1)
    )


def plane_body(links, sources):
    device_count = lax.axis_size("space")
    slabs = device_count // NT
    yz_local = links.shape[4]
    planes = links.shape[5] // device_count
    plane_sites = yz_local * device_count
    vectors = sources.shape[0]
    link_parts = links.reshape(54, yz_local, NT, slabs, planes)
    source_parts = sources.reshape(vectors * 6, yz_local, NT, slabs, planes)
    link_send = jnp.transpose(link_parts, (0, 3, 2, 4, 1)).reshape(
        54, device_count, planes, yz_local
    )
    source_send = jnp.transpose(source_parts, (0, 3, 2, 4, 1)).reshape(
        vectors * 6, device_count, planes, yz_local
    )
    link_recv, source_recv = (
        lax.all_to_all(link_send, "space", split_axis=1, concat_axis=3, tiled=True),
        lax.all_to_all(source_send, "space", split_axis=1, concat_axis=3, tiled=True),
    )
    gauge_local = link_recv.reshape(3, 3, 3, 2, planes, plane_sites)
    source_field = source_recv.reshape(vectors, 3, 2, planes, plane_sites)
    z_index = jnp.arange(plane_sites, dtype=jnp.int32) % LS
    x_top = gauge_local[0]
    x_rest = gauge_local[0][:, :, :, :-1]
    y_back = jnp.roll(gauge_local[1], LS, axis=-1)
    z_back = z_behind(gauge_local[2], LS, z_index)

    def fetch_lower(vector):
        return shifted(apply_dagger(x_top, vector), "space", NT)

    def hop_sum(vector):
        upper_face = shifted(vector, "space", -NT)
        lower_face = fetch_lower(vector)
        ahead = apply_link(
            gauge_local[0], jnp.concatenate([vector[:, :, :, 1:], upper_face], axis=3)
        )
        behind = jnp.concatenate([lower_face, apply_dagger(x_rest, vector[:, :, :, :-1])], axis=3)
        summed = ahead + behind
        summed = (
            summed
            + apply_link(gauge_local[1], jnp.roll(vector, -LS, axis=-1))
            + apply_dagger(y_back, jnp.roll(vector, LS, axis=-1))
        )
        summed = (
            summed
            + apply_link(gauge_local[2], z_ahead(vector, LS, z_index))
            + apply_dagger(z_back, z_behind(vector, LS, z_index))
        )
        return summed

    def scaled(vector):
        return hop_sum(vector) * (-1.0 / 6.0)

    previous = source_field
    current = scaled(previous)
    filtered = cheb_coeffs[0] * previous + cheb_coeffs[1] * current
    for degree in range(2, 5):
        following = 2.0 * scaled(current) - previous
        filtered = filtered + cheb_coeffs[degree] * following
        previous, current = (current, following)
    outgoing = filtered.reshape(vectors * 6, 1, planes, plane_sites)
    returned = lax.all_to_all(outgoing, "space", split_axis=3, concat_axis=1, tiled=True)
    ordered = jnp.transpose(
        returned.reshape(vectors * 6, slabs, NT, planes, yz_local), (0, 4, 2, 1, 3)
    )
    return ordered.reshape(vectors, 3, 2, yz_local, NT * slabs * planes)


def body(links, sources):
    sites, planes = sources.shape[3:]
    if sites == 2 * LS and planes == 2 * NT and sources.shape[0] % 8 == 0:
        return halo_body(links, sources)
    return plane_body(links, sources)


def solution(mesh):
    in_specs = (
        P(None, None, None, None, "space", "groups"),
        P(None, None, None, "space", "groups"),
    )
    out_specs = P(None, None, None, "space", "groups")
    return jax.shard_map(body, mesh=mesh, in_specs=in_specs, out_specs=out_specs, check_vma=False)
```

```python
import functools

import jax
import jax.numpy as jnp
from jax import lax
from jax.experimental import pallas as pl
from jax.experimental.pallas import tpu as pltpu
from jax.sharding import PartitionSpec as P

NT = 8
LS = 32

cheb_coeffs = (0.6, -0.5, 0.35, -0.25, 0.15)


def power_coeffs():
    c0, c1, c2, c3, c4 = cheb_coeffs
    return (c0 - c2 + c4, c1 - 3.0 * c3, 2.0 * c2 - 8.0 * c4, 4.0 * c3, 8.0 * c4)


def lane_ids():
    return lax.broadcasted_iota(jnp.int32, (8, 128), 1)


def sublane_ids():
    return lax.broadcasted_iota(jnp.int32, (8, 128), 0)


def low_half():
    return (lane_ids() // LS) % 2 == 0


def first_of(p, q, low):
    return jnp.where(low, p, pltpu.roll(q, LS, 1))


def second_of(p, q, low):
    return jnp.where(low, pltpu.roll(p, 128 - LS, 1), q)


def z_next(value, z):
    return jnp.where(z == LS - 1, pltpu.roll(value, LS - 1, 1), pltpu.roll(value, 127, 1))


def z_prev(value, z):
    return jnp.where(z == 0, pltpu.roll(value, 129 - LS, 1), pltpu.roll(value, 1, 1))


def x_other(value, even):
    return jnp.where(even, pltpu.roll(value, 7, 0), pltpu.roll(value, 1, 0))


def mat_vec(load, vectors, sums, dagger=False):
    for a in range(3):
        for b in range(3):
            w_re, w_im = load(b, a) if dagger else load(a, b)
            for vec, acc in zip(vectors, sums):
                v_re, v_im = vec[2 * b], vec[2 * b + 1]
                if dagger:
                    acc[2 * a] = acc[2 * a] + w_re * v_re + w_im * v_im
                    acc[2 * a + 1] = acc[2 * a + 1] + w_re * v_im - w_im * v_re
                else:
                    acc[2 * a] = acc[2 * a] + w_re * v_re - w_im * v_im
                    acc[2 * a + 1] = acc[2 * a + 1] + w_re * v_im + w_im * v_re


def zeros(count):
    return [[jnp.zeros((8, 128), jnp.float32) for _ in range(6)] for _ in range(count)]


def link_at(ref, *index):
    return lambda a, b: (ref[index + (a, b, 0)], ref[index + (a, b, 1)])


def tile(ref, index):
    return jnp.concatenate([ref[index + (slice(0, 8),)], ref[index + (slice(8, 16),)]], axis=1)


def parts(*refs):
    return [(refs[0], 0), (refs[0], 1)] if len(refs) == 1 else [(ref, 0) for ref in refs]


def by_parity(run, near, far):
    odd = lax.axis_index("space") % 2 == 1

    @pl.when(odd)
    def _():
        run(near, far)

    @pl.when(jnp.logical_not(odd))
    def _():
        run(far, near)


def each_group(ref, body):
    count = ref.shape[1]

    def step(i, carry):
        body([2 * i, 2 * i + 1])
        return carry

    lax.fori_loop(0, count // 2, step, 0, unroll=count <= 5)
    if count % 2:
        body([count - 1])


def take(ref, row, pairs):
    return [[ref[row, n, k] for k in range(6)] for n in pairs]


def put(ref, row, pairs, vectors):
    for n, vec in zip(pairs, vectors):
        for k in range(6):
            ref[row, n, k] = vec[k]


def pack_links(links, inner, edge, arrive):
    low = low_half()
    z = lane_ids() % LS
    even = sublane_ids() % 2 == 0
    entries = [(a, b, part) for a in range(3) for b in range(3) for part in range(2)]
    rows = tuple(enumerate((first_of, second_of)))

    arrive(1)
    for a, b, part in entries:
        y_link = tile(links, (1, a, b, part)) * (-1.0 / 6.0)
        u_y = first_of(y_link, y_link, low)
        inner[0, 3, a, b, part] = u_y
        inner[1, 3, b, a, part] = u_y if part == 0 else -u_y
        edge[a, b, part] = second_of(y_link, y_link, low)
    arrive(2)
    for a, b, part in entries:
        z_link = tile(links, (2, a, b, part)) * (-1.0 / 6.0)
        for row, pick in rows:
            u_z = pick(z_link, z_link, low)
            inner[row, 1, a, b, part] = u_z
            u_z = z_prev(u_z, z)
            inner[row, 2, b, a, part] = u_z if part == 0 else -u_z
    arrive(0)
    for part in range(2):
        x_link = [
            [tile(links, (0, a, b, part)) * (-1.0 / 6.0) for b in range(3)] for a in range(3)
        ]
        for a in range(3):
            for b in range(3):
                other = x_other(x_link[b][a], even)
                both = x_link[a][b] + (other if part == 0 else -other)
                for row, pick in rows:
                    inner[row, 0, a, b, part] = pick(both, both, low)


def add_inner(inner, row, pairs, field, sums):
    z = lane_ids() % LS
    even = sublane_ids() % 2 == 0
    here = take(field, row, pairs)
    mat_vec(link_at(inner, row, 0), [[x_other(c, even) for c in vec] for vec in here], sums)
    mat_vec(link_at(inner, row, 1), [[z_next(c, z) for c in vec] for vec in here], sums)
    mat_vec(link_at(inner, row, 2), [[z_prev(c, z) for c in vec] for vec in here], sums)
    mat_vec(link_at(inner, row, 3), take(field, 1 - row, pairs), sums)


def scaled_rows(coeff, start, row, pairs):
    return [[coeff * c for c in vec] for vec in take(start, row, pairs)]


def send(edge, pairs, part, row, vectors, out):
    if row == 1:
        field, vectors = vectors, zeros(len(pairs))
        mat_vec(link_at(edge), field, vectors, dagger=True)
    put(*out[part], pairs, vectors)


def local_sums(coeff, pairs, row, rows, start, inner):
    sums = scaled_rows(coeff, start, row, pairs)
    add_inner(inner, row, pairs, rows, sums)
    return sums


def open_round(coeff, pairs, rows, start, inner, edge, sums_out, down, up):
    for row, out in enumerate((down, up)):
        sums = local_sums(coeff, pairs, row, rows, start, inner)
        put(sums_out, row, pairs, sums)
        send(edge, pairs, 0, row, take(rows, row, pairs), out)
        send(edge, pairs, 1, row, sums, out)


def close_round(coeff, pairs, below, above, rows, sums_in, start, inner, edge, middle):
    lower = [
        [s + u for s, u in zip(*both)]
        for both in zip(take(sums_in, 0, pairs), take(*below[0], pairs))
    ]
    put(middle, 0, pairs, lower)
    upper = take(sums_in, 1, pairs)
    mat_vec(link_at(edge), take(*above[0], pairs), upper)
    put(middle, 1, pairs, upper)
    result = []
    for row in range(2):
        sums = [
            [c + (1.0 / 36.0) * r for c, r in zip(*both)]
            for both in zip(scaled_rows(coeff, start, row, pairs), take(rows, row, pairs))
        ]
        add_inner(inner, row, pairs, middle, sums)
        if row == 0:
            sums = [
                [s + u for s, u in zip(*both)] for both in zip(sums, take(*below[1], pairs))
            ]
        else:
            mat_vec(link_at(edge), take(*above[1], pairs), sums)
        result.append(sums)
    return result


def pack_rows(source, rows, arrive=lambda n: None):
    low = low_half()

    def body(pairs):
        for n in pairs:
            arrive(n)
        for n in pairs:
            for k in range(6):
                p, q = source(2 * n, k), source(2 * n + 1, k)
                rows[0, n, k] = first_of(p, q, low)
                rows[1, n, k] = second_of(p, q, low)

    each_group(rows, body)


def start_chunk(coeff, rows, inner, edge, sums, far_out, near_out):
    def run(down, up):
        each_group(
            rows,
            lambda pairs: open_round(coeff, pairs, rows, rows, inner, edge, sums, down, up),
        )

    by_parity(run, parts(near_out), parts(far_out))


def first_kernel(coeff, src, links, inner, edge, rows, far_sums, far_out, later, now, held, sems):
    count = now.shape[0]
    link_copies = [
        pltpu.make_async_copy(links.at[mu], held.at[mu], sems.at[mu]) for mu in range(3)
    ]

    def first_copy(n):
        here = pl.ds(2 * n, 2)
        return pltpu.make_async_copy(src.at[here], now.at[here], sems.at[4 + n])

    rest = src.at[pl.ds(count, later.shape[0])]
    later_copy = pltpu.make_async_copy(rest, later, sems.at[3])
    for mu in (1, 2, 0):
        link_copies[mu].start()
    for n in range(count // 2):
        first_copy(n).start()
    later_copy.start()
    pack_links(held, inner, edge, lambda mu: link_copies[mu].wait())
    pack_rows(lambda n, k: tile(now, (n, k)), rows, lambda n: first_copy(n).wait())

    def run(down, up):
        row, out = (0, down) if up is None else (1, up)

        def body(pairs):
            sums = local_sums(coeff, pairs, row, rows, rows, inner)
            put(far_sums, 0, pairs, sums)
            send(edge, pairs, 0, row, take(rows, row, pairs), out)
            send(edge, pairs, 1, row, sums, out)

        each_group(rows, body)

    by_parity(run, None, parts(far_out))
    later_copy.wait()


def start_kernel(coeff, later, inner, edge, first_rows, far_sums, *refs):
    first_sums, *first_near, rows, sums, far_out, near_out = refs

    def run(down, up):
        row, out = (0, down) if up is None else (1, up)

        def body(pairs):
            ends = local_sums(coeff, pairs, row, first_rows, first_rows, inner)
            put(first_sums, row, pairs, ends)
            put(first_sums, 1 - row, pairs, take(far_sums, 0, pairs))
            send(edge, pairs, 0, row, take(first_rows, row, pairs), out)
            send(edge, pairs, 1, row, ends, out)

        each_group(first_rows, body)

    by_parity(run, parts(*first_near), None)
    pack_rows(lambda n, k: tile(later, (n, k)), rows)
    start_chunk(coeff, rows, inner, edge, sums, far_out, near_out)


def round_kernel(coeff, next_coeff, far_in, *refs):
    *near_in, rows, sums_in, start, inner, edge = refs[:-5]
    rows_out, sums_out, far_out, near_out, middle = refs[-5:]

    def run(lower_side, upper_side):
        below, down = lower_side
        above, up = upper_side

        def body(pairs):
            result = close_round(
                coeff, pairs, below, above, rows, sums_in, start, inner, edge, middle
            )
            for row in range(2):
                put(rows_out, row, pairs, result[row])
            open_round(next_coeff, pairs, rows_out, start, inner, edge, sums_out, down, up)

        each_group(rows, body)

    near_side = parts(*near_in), parts(near_out)
    by_parity(run, near_side, (parts(far_in), parts(far_out)))


def last_kernel(coeff, first, lead, far_in, near_in, rows, sums_in, start, inner, edge, *rest):
    out, middle, filled, sems = rest[-4:]
    low = low_half()

    def store(n):
        here = pl.ds(2 * n, 2)
        there = pl.ds(first + 2 * n, 2)
        return pltpu.make_async_copy(filled.at[here], out.at[there], sems.at[n])

    def run(below, above):
        def body(pairs):
            lower, upper = close_round(
                coeff, pairs, below, above, rows, sums_in, start, inner, edge, middle
            )
            for n, bottom, top in zip(pairs, lower, upper):
                for k in range(6):
                    p = first_of(bottom[k], top[k], low) * lead
                    q = second_of(bottom[k], top[k], low) * lead
                    for m, value in ((2 * n, p), (2 * n + 1, q)):
                        filled[m, k, 0:8] = value[:, : 2 * LS]
                        filled[m, k, 8:16] = value[:, 2 * LS :]
                store(n).start()

        each_group(rows, body)

    by_parity(run, parts(near_in), parts(far_in))
    for n in range(rows.shape[1]):
        store(n).wait()


VMEM_LIMIT = 32 * 1024 * 1024


def call(
    kernel, outs, args, flops, scratch=(), in_hbm=(), out_hbm=False, aliases={}, unread=()
):
    moved = sum(4 * a.size for a in args) + sum(4 * o.size for o in outs)
    args = [
        pltpu.with_memory_space_constraint(a, pltpu.HBM) if i in in_hbm else a
        for i, a in enumerate(args)
    ]
    vmem = pl.BlockSpec(memory_space=pltpu.VMEM)
    hbm = pl.BlockSpec(memory_space=pltpu.HBM)
    anywhere = pl.BlockSpec(memory_space=pl.ANY)
    return pl.pallas_call(
        kernel,
        out_shape=outs,
        in_specs=[
            hbm if i in in_hbm else anywhere if i in unread else vmem for i in range(len(args))
        ],
        out_specs=[hbm if out_hbm else vmem] * len(outs),
        scratch_shapes=list(scratch),
        input_output_aliases=aliases,
        compiler_params=pltpu.CompilerParams(vmem_limit_bytes=VMEM_LIMIT),
        cost_estimate=pl.CostEstimate(flops=flops, bytes_accessed=moved, transcendentals=0),
    )(*args)


def chunk_sizes(pairs):
    first = pairs * 7 // 12
    return (first, pairs - first)


def halo_body(links, sources):
    vectors = sources.shape[0]
    sizes = chunk_sizes(vectors // 2)
    chunks = range(len(sizes))
    first = [2 * sum(sizes[:chunk]) for chunk in chunks]
    sites, planes = links.shape[4:]
    f32 = functools.partial(jax.ShapeDtypeStruct, dtype=jnp.float32)
    both = [f32((2, pairs, 6, 8, 128)) for pairs in sizes]
    middle = [pltpu.VMEM(shape.shape, jnp.float32) for shape in both]
    raw = [(2 * pairs, 6, planes, sites) for pairs in sizes]
    source_view = jnp.swapaxes(sources, 3, 4).reshape(vectors, 6, planes, sites)
    link_view = jnp.swapaxes(links, 4, 5)
    powers = power_coeffs()
    lead = powers[4]
    steps = [powers[power] / lead for power in (3, 2, 1, 0)]
    work = [2 * pairs * 36 * 2 * 1024 for pairs in sizes]
    count = lax.axis_size("space")
    near_pairs = [(d, d ^ 1) for d in range(count)]
    far_pairs = [(d, (d + 1 if d % 2 else d - 1) % count) for d in range(count)]

    def to_far(value):
        return lax.ppermute(value, "space", far_pairs)

    def to_near(value):
        return lax.ppermute(value, "space", near_pairs)

    inner, edge, rows, far_sums, far_out, later = call(
        functools.partial(first_kernel, steps[0]),
        [
            f32((2, 4, 3, 3, 2, 8, 128)),
            f32((3, 3, 2, 8, 128)),
            both[0],
            f32((1, *both[0].shape[1:])),
            both[0],
            f32((vectors - first[1], 6, planes, sites)),
        ],
        [source_view, link_view],
        6 * work[0],
        [
            pltpu.VMEM(raw[0], jnp.float32),
            pltpu.VMEM(link_view.shape, jnp.float32),
            pltpu.SemaphoreType.DMA((4 + sizes[0],)),
        ],
        (0, 1),
    )
    far = to_far(far_out)
    half = f32((1, *both[0].shape[1:]))
    first_sums, *first_near, second_rows, second_sums, far_out, near_out = call(
        functools.partial(start_kernel, steps[0]),
        [both[0], half, half] + [both[1]] * 4,
        [later, inner, edge, rows, far_sums],
        6 * work[1],
    )
    start = [rows, second_rows]
    fields = [(rows, first_sums), (second_rows, second_sums)]
    halos = [(far, *map(to_near, first_near)), (to_far(far_out), to_near(near_out))]
    for chunk in chunks:
        rows, sums, *sends = call(
            functools.partial(round_kernel, steps[1], steps[2]),
            [both[chunk]] * 4,
            [*halos[chunk], *fields[chunk], start[chunk], inner, edge],
            12 * work[chunk],
            [middle[chunk]],
        )
        fields[chunk] = (rows, sums)
        halos[chunk] = (to_far(sends[0]), to_near(sends[1]))
    out = None
    for chunk in chunks:
        args = [*halos[chunk], *fields[chunk], start[chunk], inner, edge]
        (out,) = call(
            functools.partial(last_kernel, steps[3], first[chunk], lead),
            [f32(source_view.shape)],
            args if out is None else args + [out],
            6 * work[chunk],
            [
                middle[chunk],
                pltpu.VMEM(raw[chunk], jnp.float32),
                pltpu.SemaphoreType.DMA((sizes[chunk],)),
            ],
            () if out is None else (len(args),),
            True,
            {} if out is None else {len(args): 0},
        )
    return jnp.swapaxes(out.reshape(vectors, 3, 2, planes, sites), 3, 4)


def shifted(value, axis, steps):
    count = lax.axis_size(axis)
    pairs = [(source, (source + steps) % count) for source in range(count)]
    return lax.ppermute(value, axis, pairs)


def apply_link(link, vector):
    real_part = 0.0
    imag_part = 0.0
    for column in range(3):
        link_re = link[:, column, 0][None]
        link_im = link[:, column, 1][None]
        vec_re = vector[:, column, 0][:, None]
        vec_im = vector[:, column, 1][:, None]
        real_part = real_part + link_re * vec_re - link_im * vec_im
        imag_part = imag_part + link_re * vec_im + link_im * vec_re
    return jnp.stack([real_part, imag_part], axis=2)


def apply_dagger(link, vector):
    real_part = 0.0
    imag_part = 0.0
    for column in range(3):
        link_re = link[column, :, 0][None]
        link_im = link[column, :, 1][None]
        vec_re = vector[:, column, 0][:, None]
        vec_im = vector[:, column, 1][:, None]
        real_part = real_part + link_re * vec_re + link_im * vec_im
        imag_part = imag_part + link_re * vec_im - link_im * vec_re
    return jnp.stack([real_part, imag_part], axis=2)


def z_ahead(array, extent, z_index):
    return jnp.where(
        z_index == extent - 1, jnp.roll(array, extent - 1, axis=-1), jnp.roll(array, -1, axis=-1)
    )


def z_behind(array, extent, z_index):
    return jnp.where(
        z_index == 0, jnp.roll(array, 1 - extent, axis=-1), jnp.roll(array, 1, axis=-1)
    )


def plane_body(links, sources):
    device_count = lax.axis_size("space")
    slabs = device_count // NT
    yz_local = links.shape[4]
    planes = links.shape[5] // device_count
    plane_sites = yz_local * device_count
    vectors = sources.shape[0]
    link_parts = links.reshape(54, yz_local, NT, slabs, planes)
    source_parts = sources.reshape(vectors * 6, yz_local, NT, slabs, planes)
    link_send = jnp.transpose(link_parts, (0, 3, 2, 4, 1)).reshape(
        54, device_count, planes, yz_local
    )
    source_send = jnp.transpose(source_parts, (0, 3, 2, 4, 1)).reshape(
        vectors * 6, device_count, planes, yz_local
    )
    link_recv, source_recv = (
        lax.all_to_all(link_send, "space", split_axis=1, concat_axis=3, tiled=True),
        lax.all_to_all(source_send, "space", split_axis=1, concat_axis=3, tiled=True),
    )
    gauge_local = link_recv.reshape(3, 3, 3, 2, planes, plane_sites)
    source_field = source_recv.reshape(vectors, 3, 2, planes, plane_sites)
    z_index = jnp.arange(plane_sites, dtype=jnp.int32) % LS
    x_top = gauge_local[0]
    x_rest = gauge_local[0][:, :, :, :-1]
    y_back = jnp.roll(gauge_local[1], LS, axis=-1)
    z_back = z_behind(gauge_local[2], LS, z_index)

    def fetch_lower(vector):
        return shifted(apply_dagger(x_top, vector), "space", NT)

    def hop_sum(vector):
        upper_face = shifted(vector, "space", -NT)
        lower_face = fetch_lower(vector)
        ahead = apply_link(
            gauge_local[0], jnp.concatenate([vector[:, :, :, 1:], upper_face], axis=3)
        )
        behind = jnp.concatenate([lower_face, apply_dagger(x_rest, vector[:, :, :, :-1])], axis=3)
        summed = ahead + behind
        summed = (
            summed
            + apply_link(gauge_local[1], jnp.roll(vector, -LS, axis=-1))
            + apply_dagger(y_back, jnp.roll(vector, LS, axis=-1))
        )
        summed = (
            summed
            + apply_link(gauge_local[2], z_ahead(vector, LS, z_index))
            + apply_dagger(z_back, z_behind(vector, LS, z_index))
        )
        return summed

    def scaled(vector):
        return hop_sum(vector) * (-1.0 / 6.0)

    previous = source_field
    current = scaled(previous)
    filtered = cheb_coeffs[0] * previous + cheb_coeffs[1] * current
    for degree in range(2, 5):
        following = 2.0 * scaled(current) - previous
        filtered = filtered + cheb_coeffs[degree] * following
        previous, current = (current, following)
    outgoing = filtered.reshape(vectors * 6, 1, planes, plane_sites)
    returned = lax.all_to_all(outgoing, "space", split_axis=3, concat_axis=1, tiled=True)
    ordered = jnp.transpose(
        returned.reshape(vectors * 6, slabs, NT, planes, yz_local), (0, 4, 2, 1, 3)
    )
    return ordered.reshape(vectors, 3, 2, yz_local, NT * slabs * planes)


def body(links, sources):
    sites, planes = sources.shape[3:]
    if sites == 2 * LS and planes == 2 * NT and sources.shape[0] % 8 == 0:
        return halo_body(links, sources)
    return plane_body(links, sources)


def solution(mesh):
    in_specs = (
        P(None, None, None, None, "space", "groups"),
        P(None, None, None, "space", "groups"),
    )
    out_specs = P(None, None, None, "space", "groups")
    return jax.shard_map(body, mesh=mesh, in_specs=in_specs, out_specs=out_specs, check_vma=False)
```

```python
import functools

import jax
import jax.numpy as jnp
from jax import lax
from jax.experimental import pallas as pl
from jax.experimental.pallas import tpu as pltpu
from jax.sharding import PartitionSpec as P

NT = 8
LS = 32

cheb_coeffs = (0.6, -0.5, 0.35, -0.25, 0.15)


def power_coeffs():
    c0, c1, c2, c3, c4 = cheb_coeffs
    return (c0 - c2 + c4, c1 - 3.0 * c3, 2.0 * c2 - 8.0 * c4, 4.0 * c3, 8.0 * c4)


def lane_ids():
    return lax.broadcasted_iota(jnp.int32, (8, 128), 1)


def sublane_ids():
    return lax.broadcasted_iota(jnp.int32, (8, 128), 0)


def low_half():
    return (lane_ids() // LS) % 2 == 0


def first_of(p, q, low):
    return jnp.where(low, p, pltpu.roll(q, LS, 1))


def second_of(p, q, low):
    return jnp.where(low, pltpu.roll(p, 128 - LS, 1), q)


def z_next(value, z):
    return jnp.where(z == LS - 1, pltpu.roll(value, LS - 1, 1), pltpu.roll(value, 127, 1))


def z_prev(value, z):
    return jnp.where(z == 0, pltpu.roll(value, 129 - LS, 1), pltpu.roll(value, 1, 1))


def x_other(value, even):
    return jnp.where(even, pltpu.roll(value, 7, 0), pltpu.roll(value, 1, 0))


def mat_vec(load, vectors, sums, dagger=False):
    for a in range(3):
        for b in range(3):
            w_re, w_im = load(b, a) if dagger else load(a, b)
            for vec, acc in zip(vectors, sums):
                v_re, v_im = vec[2 * b], vec[2 * b + 1]
                if dagger:
                    acc[2 * a] = acc[2 * a] + w_re * v_re + w_im * v_im
                    acc[2 * a + 1] = acc[2 * a + 1] + w_re * v_im - w_im * v_re
                else:
                    acc[2 * a] = acc[2 * a] + w_re * v_re - w_im * v_im
                    acc[2 * a + 1] = acc[2 * a + 1] + w_re * v_im + w_im * v_re


def zeros(count):
    return [[jnp.zeros((8, 128), jnp.float32) for _ in range(6)] for _ in range(count)]


def link_at(ref, *index):
    return lambda a, b: (ref[index + (a, b, 0)], ref[index + (a, b, 1)])


def tile(ref, index):
    return jnp.concatenate([ref[index + (slice(0, 8),)], ref[index + (slice(8, 16),)]], axis=1)


def parts(*refs):
    return [(refs[0], 0), (refs[0], 1)] if len(refs) == 1 else [(ref, 0) for ref in refs]


def by_parity(run, near, far):
    odd = lax.axis_index("space") % 2 == 1

    @pl.when(odd)
    def _():
        run(near, far)

    @pl.when(jnp.logical_not(odd))
    def _():
        run(far, near)


def each_group(ref, body):
    count = ref.shape[1]

    def step(i, carry):
        body([2 * i, 2 * i + 1])
        return carry

    lax.fori_loop(0, count // 2, step, 0, unroll=count <= 5)
    if count % 2:
        body([count - 1])


def take(ref, row, pairs):
    return [[ref[row, n, k] for k in range(6)] for n in pairs]


def put(ref, row, pairs, vectors):
    for n, vec in zip(pairs, vectors):
        for k in range(6):
            ref[row, n, k] = vec[k]


def pack_edge(links, edge):
    low = low_half()
    for a in range(3):
        for b in range(3):
            for part in range(2):
                y_link = tile(links, (1, a, b, part)) * (-1.0 / 6.0)
                edge[a, b, part] = second_of(y_link, y_link, low)


def pack_links(links, inner, slot, row):
    low = low_half()
    z = lane_ids() % LS
    even = sublane_ids() % 2 == 0
    pick = second_of if row else first_of
    for part in range(2):
        x_link, y_link, z_link = (
            [
                [tile(links, (mu, a, b, part)) * (-1.0 / 6.0) for b in range(3)]
                for a in range(3)
            ]
            for mu in range(3)
        )
        for a in range(3):
            for b in range(3):
                other = x_other(x_link[b][a], even)
                both = x_link[a][b] + (other if part == 0 else -other)
                inner[slot, 0, a, b, part] = pick(both, both, low)
                u_z = pick(z_link[a][b], z_link[a][b], low)
                inner[slot, 1, a, b, part] = u_z
                u_z = z_prev(u_z, z)
                inner[slot, 2, b, a, part] = u_z if part == 0 else -u_z
                u_y = first_of(y_link[a][b], y_link[a][b], low)
                if row == 0:
                    inner[slot, 3, a, b, part] = u_y
                else:
                    inner[slot, 3, b, a, part] = u_y if part == 0 else -u_y


def add_x_and_z(inner, slot, vectors, sums):
    z = lane_ids() % LS
    even = sublane_ids() % 2 == 0
    mat_vec(link_at(inner, slot, 0), [[x_other(c, even) for c in vec] for vec in vectors], sums)
    mat_vec(link_at(inner, slot, 1), [[z_next(c, z) for c in vec] for vec in vectors], sums)
    mat_vec(link_at(inner, slot, 2), [[z_prev(c, z) for c in vec] for vec in vectors], sums)


def add_inner(inner, slot, row, pairs, field, sums):
    add_x_and_z(inner, slot, take(field, row, pairs), sums)
    mat_vec(link_at(inner, slot, 3), take(field, 1 - row, pairs), sums)


def scaled_rows(coeff, start, row, pairs):
    return [[coeff * c for c in vec] for vec in take(start, row, pairs)]


def send(edge, pairs, part, row, vectors, out):
    if row == 1:
        field, vectors = vectors, zeros(len(pairs))
        mat_vec(link_at(edge), field, vectors, dagger=True)
    put(*out[part], pairs, vectors)


def local_sums(coeff, pairs, row, rows, start, inner, slot):
    sums = scaled_rows(coeff, start, row, pairs)
    add_inner(inner, slot, row, pairs, rows, sums)
    return sums


def open_round(coeff, pairs, rows, start, inner, edge, sums_out, down, up):
    for row, out in enumerate((down, up)):
        sums = local_sums(coeff, pairs, row, rows, start, inner, row)
        put(sums_out, row, pairs, sums)
        send(edge, pairs, 0, row, take(rows, row, pairs), out)
        send(edge, pairs, 1, row, sums, out)


def plus(sums, more):
    return [[s + m for s, m in zip(*both)] for both in zip(sums, more)]


def add_message(edge, pairs, part, row, message, sums):
    received = take(*message[part], pairs)
    if row == 0:
        return plus(sums, received)
    mat_vec(link_at(edge), received, sums)
    return sums


def second_start(coeff, pairs, row, rows, start):
    return [
        [c + (1.0 / 36.0) * r for c, r in zip(*both)]
        for both in zip(scaled_rows(coeff, start, row, pairs), take(rows, row, pairs))
    ]


def close_round(coeff, pairs, below, above, rows, sums_in, start, inner, edge, middle):
    for row, message in enumerate((below, above)):
        sums = take(sums_in, row, pairs)
        put(middle, row, pairs, add_message(edge, pairs, 0, row, message, sums))
    result = []
    for row, message in enumerate((below, above)):
        sums = second_start(coeff, pairs, row, rows, start)
        add_inner(inner, row, row, pairs, middle, sums)
        result.append(add_message(edge, pairs, 1, row, message, sums))
    return result


def side(below, above):
    return (0, below) if above is None else (1, above)


def pack_rows(source, rows, arrive=lambda n: None):
    low = low_half()

    def body(pairs):
        for n in pairs:
            arrive(n)
        for n in pairs:
            for k in range(6):
                p, q = source(2 * n, k), source(2 * n + 1, k)
                rows[0, n, k] = first_of(p, q, low)
                rows[1, n, k] = second_of(p, q, low)

    each_group(rows, body)


def start_chunk(coeff, rows, inner, edge, sums, far_out, near_out):
    def run(down, up):
        each_group(
            rows,
            lambda pairs: open_round(coeff, pairs, rows, rows, inner, edge, sums, down, up),
        )

    by_parity(run, parts(near_out), parts(far_out))


def first_kernel(coeff, src, links, inner, edge, rows, far_sums, far_out, later, held, now, sems):
    count = now.shape[0]
    link_copies = [
        pltpu.make_async_copy(links.at[mu], held.at[mu], sems.at[mu]) for mu in range(3)
    ]

    def first_copy(n):
        here = pl.ds(2 * n, 2)
        return pltpu.make_async_copy(src.at[here], now.at[here], sems.at[4 + n])

    rest = src.at[pl.ds(count, later.shape[0])]
    later_copy = pltpu.make_async_copy(rest, later, sems.at[3])
    for mu in (1, 2, 0):
        link_copies[mu].start()
    for n in range(count // 2):
        first_copy(n).start()
    later_copy.start()
    link_copies[1].wait()
    pack_edge(held, edge)
    link_copies[2].wait()
    link_copies[0].wait()
    by_parity(lambda *sides: pack_links(held, inner, 0, side(*sides)[0]), None, True)
    pack_rows(lambda n, k: tile(now, (n, k)), rows, lambda n: first_copy(n).wait())

    def run(*sides):
        row, out = side(*sides)

        def body(pairs):
            sums = local_sums(coeff, pairs, row, rows, rows, inner, 0)
            put(far_sums, 0, pairs, sums)
            send(edge, pairs, 0, row, take(rows, row, pairs), out)
            send(edge, pairs, 1, row, sums, out)

        each_group(rows, body)

    by_parity(run, None, parts(far_out))
    later_copy.wait()


def start_kernel(coeff, later, links, far_inner, edge, first_rows, far_sums, inner, *refs):
    first_sums, *first_near, rows, sums, far_out, near_out = refs

    def run(*sides):
        row, out = side(*sides)
        pack_links(links, inner, row, row)
        for term in range(4):
            for a in range(3):
                for b in range(3):
                    for part in range(2):
                        inner[1 - row, term, a, b, part] = far_inner[0, term, a, b, part]

        def body(pairs):
            ends = local_sums(coeff, pairs, row, first_rows, first_rows, inner, row)
            put(first_sums, row, pairs, ends)
            put(first_sums, 1 - row, pairs, take(far_sums, 0, pairs))
            send(edge, pairs, 0, row, take(first_rows, row, pairs), out)
            send(edge, pairs, 1, row, ends, out)

        each_group(first_rows, body)

    by_parity(run, parts(*first_near), None)
    pack_rows(lambda n, k: tile(later, (n, k)), rows)
    start_chunk(coeff, rows, inner, edge, sums, far_out, near_out)


def round_kernel(coeff, next_coeff, far_in, *refs):
    *near_in, rows, sums_in, start, inner, edge = refs[:-5]
    rows_out, sums_out, far_out, near_out, middle = refs[-5:]

    def run(lower_side, upper_side):
        below, down = lower_side
        above, up = upper_side

        def body(pairs):
            result = close_round(
                coeff, pairs, below, above, rows, sums_in, start, inner, edge, middle
            )
            for row in range(2):
                put(rows_out, row, pairs, result[row])
            open_round(next_coeff, pairs, rows_out, start, inner, edge, sums_out, down, up)

        each_group(rows, body)

    near_side = parts(*near_in), parts(near_out)
    by_parity(run, near_side, (parts(far_in), parts(far_out)))


def near_kernel(coeff, near_in, rows, sums_in, start, inner, edge, partial, middle):
    def run(*sides):
        row, message = side(*sides)

        def body(pairs):
            first = add_message(edge, pairs, 0, row, message, take(sums_in, row, pairs))
            put(middle, row, pairs, first)
            sums = second_start(coeff, pairs, row, rows, start)
            add_x_and_z(inner, row, take(middle, row, pairs), sums)
            put(partial, row, pairs, add_message(edge, pairs, 1, row, message, sums))
            sums = second_start(coeff, pairs, 1 - row, rows, start)
            mat_vec(link_at(inner, 1 - row, 3), take(middle, row, pairs), sums)
            put(partial, 1 - row, pairs, sums)

        each_group(rows, body)

    by_parity(run, parts(near_in), None)


def last_kernel(first, lead, far_in, partial, sums_in, inner, edge, *rest):
    out, middle, filled, sems = rest[-4:]
    low = low_half()

    def store(n):
        here = pl.ds(2 * n, 2)
        there = pl.ds(first + 2 * n, 2)
        return pltpu.make_async_copy(filled.at[here], out.at[there], sems.at[n])

    def run(*sides):
        row, message = side(*sides)

        def body(pairs):
            sums = add_message(edge, pairs, 0, row, message, take(sums_in, row, pairs))
            put(middle, row, pairs, sums)
            ends = [None, None]
            ends[1 - row] = take(partial, 1 - row, pairs)
            mat_vec(link_at(inner, 1 - row, 3), take(middle, row, pairs), ends[1 - row])
            sums = take(partial, row, pairs)
            add_x_and_z(inner, row, take(middle, row, pairs), sums)
            ends[row] = add_message(edge, pairs, 1, row, message, sums)
            lower, upper = ends
            for n, bottom, top in zip(pairs, lower, upper):
                for k in range(6):
                    p = first_of(bottom[k], top[k], low) * lead
                    q = second_of(bottom[k], top[k], low) * lead
                    for m, value in ((2 * n, p), (2 * n + 1, q)):
                        filled[m, k, 0:8] = value[:, : 2 * LS]
                        filled[m, k, 8:16] = value[:, 2 * LS :]
                store(n).start()

        each_group(sums_in, body)

    by_parity(run, None, parts(far_in))
    for n in range(sums_in.shape[1]):
        store(n).wait()


VMEM_LIMIT = 32 * 1024 * 1024


def call(
    kernel, outs, args, flops, scratch=(), in_hbm=(), out_hbm=False, aliases={}, unread=()
):
    moved = sum(4 * a.size for a in args) + sum(4 * o.size for o in outs)
    args = [
        pltpu.with_memory_space_constraint(a, pltpu.HBM) if i in in_hbm else a
        for i, a in enumerate(args)
    ]
    vmem = pl.BlockSpec(memory_space=pltpu.VMEM)
    hbm = pl.BlockSpec(memory_space=pltpu.HBM)
    anywhere = pl.BlockSpec(memory_space=pl.ANY)
    return pl.pallas_call(
        kernel,
        out_shape=outs,
        in_specs=[
            hbm if i in in_hbm else anywhere if i in unread else vmem for i in range(len(args))
        ],
        out_specs=[hbm if out_hbm else vmem] * len(outs),
        scratch_shapes=list(scratch),
        input_output_aliases=aliases,
        compiler_params=pltpu.CompilerParams(vmem_limit_bytes=VMEM_LIMIT),
        cost_estimate=pl.CostEstimate(flops=flops, bytes_accessed=moved, transcendentals=0),
    )(*args)


def chunk_sizes(pairs):
    first = pairs * 7 // 12
    return (first, pairs - first)


def halo_body(links, sources):
    vectors = sources.shape[0]
    sizes = chunk_sizes(vectors // 2)
    chunks = range(len(sizes))
    first = [2 * sum(sizes[:chunk]) for chunk in chunks]
    sites, planes = links.shape[4:]
    f32 = functools.partial(jax.ShapeDtypeStruct, dtype=jnp.float32)
    both = [f32((2, pairs, 6, 8, 128)) for pairs in sizes]
    middle = [pltpu.VMEM(shape.shape, jnp.float32) for shape in both]
    raw = [(2 * pairs, 6, planes, sites) for pairs in sizes]
    source_view = jnp.swapaxes(sources, 3, 4).reshape(vectors, 6, planes, sites)
    link_view = jnp.swapaxes(links, 4, 5)
    powers = power_coeffs()
    lead = powers[4]
    steps = [powers[power] / lead for power in (3, 2, 1, 0)]
    work = [2 * pairs * 36 * 2 * 1024 for pairs in sizes]
    count = lax.axis_size("space")
    near_pairs = [(d, d ^ 1) for d in range(count)]
    far_pairs = [(d, (d + 1 if d % 2 else d - 1) % count) for d in range(count)]

    def to_far(value):
        return lax.ppermute(value, "space", far_pairs)

    def to_near(value):
        return lax.ppermute(value, "space", near_pairs)

    far_inner, edge, rows, far_sums, far_out, later, held = call(
        functools.partial(first_kernel, steps[0]),
        [
            f32((1, 4, 3, 3, 2, 8, 128)),
            f32((3, 3, 2, 8, 128)),
            both[0],
            f32((1, *both[0].shape[1:])),
            both[0],
            f32((vectors - first[1], 6, planes, sites)),
            f32(link_view.shape),
        ],
        [source_view, link_view],
        6 * work[0],
        [
            pltpu.VMEM(raw[0], jnp.float32),
            pltpu.SemaphoreType.DMA((4 + sizes[0],)),
        ],
        (0, 1),
    )
    far = to_far(far_out)
    half = f32((1, *both[0].shape[1:]))
    inner, first_sums, *first_near, second_rows, second_sums, far_out, near_out = call(
        functools.partial(start_kernel, steps[0]),
        [f32((2, 4, 3, 3, 2, 8, 128)), both[0], half, half] + [both[1]] * 4,
        [later, held, far_inner, edge, rows, far_sums],
        6 * work[1],
    )
    start = [rows, second_rows]
    fields = [(rows, first_sums), (second_rows, second_sums)]
    halos = [(far, *map(to_near, first_near)), (to_far(far_out), to_near(near_out))]
    for chunk in chunks:
        rows, sums, *sends = call(
            functools.partial(round_kernel, steps[1], steps[2]),
            [both[chunk]] * 4,
            [*halos[chunk], *fields[chunk], start[chunk], inner, edge],
            12 * work[chunk],
            [middle[chunk]],
        )
        fields[chunk] = (rows, sums)
        halos[chunk] = (to_far(sends[0]), to_near(sends[1]))
    out = None
    for chunk in chunks:
        far_in, near_in = halos[chunk]
        (partial,) = call(
            functools.partial(near_kernel, steps[3]),
            [both[chunk]],
            [near_in, *fields[chunk], start[chunk], inner, edge],
            4 * work[chunk],
            [middle[chunk]],
        )
        args = [far_in, partial, fields[chunk][1], inner, edge]
        (out,) = call(
            functools.partial(last_kernel, first[chunk], lead),
            [f32(source_view.shape)],
            args if out is None else args + [out],
            6 * work[chunk],
            [
                middle[chunk],
                pltpu.VMEM(raw[chunk], jnp.float32),
                pltpu.SemaphoreType.DMA((sizes[chunk],)),
            ],
            () if out is None else (len(args),),
            True,
            {} if out is None else {len(args): 0},
        )
    return jnp.swapaxes(out.reshape(vectors, 3, 2, planes, sites), 3, 4)


def shifted(value, axis, steps):
    count = lax.axis_size(axis)
    pairs = [(source, (source + steps) % count) for source in range(count)]
    return lax.ppermute(value, axis, pairs)


def apply_link(link, vector):
    real_part = 0.0
    imag_part = 0.0
    for column in range(3):
        link_re = link[:, column, 0][None]
        link_im = link[:, column, 1][None]
        vec_re = vector[:, column, 0][:, None]
        vec_im = vector[:, column, 1][:, None]
        real_part = real_part + link_re * vec_re - link_im * vec_im
        imag_part = imag_part + link_re * vec_im + link_im * vec_re
    return jnp.stack([real_part, imag_part], axis=2)


def apply_dagger(link, vector):
    real_part = 0.0
    imag_part = 0.0
    for column in range(3):
        link_re = link[column, :, 0][None]
        link_im = link[column, :, 1][None]
        vec_re = vector[:, column, 0][:, None]
        vec_im = vector[:, column, 1][:, None]
        real_part = real_part + link_re * vec_re + link_im * vec_im
        imag_part = imag_part + link_re * vec_im - link_im * vec_re
    return jnp.stack([real_part, imag_part], axis=2)


def z_ahead(array, extent, z_index):
    return jnp.where(
        z_index == extent - 1, jnp.roll(array, extent - 1, axis=-1), jnp.roll(array, -1, axis=-1)
    )


def z_behind(array, extent, z_index):
    return jnp.where(
        z_index == 0, jnp.roll(array, 1 - extent, axis=-1), jnp.roll(array, 1, axis=-1)
    )


def plane_body(links, sources):
    device_count = lax.axis_size("space")
    slabs = device_count // NT
    yz_local = links.shape[4]
    planes = links.shape[5] // device_count
    plane_sites = yz_local * device_count
    vectors = sources.shape[0]
    link_parts = links.reshape(54, yz_local, NT, slabs, planes)
    source_parts = sources.reshape(vectors * 6, yz_local, NT, slabs, planes)
    link_send = jnp.transpose(link_parts, (0, 3, 2, 4, 1)).reshape(
        54, device_count, planes, yz_local
    )
    source_send = jnp.transpose(source_parts, (0, 3, 2, 4, 1)).reshape(
        vectors * 6, device_count, planes, yz_local
    )
    link_recv, source_recv = (
        lax.all_to_all(link_send, "space", split_axis=1, concat_axis=3, tiled=True),
        lax.all_to_all(source_send, "space", split_axis=1, concat_axis=3, tiled=True),
    )
    gauge_local = link_recv.reshape(3, 3, 3, 2, planes, plane_sites)
    source_field = source_recv.reshape(vectors, 3, 2, planes, plane_sites)
    z_index = jnp.arange(plane_sites, dtype=jnp.int32) % LS
    x_top = gauge_local[0]
    x_rest = gauge_local[0][:, :, :, :-1]
    y_back = jnp.roll(gauge_local[1], LS, axis=-1)
    z_back = z_behind(gauge_local[2], LS, z_index)

    def fetch_lower(vector):
        return shifted(apply_dagger(x_top, vector), "space", NT)

    def hop_sum(vector):
        upper_face = shifted(vector, "space", -NT)
        lower_face = fetch_lower(vector)
        ahead = apply_link(
            gauge_local[0], jnp.concatenate([vector[:, :, :, 1:], upper_face], axis=3)
        )
        behind = jnp.concatenate([lower_face, apply_dagger(x_rest, vector[:, :, :, :-1])], axis=3)
        summed = ahead + behind
        summed = (
            summed
            + apply_link(gauge_local[1], jnp.roll(vector, -LS, axis=-1))
            + apply_dagger(y_back, jnp.roll(vector, LS, axis=-1))
        )
        summed = (
            summed
            + apply_link(gauge_local[2], z_ahead(vector, LS, z_index))
            + apply_dagger(z_back, z_behind(vector, LS, z_index))
        )
        return summed

    def scaled(vector):
        return hop_sum(vector) * (-1.0 / 6.0)

    previous = source_field
    current = scaled(previous)
    filtered = cheb_coeffs[0] * previous + cheb_coeffs[1] * current
    for degree in range(2, 5):
        following = 2.0 * scaled(current) - previous
        filtered = filtered + cheb_coeffs[degree] * following
        previous, current = (current, following)
    outgoing = filtered.reshape(vectors * 6, 1, planes, plane_sites)
    returned = lax.all_to_all(outgoing, "space", split_axis=3, concat_axis=1, tiled=True)
    ordered = jnp.transpose(
        returned.reshape(vectors * 6, slabs, NT, planes, yz_local), (0, 4, 2, 1, 3)
    )
    return ordered.reshape(vectors, 3, 2, yz_local, NT * slabs * planes)


def body(links, sources):
    sites, planes = sources.shape[3:]
    if sites == 2 * LS and planes == 2 * NT and sources.shape[0] % 8 == 0:
        return halo_body(links, sources)
    return plane_body(links, sources)


def solution(mesh):
    in_specs = (
        P(None, None, None, None, "space", "groups"),
        P(None, None, None, "space", "groups"),
    )
    out_specs = P(None, None, None, "space", "groups")
    return jax.shard_map(body, mesh=mesh, in_specs=in_specs, out_specs=out_specs, check_vma=False)
```

```python
import functools

import jax
import jax.numpy as jnp
from jax import lax
from jax.experimental import pallas as pl
from jax.experimental.pallas import tpu as pltpu
from jax.sharding import PartitionSpec as P

NT = 8
LS = 32

cheb_coeffs = (0.6, -0.5, 0.35, -0.25, 0.15)


def power_coeffs():
    c0, c1, c2, c3, c4 = cheb_coeffs
    return (c0 - c2 + c4, c1 - 3.0 * c3, 2.0 * c2 - 8.0 * c4, 4.0 * c3, 8.0 * c4)


def lane_ids():
    return lax.broadcasted_iota(jnp.int32, (8, 128), 1)


def sublane_ids():
    return lax.broadcasted_iota(jnp.int32, (8, 128), 0)


def low_half():
    return (lane_ids() // LS) % 2 == 0


def first_of(p, q, low):
    return jnp.where(low, p, pltpu.roll(q, LS, 1))


def second_of(p, q, low):
    return jnp.where(low, pltpu.roll(p, 128 - LS, 1), q)


def z_next(value, z):
    return jnp.where(z == LS - 1, pltpu.roll(value, LS - 1, 1), pltpu.roll(value, 127, 1))


def z_prev(value, z):
    return jnp.where(z == 0, pltpu.roll(value, 129 - LS, 1), pltpu.roll(value, 1, 1))


def x_other(value, even):
    return jnp.where(even, pltpu.roll(value, 7, 0), pltpu.roll(value, 1, 0))


def mat_vec(load, vectors, sums, dagger=False):
    for a in range(3):
        for b in range(3):
            w_re, w_im = load(b, a) if dagger else load(a, b)
            for vec, acc in zip(vectors, sums):
                v_re, v_im = vec[2 * b], vec[2 * b + 1]
                if dagger:
                    acc[2 * a] = acc[2 * a] + w_re * v_re + w_im * v_im
                    acc[2 * a + 1] = acc[2 * a + 1] + w_re * v_im - w_im * v_re
                else:
                    acc[2 * a] = acc[2 * a] + w_re * v_re - w_im * v_im
                    acc[2 * a + 1] = acc[2 * a + 1] + w_re * v_im + w_im * v_re


def zeros(count):
    return [[jnp.zeros((8, 128), jnp.float32) for _ in range(6)] for _ in range(count)]


def link_at(ref, *index):
    return lambda a, b: (ref[index + (a, b, 0)], ref[index + (a, b, 1)])


def tile(ref, index):
    return jnp.concatenate([ref[index + (slice(0, 8),)], ref[index + (slice(8, 16),)]], axis=1)


def parts(*refs):
    return [(refs[0], 0), (refs[0], 1)] if len(refs) == 1 else [(ref, 0) for ref in refs]


def by_parity(run, near, far):
    odd = lax.axis_index("space") % 2 == 1

    @pl.when(odd)
    def _():
        run(near, far)

    @pl.when(jnp.logical_not(odd))
    def _():
        run(far, near)


def each_group(ref, body):
    count = ref.shape[1]

    def step(i, carry):
        body([2 * i, 2 * i + 1])
        return carry

    lax.fori_loop(0, count // 2, step, 0, unroll=count <= 5)
    if count % 2:
        body([count - 1])


def take(ref, row, pairs):
    return [[ref[row, n, k] for k in range(6)] for n in pairs]


def put(ref, row, pairs, vectors):
    for n, vec in zip(pairs, vectors):
        for k in range(6):
            ref[row, n, k] = vec[k]


def pack_edge(links, edge):
    low = low_half()
    for a in range(3):
        for b in range(3):
            for part in range(2):
                y_link = tile(links, (1, a, b, part)) * (-1.0 / 6.0)
                edge[a, b, part] = second_of(y_link, y_link, low)


def pack_links(links, inner, slot, row):
    low = low_half()
    z = lane_ids() % LS
    even = sublane_ids() % 2 == 0
    pick = second_of if row else first_of
    for part in range(2):
        x_link, y_link, z_link = (
            [
                [tile(links, (mu, a, b, part)) * (-1.0 / 6.0) for b in range(3)]
                for a in range(3)
            ]
            for mu in range(3)
        )
        for a in range(3):
            for b in range(3):
                other = x_other(x_link[b][a], even)
                both = x_link[a][b] + (other if part == 0 else -other)
                inner[slot, 0, a, b, part] = pick(both, both, low)
                u_z = pick(z_link[a][b], z_link[a][b], low)
                inner[slot, 1, a, b, part] = u_z
                u_z = z_prev(u_z, z)
                inner[slot, 2, b, a, part] = u_z if part == 0 else -u_z
                u_y = first_of(y_link[a][b], y_link[a][b], low)
                if row == 0:
                    inner[slot, 3, a, b, part] = u_y
                else:
                    inner[slot, 3, b, a, part] = u_y if part == 0 else -u_y


def add_x_and_z(inner, slot, vectors, sums):
    z = lane_ids() % LS
    even = sublane_ids() % 2 == 0
    mat_vec(link_at(inner, slot, 0), [[x_other(c, even) for c in vec] for vec in vectors], sums)
    mat_vec(link_at(inner, slot, 1), [[z_next(c, z) for c in vec] for vec in vectors], sums)
    mat_vec(link_at(inner, slot, 2), [[z_prev(c, z) for c in vec] for vec in vectors], sums)


def add_inner(inner, slot, row, pairs, field, sums):
    add_x_and_z(inner, slot, take(field, row, pairs), sums)
    mat_vec(link_at(inner, slot, 3), take(field, 1 - row, pairs), sums)


def scaled_rows(coeff, start, row, pairs):
    return [[coeff * c for c in vec] for vec in take(start, row, pairs)]


def send(edge, pairs, part, row, vectors, out):
    if row == 1:
        field, vectors = vectors, zeros(len(pairs))
        mat_vec(link_at(edge), field, vectors, dagger=True)
    put(*out[part], pairs, vectors)


def local_sums(coeff, pairs, row, rows, start, inner, slot):
    sums = scaled_rows(coeff, start, row, pairs)
    add_inner(inner, slot, row, pairs, rows, sums)
    return sums


def open_round(coeff, pairs, rows, start, inner, edge, sums_out, down, up):
    for row, out in enumerate((down, up)):
        sums = local_sums(coeff, pairs, row, rows, start, inner, row)
        put(sums_out, row, pairs, sums)
        send(edge, pairs, 0, row, take(rows, row, pairs), out)
        send(edge, pairs, 1, row, sums, out)


def plus(sums, more):
    return [[s + m for s, m in zip(*both)] for both in zip(sums, more)]


def add_message(edge, pairs, part, row, message, sums):
    received = take(*message[part], pairs)
    if row == 0:
        return plus(sums, received)
    mat_vec(link_at(edge), received, sums)
    return sums


def second_start(coeff, pairs, row, rows, start):
    return [
        [c + (1.0 / 36.0) * r for c, r in zip(*both)]
        for both in zip(scaled_rows(coeff, start, row, pairs), take(rows, row, pairs))
    ]


def close_round(coeff, pairs, below, above, rows, sums_in, start, inner, edge, middle):
    for row, message in enumerate((below, above)):
        sums = take(sums_in, row, pairs)
        put(middle, row, pairs, add_message(edge, pairs, 0, row, message, sums))
    result = []
    for row, message in enumerate((below, above)):
        sums = second_start(coeff, pairs, row, rows, start)
        add_inner(inner, row, row, pairs, middle, sums)
        result.append(add_message(edge, pairs, 1, row, message, sums))
    return result


def side(below, above):
    return (0, below) if above is None else (1, above)


def pack_rows(source, rows, arrive=lambda n: None):
    low = low_half()

    def body(pairs):
        for n in pairs:
            arrive(n)
        for n in pairs:
            for k in range(6):
                p, q = source(2 * n, k), source(2 * n + 1, k)
                rows[0, n, k] = first_of(p, q, low)
                rows[1, n, k] = second_of(p, q, low)

    each_group(rows, body)


def start_chunk(coeff, rows, inner, edge, sums, far_out, near_out):
    def run(down, up):
        each_group(
            rows,
            lambda pairs: open_round(coeff, pairs, rows, rows, inner, edge, sums, down, up),
        )

    by_parity(run, parts(near_out), parts(far_out))


def first_kernel(coeff, src, links, inner, edge, rows, far_sums, far_out, later, held, now, sems):
    count = now.shape[0]
    link_copies = [
        pltpu.make_async_copy(links.at[mu], held.at[mu], sems.at[mu]) for mu in range(3)
    ]

    def first_copy(n):
        here = pl.ds(2 * n, 2)
        return pltpu.make_async_copy(src.at[here], now.at[here], sems.at[4 + n])

    rest = src.at[pl.ds(count, later.shape[0])]
    later_copy = pltpu.make_async_copy(rest, later, sems.at[3])
    for mu in (1, 2, 0):
        link_copies[mu].start()
    for n in range(count // 2):
        first_copy(n).start()
    later_copy.start()
    link_copies[1].wait()
    pack_edge(held, edge)
    link_copies[2].wait()
    link_copies[0].wait()
    by_parity(lambda *sides: pack_links(held, inner, 0, side(*sides)[0]), None, True)
    pack_rows(lambda n, k: tile(now, (n, k)), rows, lambda n: first_copy(n).wait())

    def run(*sides):
        row, out = side(*sides)

        def body(pairs):
            sums = local_sums(coeff, pairs, row, rows, rows, inner, 0)
            put(far_sums, 0, pairs, sums)
            send(edge, pairs, 0, row, take(rows, row, pairs), out)
            send(edge, pairs, 1, row, sums, out)

        each_group(rows, body)

    by_parity(run, None, parts(far_out))
    later_copy.wait()


def start_kernel(coeff, later, links, far_inner, edge, first_rows, far_sums, inner, *refs):
    first_sums, *first_near, rows, sums, far_out, near_out = refs

    def run(*sides):
        row, out = side(*sides)
        pack_links(links, inner, row, row)
        for term in range(4):
            for a in range(3):
                for b in range(3):
                    for part in range(2):
                        inner[1 - row, term, a, b, part] = far_inner[0, term, a, b, part]

        def body(pairs):
            ends = local_sums(coeff, pairs, row, first_rows, first_rows, inner, row)
            put(first_sums, row, pairs, ends)
            put(first_sums, 1 - row, pairs, take(far_sums, 0, pairs))
            send(edge, pairs, 0, row, take(first_rows, row, pairs), out)
            send(edge, pairs, 1, row, ends, out)

        each_group(first_rows, body)

    by_parity(run, parts(*first_near), None)
    pack_rows(lambda n, k: tile(later, (n, k)), rows)
    start_chunk(coeff, rows, inner, edge, sums, far_out, near_out)


def round_kernel(coeff, next_coeff, far_in, *refs):
    *near_in, rows, sums_in, start, inner, edge = refs[:-5]
    rows_out, sums_out, far_out, near_out, middle = refs[-5:]

    def run(lower_side, upper_side):
        below, down = lower_side
        above, up = upper_side

        def body(pairs):
            result = close_round(
                coeff, pairs, below, above, rows, sums_in, start, inner, edge, middle
            )
            for row in range(2):
                put(rows_out, row, pairs, result[row])
            open_round(next_coeff, pairs, rows_out, start, inner, edge, sums_out, down, up)

        each_group(rows, body)

    near_side = parts(*near_in), parts(near_out)
    by_parity(run, near_side, (parts(far_in), parts(far_out)))


def last_kernel(coeff, first, lead, far_in, near_in, rows, sums_in, start, inner, edge, *rest):
    out, middle, filled, sems = rest[-4:]
    low = low_half()

    def store(n):
        here = pl.ds(2 * n, 2)
        there = pl.ds(first + 2 * n, 2)
        return pltpu.make_async_copy(filled.at[here], out.at[there], sems.at[n])

    def run(below, above):
        def body(pairs):
            lower, upper = close_round(
                coeff, pairs, below, above, rows, sums_in, start, inner, edge, middle
            )
            for n, bottom, top in zip(pairs, lower, upper):
                for k in range(6):
                    p = first_of(bottom[k], top[k], low) * lead
                    q = second_of(bottom[k], top[k], low) * lead
                    for m, value in ((2 * n, p), (2 * n + 1, q)):
                        filled[m, k, 0:8] = value[:, : 2 * LS]
                        filled[m, k, 8:16] = value[:, 2 * LS :]
                store(n).start()

        each_group(rows, body)

    by_parity(run, parts(near_in), parts(far_in))
    for n in range(rows.shape[1]):
        store(n).wait()


VMEM_LIMIT = 32 * 1024 * 1024


def call(
    kernel, outs, args, flops, scratch=(), in_hbm=(), out_hbm=False, aliases={}, unread=()
):
    moved = sum(4 * a.size for a in args) + sum(4 * o.size for o in outs)
    args = [
        pltpu.with_memory_space_constraint(a, pltpu.HBM) if i in in_hbm else a
        for i, a in enumerate(args)
    ]
    vmem = pl.BlockSpec(memory_space=pltpu.VMEM)
    hbm = pl.BlockSpec(memory_space=pltpu.HBM)
    anywhere = pl.BlockSpec(memory_space=pl.ANY)
    return pl.pallas_call(
        kernel,
        out_shape=outs,
        in_specs=[
            hbm if i in in_hbm else anywhere if i in unread else vmem for i in range(len(args))
        ],
        out_specs=[hbm if out_hbm else vmem] * len(outs),
        scratch_shapes=list(scratch),
        input_output_aliases=aliases,
        compiler_params=pltpu.CompilerParams(vmem_limit_bytes=VMEM_LIMIT),
        cost_estimate=pl.CostEstimate(flops=flops, bytes_accessed=moved, transcendentals=0),
    )(*args)


def chunk_sizes(pairs):
    first = pairs * 7 // 12
    return (first, pairs - first)


def halo_body(links, sources):
    vectors = sources.shape[0]
    sizes = chunk_sizes(vectors // 2)
    chunks = range(len(sizes))
    first = [2 * sum(sizes[:chunk]) for chunk in chunks]
    sites, planes = links.shape[4:]
    f32 = functools.partial(jax.ShapeDtypeStruct, dtype=jnp.float32)
    both = [f32((2, pairs, 6, 8, 128)) for pairs in sizes]
    middle = [pltpu.VMEM(shape.shape, jnp.float32) for shape in both]
    raw = [(2 * pairs, 6, planes, sites) for pairs in sizes]
    source_view = jnp.swapaxes(sources, 3, 4).reshape(vectors, 6, planes, sites)
    link_view = jnp.swapaxes(links, 4, 5)
    powers = power_coeffs()
    lead = powers[4]
    steps = [powers[power] / lead for power in (3, 2, 1, 0)]
    work = [2 * pairs * 36 * 2 * 1024 for pairs in sizes]
    count = lax.axis_size("space")
    near_pairs = [(d, d ^ 1) for d in range(count)]
    far_pairs = [(d, (d + 1 if d % 2 else d - 1) % count) for d in range(count)]

    def to_far(value):
        return lax.ppermute(value, "space", far_pairs)

    def to_near(value):
        return lax.ppermute(value, "space", near_pairs)

    far_inner, edge, rows, far_sums, far_out, later, held = call(
        functools.partial(first_kernel, steps[0]),
        [
            f32((1, 4, 3, 3, 2, 8, 128)),
            f32((3, 3, 2, 8, 128)),
            both[0],
            f32((1, *both[0].shape[1:])),
            both[0],
            f32((vectors - first[1], 6, planes, sites)),
            f32(link_view.shape),
        ],
        [source_view, link_view],
        6 * work[0],
        [
            pltpu.VMEM(raw[0], jnp.float32),
            pltpu.SemaphoreType.DMA((4 + sizes[0],)),
        ],
        (0, 1),
    )
    far = to_far(far_out)
    half = f32((1, *both[0].shape[1:]))
    inner, first_sums, *first_near, second_rows, second_sums, far_out, near_out = call(
        functools.partial(start_kernel, steps[0]),
        [f32((2, 4, 3, 3, 2, 8, 128)), both[0], half, half] + [both[1]] * 4,
        [later, held, far_inner, edge, rows, far_sums],
        6 * work[1],
    )
    start = [rows, second_rows]
    fields = [(rows, first_sums), (second_rows, second_sums)]
    halos = [(far, *map(to_near, first_near)), (to_far(far_out), to_near(near_out))]
    for chunk in chunks:
        rows, sums, *sends = call(
            functools.partial(round_kernel, steps[1], steps[2]),
            [both[chunk]] * 4,
            [*halos[chunk], *fields[chunk], start[chunk], inner, edge],
            12 * work[chunk],
            [middle[chunk]],
        )
        fields[chunk] = (rows, sums)
        halos[chunk] = (to_far(sends[0]), to_near(sends[1]))
    out = None
    for chunk in chunks:
        args = [*halos[chunk], *fields[chunk], start[chunk], inner, edge]
        (out,) = call(
            functools.partial(last_kernel, steps[3], first[chunk], lead),
            [f32(source_view.shape)],
            args if out is None else args + [out],
            6 * work[chunk],
            [
                middle[chunk],
                pltpu.VMEM(raw[chunk], jnp.float32),
                pltpu.SemaphoreType.DMA((sizes[chunk],)),
            ],
            () if out is None else (len(args),),
            True,
            {} if out is None else {len(args): 0},
        )
    return jnp.swapaxes(out.reshape(vectors, 3, 2, planes, sites), 3, 4)


def shifted(value, axis, steps):
    count = lax.axis_size(axis)
    pairs = [(source, (source + steps) % count) for source in range(count)]
    return lax.ppermute(value, axis, pairs)


def apply_link(link, vector):
    real_part = 0.0
    imag_part = 0.0
    for column in range(3):
        link_re = link[:, column, 0][None]
        link_im = link[:, column, 1][None]
        vec_re = vector[:, column, 0][:, None]
        vec_im = vector[:, column, 1][:, None]
        real_part = real_part + link_re * vec_re - link_im * vec_im
        imag_part = imag_part + link_re * vec_im + link_im * vec_re
    return jnp.stack([real_part, imag_part], axis=2)


def apply_dagger(link, vector):
    real_part = 0.0
    imag_part = 0.0
    for column in range(3):
        link_re = link[column, :, 0][None]
        link_im = link[column, :, 1][None]
        vec_re = vector[:, column, 0][:, None]
        vec_im = vector[:, column, 1][:, None]
        real_part = real_part + link_re * vec_re + link_im * vec_im
        imag_part = imag_part + link_re * vec_im - link_im * vec_re
    return jnp.stack([real_part, imag_part], axis=2)


def z_ahead(array, extent, z_index):
    return jnp.where(
        z_index == extent - 1, jnp.roll(array, extent - 1, axis=-1), jnp.roll(array, -1, axis=-1)
    )


def z_behind(array, extent, z_index):
    return jnp.where(
        z_index == 0, jnp.roll(array, 1 - extent, axis=-1), jnp.roll(array, 1, axis=-1)
    )


def plane_body(links, sources):
    device_count = lax.axis_size("space")
    slabs = device_count // NT
    yz_local = links.shape[4]
    planes = links.shape[5] // device_count
    plane_sites = yz_local * device_count
    vectors = sources.shape[0]
    link_parts = links.reshape(54, yz_local, NT, slabs, planes)
    source_parts = sources.reshape(vectors * 6, yz_local, NT, slabs, planes)
    link_send = jnp.transpose(link_parts, (0, 3, 2, 4, 1)).reshape(
        54, device_count, planes, yz_local
    )
    source_send = jnp.transpose(source_parts, (0, 3, 2, 4, 1)).reshape(
        vectors * 6, device_count, planes, yz_local
    )
    link_recv, source_recv = (
        lax.all_to_all(link_send, "space", split_axis=1, concat_axis=3, tiled=True),
        lax.all_to_all(source_send, "space", split_axis=1, concat_axis=3, tiled=True),
    )
    gauge_local = link_recv.reshape(3, 3, 3, 2, planes, plane_sites)
    source_field = source_recv.reshape(vectors, 3, 2, planes, plane_sites)
    z_index = jnp.arange(plane_sites, dtype=jnp.int32) % LS
    x_top = gauge_local[0]
    x_rest = gauge_local[0][:, :, :, :-1]
    y_back = jnp.roll(gauge_local[1], LS, axis=-1)
    z_back = z_behind(gauge_local[2], LS, z_index)

    def fetch_lower(vector):
        return shifted(apply_dagger(x_top, vector), "space", NT)

    def hop_sum(vector):
        upper_face = shifted(vector, "space", -NT)
        lower_face = fetch_lower(vector)
        ahead = apply_link(
            gauge_local[0], jnp.concatenate([vector[:, :, :, 1:], upper_face], axis=3)
        )
        behind = jnp.concatenate([lower_face, apply_dagger(x_rest, vector[:, :, :, :-1])], axis=3)
        summed = ahead + behind
        summed = (
            summed
            + apply_link(gauge_local[1], jnp.roll(vector, -LS, axis=-1))
            + apply_dagger(y_back, jnp.roll(vector, LS, axis=-1))
        )
        summed = (
            summed
            + apply_link(gauge_local[2], z_ahead(vector, LS, z_index))
            + apply_dagger(z_back, z_behind(vector, LS, z_index))
        )
        return summed

    def scaled(vector):
        return hop_sum(vector) * (-1.0 / 6.0)

    previous = source_field
    current = scaled(previous)
    filtered = cheb_coeffs[0] * previous + cheb_coeffs[1] * current
    for degree in range(2, 5):
        following = 2.0 * scaled(current) - previous
        filtered = filtered + cheb_coeffs[degree] * following
        previous, current = (current, following)
    outgoing = filtered.reshape(vectors * 6, 1, planes, plane_sites)
    returned = lax.all_to_all(outgoing, "space", split_axis=3, concat_axis=1, tiled=True)
    ordered = jnp.transpose(
        returned.reshape(vectors * 6, slabs, NT, planes, yz_local), (0, 4, 2, 1, 3)
    )
    return ordered.reshape(vectors, 3, 2, yz_local, NT * slabs * planes)


def body(links, sources):
    sites, planes = sources.shape[3:]
    if sites == 2 * LS and planes == 2 * NT and sources.shape[0] % 8 == 0:
        return halo_body(links, sources)
    return plane_body(links, sources)


def solution(mesh):
    in_specs = (
        P(None, None, None, None, "space", "groups"),
        P(None, None, None, "space", "groups"),
    )
    out_specs = P(None, None, None, "space", "groups")
    return jax.shard_map(body, mesh=mesh, in_specs=in_specs, out_specs=out_specs, check_vma=False)
```

```python
import functools

import jax
import jax.numpy as jnp
from jax import lax
from jax.experimental import pallas as pl
from jax.experimental.pallas import tpu as pltpu
from jax.sharding import PartitionSpec as P

NT = 8
LS = 32

cheb_coeffs = (0.6, -0.5, 0.35, -0.25, 0.15)


def power_coeffs():
    c0, c1, c2, c3, c4 = cheb_coeffs
    return (c0 - c2 + c4, c1 - 3.0 * c3, 2.0 * c2 - 8.0 * c4, 4.0 * c3, 8.0 * c4)


def lane_ids():
    return lax.broadcasted_iota(jnp.int32, (8, 128), 1)


def sublane_ids():
    return lax.broadcasted_iota(jnp.int32, (8, 128), 0)


def low_half():
    return (lane_ids() // LS) % 2 == 0


def first_of(p, q, low):
    return jnp.where(low, p, pltpu.roll(q, LS, 1))


def second_of(p, q, low):
    return jnp.where(low, pltpu.roll(p, 128 - LS, 1), q)


def z_next(value, z):
    return jnp.where(z == LS - 1, pltpu.roll(value, LS - 1, 1), pltpu.roll(value, 127, 1))


def z_prev(value, z):
    return jnp.where(z == 0, pltpu.roll(value, 129 - LS, 1), pltpu.roll(value, 1, 1))


def x_other(value, even):
    return jnp.where(even, pltpu.roll(value, 7, 0), pltpu.roll(value, 1, 0))


def mat_vec(load, vectors, sums, dagger=False):
    for a in range(3):
        for b in range(3):
            w_re, w_im = load(b, a) if dagger else load(a, b)
            for vec, acc in zip(vectors, sums):
                v_re, v_im = vec[2 * b], vec[2 * b + 1]
                if dagger:
                    acc[2 * a] = acc[2 * a] + w_re * v_re + w_im * v_im
                    acc[2 * a + 1] = acc[2 * a + 1] + w_re * v_im - w_im * v_re
                else:
                    acc[2 * a] = acc[2 * a] + w_re * v_re - w_im * v_im
                    acc[2 * a + 1] = acc[2 * a + 1] + w_re * v_im + w_im * v_re


def zeros(count):
    return [[jnp.zeros((8, 128), jnp.float32) for _ in range(6)] for _ in range(count)]


def link_at(ref, *index):
    return lambda a, b: (ref[index + (a, b, 0)], ref[index + (a, b, 1)])


def tile(ref, index):
    return jnp.concatenate([ref[index + (slice(0, 8),)], ref[index + (slice(8, 16),)]], axis=1)


def parts(*refs):
    return [(refs[0], 0), (refs[0], 1)] if len(refs) == 1 else [(ref, 0) for ref in refs]


def by_parity(run, near, far):
    odd = lax.axis_index("space") % 2 == 1

    @pl.when(odd)
    def _():
        run(near, far)

    @pl.when(jnp.logical_not(odd))
    def _():
        run(far, near)


def each_group(ref, body):
    count = ref.shape[1]

    def step(i, carry):
        body([2 * i, 2 * i + 1])
        return carry

    lax.fori_loop(0, count // 2, step, 0, unroll=count <= 5)
    if count % 2:
        body([count - 1])


def take(ref, row, pairs):
    return [[ref[row, n, k] for k in range(6)] for n in pairs]


def put(ref, row, pairs, vectors):
    for n, vec in zip(pairs, vectors):
        for k in range(6):
            ref[row, n, k] = vec[k]


def pack_edge(links, edge):
    low = low_half()
    for a in range(3):
        for b in range(3):
            for part in range(2):
                y_link = tile(links, (1, a, b, part)) * (-1.0 / 6.0)
                edge[a, b, part] = second_of(y_link, y_link, low)


def pack_links(links, inner, slot, row):
    low = low_half()
    z = lane_ids() % LS
    even = sublane_ids() % 2 == 0
    pick = second_of if row else first_of
    for part in range(2):
        x_link, y_link, z_link = (
            [
                [tile(links, (mu, a, b, part)) * (-1.0 / 6.0) for b in range(3)]
                for a in range(3)
            ]
            for mu in range(3)
        )
        for a in range(3):
            for b in range(3):
                other = x_other(x_link[b][a], even)
                both = x_link[a][b] + (other if part == 0 else -other)
                inner[slot, 0, a, b, part] = pick(both, both, low)
                u_z = pick(z_link[a][b], z_link[a][b], low)
                inner[slot, 1, a, b, part] = u_z
                u_z = z_prev(u_z, z)
                inner[slot, 2, b, a, part] = u_z if part == 0 else -u_z
                u_y = first_of(y_link[a][b], y_link[a][b], low)
                if row == 0:
                    inner[slot, 3, a, b, part] = u_y
                else:
                    inner[slot, 3, b, a, part] = u_y if part == 0 else -u_y


def add_x_and_z(inner, slot, vectors, sums):
    z = lane_ids() % LS
    even = sublane_ids() % 2 == 0
    mat_vec(link_at(inner, slot, 0), [[x_other(c, even) for c in vec] for vec in vectors], sums)
    mat_vec(link_at(inner, slot, 1), [[z_next(c, z) for c in vec] for vec in vectors], sums)
    mat_vec(link_at(inner, slot, 2), [[z_prev(c, z) for c in vec] for vec in vectors], sums)


def add_inner(inner, slot, row, pairs, field, sums):
    add_x_and_z(inner, slot, take(field, row, pairs), sums)
    mat_vec(link_at(inner, slot, 3), take(field, 1 - row, pairs), sums)


def scaled_rows(coeff, start, row, pairs):
    return [[coeff * c for c in vec] for vec in take(start, row, pairs)]


def send(edge, pairs, part, row, vectors, out):
    if row == 1:
        field, vectors = vectors, zeros(len(pairs))
        mat_vec(link_at(edge), field, vectors, dagger=True)
    put(*out[part], pairs, vectors)


def local_sums(coeff, pairs, row, rows, start, inner, slot):
    sums = scaled_rows(coeff, start, row, pairs)
    add_inner(inner, slot, row, pairs, rows, sums)
    return sums


def open_round(coeff, pairs, rows, start, inner, edge, sums_out, down, up):
    for row, out in enumerate((down, up)):
        sums = local_sums(coeff, pairs, row, rows, start, inner, row)
        put(sums_out, row, pairs, sums)
        send(edge, pairs, 0, row, take(rows, row, pairs), out)
        send(edge, pairs, 1, row, sums, out)


def plus(sums, more):
    return [[s + m for s, m in zip(*both)] for both in zip(sums, more)]


def add_message(edge, pairs, part, row, message, sums):
    received = take(*message[part], pairs)
    if row == 0:
        return plus(sums, received)
    mat_vec(link_at(edge), received, sums)
    return sums


def second_start(coeff, pairs, row, rows, start):
    return [
        [c + (1.0 / 36.0) * r for c, r in zip(*both)]
        for both in zip(scaled_rows(coeff, start, row, pairs), take(rows, row, pairs))
    ]


def close_round(coeff, pairs, below, above, rows, sums_in, start, inner, edge, middle):
    for row, message in enumerate((below, above)):
        sums = take(sums_in, row, pairs)
        put(middle, row, pairs, add_message(edge, pairs, 0, row, message, sums))
    result = []
    for row, message in enumerate((below, above)):
        sums = second_start(coeff, pairs, row, rows, start)
        add_inner(inner, row, row, pairs, middle, sums)
        result.append(add_message(edge, pairs, 1, row, message, sums))
    return result


def side(below, above):
    return (0, below) if above is None else (1, above)


def pack_rows(source, rows, arrive=lambda n: None):
    low = low_half()

    def body(pairs):
        for n in pairs:
            arrive(n)
        for n in pairs:
            for k in range(6):
                p, q = source(2 * n, k), source(2 * n + 1, k)
                rows[0, n, k] = first_of(p, q, low)
                rows[1, n, k] = second_of(p, q, low)

    each_group(rows, body)


def start_chunk(coeff, rows, inner, edge, sums, far_out, near_out):
    def run(down, up):
        each_group(
            rows,
            lambda pairs: open_round(coeff, pairs, rows, rows, inner, edge, sums, down, up),
        )

    by_parity(run, parts(near_out), parts(far_out))


def first_kernel(coeff, src, links, inner, edge, rows, far_sums, far_out, later, held, now, sems):
    count = now.shape[0]
    link_copies = [
        pltpu.make_async_copy(links.at[mu], held.at[mu], sems.at[mu]) for mu in range(3)
    ]

    def first_copy(n):
        here = pl.ds(2 * n, 2)
        return pltpu.make_async_copy(src.at[here], now.at[here], sems.at[4 + n])

    rest = src.at[pl.ds(count, later.shape[0])]
    later_copy = pltpu.make_async_copy(rest, later, sems.at[3])
    link_copies[1].start()
    for n in range(count // 2):
        first_copy(n).start()
    link_copies[2].start()
    link_copies[0].start()
    later_copy.start()
    link_copies[1].wait()
    pack_edge(held, edge)
    pack_rows(lambda n, k: tile(now, (n, k)), rows, lambda n: first_copy(n).wait())
    link_copies[2].wait()
    link_copies[0].wait()
    by_parity(lambda *sides: pack_links(held, inner, 0, side(*sides)[0]), None, True)

    def run(*sides):
        row, out = side(*sides)

        def body(pairs):
            sums = local_sums(coeff, pairs, row, rows, rows, inner, 0)
            put(far_sums, 0, pairs, sums)
            send(edge, pairs, 0, row, take(rows, row, pairs), out)
            send(edge, pairs, 1, row, sums, out)

        each_group(rows, body)

    by_parity(run, None, parts(far_out))
    later_copy.wait()


def start_kernel(coeff, later, links, far_inner, edge, first_rows, far_sums, inner, *refs):
    first_sums, *first_near, rows, sums, far_out, near_out = refs

    def run(*sides):
        row, out = side(*sides)
        pack_links(links, inner, row, row)
        for term in range(4):
            for a in range(3):
                for b in range(3):
                    for part in range(2):
                        inner[1 - row, term, a, b, part] = far_inner[0, term, a, b, part]

        def body(pairs):
            ends = local_sums(coeff, pairs, row, first_rows, first_rows, inner, row)
            put(first_sums, row, pairs, ends)
            put(first_sums, 1 - row, pairs, take(far_sums, 0, pairs))
            send(edge, pairs, 0, row, take(first_rows, row, pairs), out)
            send(edge, pairs, 1, row, ends, out)

        each_group(first_rows, body)

    by_parity(run, parts(*first_near), None)
    pack_rows(lambda n, k: tile(later, (n, k)), rows)
    start_chunk(coeff, rows, inner, edge, sums, far_out, near_out)


def round_kernel(coeff, next_coeff, far_in, *refs):
    *near_in, rows, sums_in, start, inner, edge = refs[:-5]
    rows_out, sums_out, far_out, near_out, middle = refs[-5:]

    def run(lower_side, upper_side):
        below, down = lower_side
        above, up = upper_side

        def body(pairs):
            result = close_round(
                coeff, pairs, below, above, rows, sums_in, start, inner, edge, middle
            )
            for row in range(2):
                put(rows_out, row, pairs, result[row])
            open_round(next_coeff, pairs, rows_out, start, inner, edge, sums_out, down, up)

        each_group(rows, body)

    near_side = parts(*near_in), parts(near_out)
    by_parity(run, near_side, (parts(far_in), parts(far_out)))


def last_kernel(coeff, first, lead, far_in, near_in, rows, sums_in, start, inner, edge, *rest):
    out, middle, filled, sems = rest[-4:]
    low = low_half()

    def store(n):
        here = pl.ds(2 * n, 2)
        there = pl.ds(first + 2 * n, 2)
        return pltpu.make_async_copy(filled.at[here], out.at[there], sems.at[n])

    def run(below, above):
        def body(pairs):
            lower, upper = close_round(
                coeff, pairs, below, above, rows, sums_in, start, inner, edge, middle
            )
            for n, bottom, top in zip(pairs, lower, upper):
                for k in range(6):
                    p = first_of(bottom[k], top[k], low) * lead
                    q = second_of(bottom[k], top[k], low) * lead
                    for m, value in ((2 * n, p), (2 * n + 1, q)):
                        filled[m, k, 0:8] = value[:, : 2 * LS]
                        filled[m, k, 8:16] = value[:, 2 * LS :]
                store(n).start()

        each_group(rows, body)

    by_parity(run, parts(near_in), parts(far_in))
    for n in range(rows.shape[1]):
        store(n).wait()


VMEM_LIMIT = 32 * 1024 * 1024


def call(
    kernel, outs, args, flops, scratch=(), in_hbm=(), out_hbm=False, aliases={}, unread=()
):
    moved = sum(4 * a.size for a in args) + sum(4 * o.size for o in outs)
    args = [
        pltpu.with_memory_space_constraint(a, pltpu.HBM) if i in in_hbm else a
        for i, a in enumerate(args)
    ]
    vmem = pl.BlockSpec(memory_space=pltpu.VMEM)
    hbm = pl.BlockSpec(memory_space=pltpu.HBM)
    anywhere = pl.BlockSpec(memory_space=pl.ANY)
    return pl.pallas_call(
        kernel,
        out_shape=outs,
        in_specs=[
            hbm if i in in_hbm else anywhere if i in unread else vmem for i in range(len(args))
        ],
        out_specs=[hbm if out_hbm else vmem] * len(outs),
        scratch_shapes=list(scratch),
        input_output_aliases=aliases,
        compiler_params=pltpu.CompilerParams(vmem_limit_bytes=VMEM_LIMIT),
        cost_estimate=pl.CostEstimate(flops=flops, bytes_accessed=moved, transcendentals=0),
    )(*args)


def chunk_sizes(pairs):
    first = pairs * 7 // 12
    return (first, pairs - first)


def halo_body(links, sources):
    vectors = sources.shape[0]
    sizes = chunk_sizes(vectors // 2)
    chunks = range(len(sizes))
    first = [2 * sum(sizes[:chunk]) for chunk in chunks]
    sites, planes = links.shape[4:]
    f32 = functools.partial(jax.ShapeDtypeStruct, dtype=jnp.float32)
    both = [f32((2, pairs, 6, 8, 128)) for pairs in sizes]
    middle = [pltpu.VMEM(shape.shape, jnp.float32) for shape in both]
    raw = [(2 * pairs, 6, planes, sites) for pairs in sizes]
    source_view = jnp.swapaxes(sources, 3, 4).reshape(vectors, 6, planes, sites)
    link_view = jnp.swapaxes(links, 4, 5)
    powers = power_coeffs()
    lead = powers[4]
    steps = [powers[power] / lead for power in (3, 2, 1, 0)]
    work = [2 * pairs * 36 * 2 * 1024 for pairs in sizes]
    count = lax.axis_size("space")
    near_pairs = [(d, d ^ 1) for d in range(count)]
    far_pairs = [(d, (d + 1 if d % 2 else d - 1) % count) for d in range(count)]

    def to_far(value):
        return lax.ppermute(value, "space", far_pairs)

    def to_near(value):
        return lax.ppermute(value, "space", near_pairs)

    far_inner, edge, rows, far_sums, far_out, later, held = call(
        functools.partial(first_kernel, steps[0]),
        [
            f32((1, 4, 3, 3, 2, 8, 128)),
            f32((3, 3, 2, 8, 128)),
            both[0],
            f32((1, *both[0].shape[1:])),
            both[0],
            f32((vectors - first[1], 6, planes, sites)),
            f32(link_view.shape),
        ],
        [source_view, link_view],
        6 * work[0],
        [
            pltpu.VMEM(raw[0], jnp.float32),
            pltpu.SemaphoreType.DMA((4 + sizes[0],)),
        ],
        (0, 1),
    )
    far = to_far(far_out)
    half = f32((1, *both[0].shape[1:]))
    inner, first_sums, *first_near, second_rows, second_sums, far_out, near_out = call(
        functools.partial(start_kernel, steps[0]),
        [f32((2, 4, 3, 3, 2, 8, 128)), both[0], half, half] + [both[1]] * 4,
        [later, held, far_inner, edge, rows, far_sums],
        6 * work[1],
    )
    start = [rows, second_rows]
    fields = [(rows, first_sums), (second_rows, second_sums)]
    halos = [(far, *map(to_near, first_near)), (to_far(far_out), to_near(near_out))]
    for chunk in chunks:
        rows, sums, *sends = call(
            functools.partial(round_kernel, steps[1], steps[2]),
            [both[chunk]] * 4,
            [*halos[chunk], *fields[chunk], start[chunk], inner, edge],
            12 * work[chunk],
            [middle[chunk]],
        )
        fields[chunk] = (rows, sums)
        halos[chunk] = (to_far(sends[0]), to_near(sends[1]))
    out = None
    for chunk in chunks:
        args = [*halos[chunk], *fields[chunk], start[chunk], inner, edge]
        (out,) = call(
            functools.partial(last_kernel, steps[3], first[chunk], lead),
            [f32(source_view.shape)],
            args if out is None else args + [out],
            6 * work[chunk],
            [
                middle[chunk],
                pltpu.VMEM(raw[chunk], jnp.float32),
                pltpu.SemaphoreType.DMA((sizes[chunk],)),
            ],
            () if out is None else (len(args),),
            True,
            {} if out is None else {len(args): 0},
        )
    return jnp.swapaxes(out.reshape(vectors, 3, 2, planes, sites), 3, 4)


def shifted(value, axis, steps):
    count = lax.axis_size(axis)
    pairs = [(source, (source + steps) % count) for source in range(count)]
    return lax.ppermute(value, axis, pairs)


def apply_link(link, vector):
    real_part = 0.0
    imag_part = 0.0
    for column in range(3):
        link_re = link[:, column, 0][None]
        link_im = link[:, column, 1][None]
        vec_re = vector[:, column, 0][:, None]
        vec_im = vector[:, column, 1][:, None]
        real_part = real_part + link_re * vec_re - link_im * vec_im
        imag_part = imag_part + link_re * vec_im + link_im * vec_re
    return jnp.stack([real_part, imag_part], axis=2)


def apply_dagger(link, vector):
    real_part = 0.0
    imag_part = 0.0
    for column in range(3):
        link_re = link[column, :, 0][None]
        link_im = link[column, :, 1][None]
        vec_re = vector[:, column, 0][:, None]
        vec_im = vector[:, column, 1][:, None]
        real_part = real_part + link_re * vec_re + link_im * vec_im
        imag_part = imag_part + link_re * vec_im - link_im * vec_re
    return jnp.stack([real_part, imag_part], axis=2)


def z_ahead(array, extent, z_index):
    return jnp.where(
        z_index == extent - 1, jnp.roll(array, extent - 1, axis=-1), jnp.roll(array, -1, axis=-1)
    )


def z_behind(array, extent, z_index):
    return jnp.where(
        z_index == 0, jnp.roll(array, 1 - extent, axis=-1), jnp.roll(array, 1, axis=-1)
    )


def plane_body(links, sources):
    device_count = lax.axis_size("space")
    slabs = device_count // NT
    yz_local = links.shape[4]
    planes = links.shape[5] // device_count
    plane_sites = yz_local * device_count
    vectors = sources.shape[0]
    link_parts = links.reshape(54, yz_local, NT, slabs, planes)
    source_parts = sources.reshape(vectors * 6, yz_local, NT, slabs, planes)
    link_send = jnp.transpose(link_parts, (0, 3, 2, 4, 1)).reshape(
        54, device_count, planes, yz_local
    )
    source_send = jnp.transpose(source_parts, (0, 3, 2, 4, 1)).reshape(
        vectors * 6, device_count, planes, yz_local
    )
    link_recv, source_recv = (
        lax.all_to_all(link_send, "space", split_axis=1, concat_axis=3, tiled=True),
        lax.all_to_all(source_send, "space", split_axis=1, concat_axis=3, tiled=True),
    )
    gauge_local = link_recv.reshape(3, 3, 3, 2, planes, plane_sites)
    source_field = source_recv.reshape(vectors, 3, 2, planes, plane_sites)
    z_index = jnp.arange(plane_sites, dtype=jnp.int32) % LS
    x_top = gauge_local[0]
    x_rest = gauge_local[0][:, :, :, :-1]
    y_back = jnp.roll(gauge_local[1], LS, axis=-1)
    z_back = z_behind(gauge_local[2], LS, z_index)

    def fetch_lower(vector):
        return shifted(apply_dagger(x_top, vector), "space", NT)

    def hop_sum(vector):
        upper_face = shifted(vector, "space", -NT)
        lower_face = fetch_lower(vector)
        ahead = apply_link(
            gauge_local[0], jnp.concatenate([vector[:, :, :, 1:], upper_face], axis=3)
        )
        behind = jnp.concatenate([lower_face, apply_dagger(x_rest, vector[:, :, :, :-1])], axis=3)
        summed = ahead + behind
        summed = (
            summed
            + apply_link(gauge_local[1], jnp.roll(vector, -LS, axis=-1))
            + apply_dagger(y_back, jnp.roll(vector, LS, axis=-1))
        )
        summed = (
            summed
            + apply_link(gauge_local[2], z_ahead(vector, LS, z_index))
            + apply_dagger(z_back, z_behind(vector, LS, z_index))
        )
        return summed

    def scaled(vector):
        return hop_sum(vector) * (-1.0 / 6.0)

    previous = source_field
    current = scaled(previous)
    filtered = cheb_coeffs[0] * previous + cheb_coeffs[1] * current
    for degree in range(2, 5):
        following = 2.0 * scaled(current) - previous
        filtered = filtered + cheb_coeffs[degree] * following
        previous, current = (current, following)
    outgoing = filtered.reshape(vectors * 6, 1, planes, plane_sites)
    returned = lax.all_to_all(outgoing, "space", split_axis=3, concat_axis=1, tiled=True)
    ordered = jnp.transpose(
        returned.reshape(vectors * 6, slabs, NT, planes, yz_local), (0, 4, 2, 1, 3)
    )
    return ordered.reshape(vectors, 3, 2, yz_local, NT * slabs * planes)


def body(links, sources):
    sites, planes = sources.shape[3:]
    if sites == 2 * LS and planes == 2 * NT and sources.shape[0] % 8 == 0:
        return halo_body(links, sources)
    return plane_body(links, sources)


def solution(mesh):
    in_specs = (
        P(None, None, None, None, "space", "groups"),
        P(None, None, None, "space", "groups"),
    )
    out_specs = P(None, None, None, "space", "groups")
    return jax.shard_map(body, mesh=mesh, in_specs=in_specs, out_specs=out_specs, check_vma=False)
```
